128 devices in a mesh: wave: 32 (over z, x, core), fld: 4 (over y).
Axes of the slice: x: 4, y: 4, z: 4, core: 2. Of those that a mesh axis runs over, the one named last changes fastest.
Arguments:
- spec_in: bfloat16 [24, 1280, 2, 1280], P('fld', 'wave'), may hold values from -16 to 16
- legendre: bfloat16 [1280, 512, 1280], P('wave', 'fld'), may hold values from -0.15625 to 0.15625
- wave_order: int32 [1280], replicated, may hold values from 0 to 1279, as said below
- row_length: int32 [512], replicated, may hold values from 512 to 5632, as said below
- quad_weight: float32 [512], replicated, may hold values from 0.5 to 2
- mixing: float32 [24, 24], replicated, may hold values from -1.25 to 1.25
- square_gain: float32 [24], replicated, may hold values from 0.5 to 1
Outputs:
- spec_out: float32 [24, 1280, 2, 1280], P('fld', 'wave')
The draws below stay inside these ranges and needn't reach their ends.
Inputs may be any that keep to these rules, and one draw needn't show every extreme that they name: `wave_order`: A permutation of the wavenumbers in which rows 2k and 2k + 1 hold a wavenumber m and 1279 - m. `row_length`: each value is 20 + 4 i for an octahedral row index i below 1280, rounded up to a multiple of 512; one latitude has 5632.
All inputs are finite; a program needn't handle non-finite values.
Results may differ from the reference program's by a relative error of at most 0.0054.
Values may be sent and summed in bfloat16 or wider, within the bound.
A program may use at most 192 MiB of HBM per device.

```python
import math
import jax
import jax.numpy as jnp
from jax import lax

M = 1280
BLOCK = 512
FL = 24
LPAD = 5632
NLAT = 512


def pair_orders(key):
    order_key = jax.random.fold_in(key, 11)
    low_orders = jax.random.permutation(order_key, M // 2).astype(jnp.int32)
    return jnp.stack([low_orders, M - 1 - low_orders], axis=1).reshape(M).astype(jnp.int32)


def draw_wave_order(key, part):
    orders = pair_orders(key)
    return orders


def draw_spec_in(key, part):
    orders = pair_orders(key)
    key = jax.random.fold_in(key, 37)
    order_frac = orders.astype(jnp.float32) / float(M)
    flatten = jnp.minimum(jnp.sqrt(float(M) / (M - orders).astype(jnp.float32)), 6.0)
    values = jax.random.normal(key, (FL, M, 2, M), jnp.float32)
    rising = 0.4 + 1.2 * order_frac
    row_scale = 1.2 * flatten * rising
    return jnp.clip(values * row_scale[None, :, None, None], -16.0, 16.0).astype(jnp.bfloat16)


def draw_row_length(key, part):
    key = jax.random.fold_in(key, 23)
    row_key, pick_key = jax.random.split(key)
    row_index = jax.random.randint(row_key, (NLAT,), 0, M).astype(jnp.int32)
    widest = jax.random.randint(pick_key, (), 0, NLAT).astype(jnp.int32)
    row_index = jnp.where(jnp.arange(NLAT, dtype=jnp.int32) == widest, M - 1, row_index)
    row_cells = 20 + 4 * row_index
    return ((row_cells + BLOCK - 1) // BLOCK * BLOCK).astype(jnp.int32)


def block_scale(rng, dims, pieces, least, top_value):
    def one(dim, parts):
        draws = jax.random.uniform(jax.random.fold_in(jax.random.fold_in(rng, 6), dim), (parts,), jnp.float32, least / len(pieces), top_value / len(pieces))
        return jnp.repeat(jnp.exp(draws), dims[dim] // parts).reshape((-1,) + (1,) * (len(dims) - dim - 1))

    loudness = one(*pieces[0])
    for cut in pieces[1:]:
        loudness = loudness * one(*cut)
    return loudness


def scatter_about(rng, dims, scale, bound, cuts=(), kind=jnp.bfloat16):
    entries = jax.random.normal(rng, dims, jnp.float32) * scale
    if len(cuts) > 0:
        entries = block_scale(rng, dims, cuts, -0.22, 0.18) * entries
    return jnp.clip(entries, min=-bound, max=bound).astype(kind)


def setup_inputs(seed: int = 0) -> dict:
    splits = jax.random.split(jax.random.key(seed), 8)
    return {
        "spec_in": draw_spec_in(jax.random.fold_in(splits[7], 71), 0),
        "legendre": scatter_about(splits[1], (M, NLAT, M), M ** -0.5, 0.15625, ((0, 32), (1, 4))),
        "wave_order": draw_wave_order(jax.random.fold_in(splits[7], 71), 0),
        "row_length": draw_row_length(jax.random.fold_in(splits[7], 71), 0),
        "quad_weight": jnp.clip(jnp.exp(jax.random.uniform(splits[4], (NLAT,), jnp.float32, math.log(0.5), math.log(2.0))), 0.5, 2.0),
        "mixing": scatter_about(splits[5], (FL, FL), FL ** -0.5, 1.25, (), jnp.float32),
        "square_gain": jnp.clip(jax.random.uniform(splits[6], (FL,), jnp.float32, 0.5, 1.0), 0.5, 1.0),
    }


def fourier_table(orders, length, padded):
    total_rows = orders.shape[0]
    count = padded // BLOCK
    coarse_cells = lax.broadcasted_iota(jnp.int32, (total_rows, count), 1) * BLOCK
    fine_cells = lax.broadcasted_iota(jnp.int32, (total_rows, BLOCK), 1)
    scale_angle = 2.0 * math.pi / length.astype(jnp.float32)
    coarse_angle = (orders[:, None] * coarse_cells % length).astype(jnp.float32) * scale_angle
    fine_angle = (orders[:, None] * fine_cells % length).astype(jnp.float32) * scale_angle
    coarse_cos = jnp.cos(coarse_angle)[:, :, None]
    coarse_sin = jnp.sin(coarse_angle)[:, :, None]
    fine_cos = jnp.cos(fine_angle)[:, None, :]
    fine_sin = jnp.sin(fine_angle)[:, None, :]
    cosine = (coarse_cos * fine_cos - coarse_sin * fine_sin).reshape(total_rows, padded)
    sine = (coarse_sin * fine_cos + coarse_cos * fine_sin).reshape(total_rows, padded)
    cell_index = lax.broadcasted_iota(jnp.int32, (total_rows, padded), 1)
    upper_mask = (cell_index < length) & (orders[:, None] < length // 2)
    cosine = jnp.where(upper_mask, cosine, jnp.float32(0.0))
    sine_rows = jnp.where(upper_mask, -sine, jnp.float32(0.0))
    return jnp.concatenate([cosine, sine_rows], axis=0).astype(jnp.bfloat16)

def column_step(coeff_rows, length, weight, orders, mixing, square_gain, padded):
    total_rows = coeff_rows.shape[0]
    levels = coeff_rows.shape[1] // 2
    trig_rows = fourier_table(orders, length, padded)
    coefficients = coeff_rows.reshape(total_rows, levels, 2).transpose(1, 2, 0).reshape(levels, 2 * total_rows)
    grid_rows = (jnp.dot(coefficients, trig_rows, preferred_element_type=jnp.float32) * float(total_rows) ** (-0.5)).astype(jnp.bfloat16)
    mixed_rows = jnp.dot(mixing, grid_rows.astype(jnp.float32), precision=lax.Precision.HIGHEST)
    update = (mixed_rows + square_gain[:, None] * mixed_rows * mixed_rows).astype(jnp.bfloat16)
    returned = jnp.dot(update, trig_rows.T, preferred_element_type=jnp.float32)
    returned = returned * (weight * lax.rsqrt(length.astype(jnp.float32)))
    return returned.reshape(levels, 2, total_rows).transpose(2, 0, 1).reshape(total_rows, 2 * levels).astype(jnp.bfloat16)

def reference(spec_in, legendre, wave_order, row_length, quad_weight, mixing, square_gain):
    degree = jnp.arange(M, dtype=jnp.int32)
    upper_mask = degree[None, :] >= wave_order[:, None]
    masked = spec_in * upper_mask[None, :, None, :].astype(spec_in.dtype)

    def inverse_row(operands):
        table_rows, coefficients = operands
        return jnp.dot(table_rows, coefficients.reshape(FL * 2, M).T, preferred_element_type=jnp.float32)
    fourier = lax.map(inverse_row, (legendre, masked.transpose(1, 0, 2, 3))).astype(jnp.bfloat16)

    def lat_step(operands):
        coeff_rows, length, weight = operands
        return column_step(coeff_rows, length, weight, wave_order, mixing, square_gain, LPAD)
    direct = lax.map(lat_step, (fourier.transpose(1, 0, 2), row_length, quad_weight))

    def direct_row(operands):
        table_rows, coefficients = operands
        return jnp.dot(coefficients.T, table_rows, preferred_element_type=jnp.float32)
    result = lax.map(direct_row, (legendre, direct.transpose(1, 0, 2)))
    result = result.reshape(M, FL, 2, M).transpose(1, 0, 2, 3)
    return result * upper_mask[None, :, None, :].astype(jnp.float32)
```

```python
import functools
import math

import jax
import jax.numpy as jnp
import ml_dtypes
import numpy as np
from jax import lax
from jax.experimental import pallas as pl
from jax.experimental.pallas import tpu as pltpu
from jax.sharding import PartitionSpec as P

M = 1280
FL = 24
BLOCK = 512
LANES = 128
NB = M // LANES
PB = NB + 1
PACKED = PB * LANES
CHUNKS = 5
PAIRS = 4
WAVE = 32
FLD = 4
LATS = 4
FD = FL // FLD
ROWS = 2 * FD * PAIRS
XMAX = 12
F32, BF16, I32 = jnp.float32, jnp.bfloat16, jnp.int32


def wave_tables():
    v = np.arange(BLOCK)
    angle = (v[:, None] * v[None, :] % BLOCK) * (2.0 * math.pi / BLOCK)
    return np.concatenate([np.cos(angle), -np.sin(angle)], axis=1).astype(ml_dtypes.bfloat16)


def lane_maps():
    width = LATS * LANES
    lat_a, ab_a, level_a, half_a = (np.full(width, -1) for _ in range(4))
    for lat in range(LATS):
        for ab in range(2):
            for g in range(FLD):
                for c in range(2):
                    for f in range(FD):
                        at = LANES * lat + ((ab * FLD + g) * 2 + c) * FD + f
                        lat_a[at], ab_a[at], half_a[at], level_a[at] = lat, ab, c, FD * g + f
    lat_b, ab_b, level_b, half_b = (np.full(width, -2) for _ in range(4))
    for c in range(2):
        for ab in range(2):
            for lat in range(LATS):
                for f in range(FL):
                    at = LANES * (2 * c + ab) + FL * lat + f
                    lat_b[at], ab_b[at], half_b[at], level_b[at] = lat, ab, c, f
    same = (
        (lat_a[:, None] == lat_b[None, :])
        & (ab_a[:, None] == ab_b[None, :])
        & (half_a[:, None] == half_b[None, :])
    )
    pick = same & (level_a[:, None] == level_b[None, :])
    rows = (level_a[:, None] == np.arange(FL)[None, :]).astype(np.float32)
    cols = (np.arange(FL)[:, None] == level_b[None, :]).astype(np.float32)
    return same.astype(np.float32), pick.T.astype(ml_dtypes.bfloat16), rows, cols


def shift_blocks(blocks, amount, sign):
    count = len(blocks)
    for bit in (1, 2, 4, 8):
        hit = (amount & bit) != 0
        blocks = [
            jnp.where(hit, blocks[(t - sign * bit) % count], blocks[t]) for t in range(count)
        ]
    return blocks


def pack_kernel(x_ref, m_ref, out_ref):
    m = m_ref[0]
    q = m >> 7
    lane = lax.broadcasted_iota(I32, (ROWS, LANES), 1)
    first, second = [], []
    for t in range(NB):
        n = lane + LANES * t
        span = slice(LANES * t, LANES * (t + 1))
        first.append(jnp.where(n >= m, x_ref[0, 0, :, span].astype(F32), 0.0))
        second.append(jnp.where(n >= M - 1 - m, x_ref[1, 0, :, span].astype(F32), 0.0))
    moved = shift_blocks(second, q + 1, 1)
    for t in range(NB):
        out_ref[0, :, LANES * t : LANES * (t + 1)] = jnp.where(t >= q, first[t], moved[t]).astype(BF16)
    out_ref[0, :, LANES * NB :] = second[NB - 1].astype(BF16)


def unpack_kernel(parts_ref, m_ref, out_ref):
    m = m_ref[0]
    q = m >> 7
    lane = lax.broadcasted_iota(I32, (ROWS, LANES), 1)
    total = []
    for t in range(PB):
        span = slice(LANES * t, LANES * (t + 1))
        total.append(sum(parts_ref[g, 0, :, span].astype(F32) for g in range(FLD)))
    moved = [jnp.where(t == q, total[NB], total[t]) for t in range(NB)]
    moved = shift_blocks(moved, q + 1, -1)
    for t in range(NB):
        n = lane + LANES * t
        span = slice(LANES * t, LANES * (t + 1))
        out_ref[0, 0, :, span] = jnp.where(n >= m, total[t], 0.0)
        out_ref[1, 0, :, span] = jnp.where(n >= M - 1 - m, moved[t], 0.0)


def load_packed(leg_ref, packed_ref, i, q):
    for t in range(PB):
        if t < NB:
            lower = (q > t).astype(I32)
            at = t + lower * (NB - 1 - q)
        else:
            lower, at = 1, NB - 1
        packed_ref[:, LANES * t : LANES * (t + 1)] = leg_ref[
            2 * i + lower, :, pl.ds(pl.multiple_of(at * LANES, LANES), LANES)
        ]


def inverse_kernel(order_ref, g_ref, leg_ref, mix_ref, out_ref, coeff, packed, wide, turn):
    chunk = pl.program_id(0)
    for t in range(PB):
        for g in range(FLD):
            coeff[t, ROWS * g : ROWS * (g + 1)] = g_ref[
                g, 0, :, LANES * t : LANES * (t + 1)
            ].astype(F32)
    for i in range(PAIRS):
        q = order_ref[2 * PAIRS * chunk + 2 * i] >> 7
        load_packed(leg_ref, packed, i, q)
        weights = []
        for t in range(PB):
            block = coeff[t, pl.ds(i, ROWS, stride=PAIRS), :]
            if t < NB:
                is_first = jnp.where(t >= q, 1.0, 0.0).astype(F32)
            else:
                is_first = jnp.float32(0.0)
            lead = block * is_first
            weights.append(
                jnp.concatenate([lead, block - lead, jnp.zeros((32, LANES), F32)], axis=0).astype(BF16)
            )
        fourier = lax.dot_general(
            packed[...],
            jnp.concatenate(weights, axis=1),
            (((1,), (1,)), ((), ())),
            preferred_element_type=F32,
        ).astype(BF16)
        for lat in range(LATS):
            wide[WAVE * i : WAVE * (i + 1), LANES * lat : LANES * (lat + 1)] = fourier[
                WAVE * lat : WAVE * (lat + 1)
            ]
    mixed = jnp.dot(wide[...], mix_ref[0], preferred_element_type=F32) + jnp.dot(
        wide[...], mix_ref[1], preferred_element_type=F32
    )
    for c in range(2):
        for ab in range(2):
            for i in range(PAIRS):
                at = 2 * c + ab
                turn[pl.ds(c * 8 + ab * PAIRS + i, WAVE, stride=16), :] = mixed[
                    WAVE * i : WAVE * (i + 1), LANES * at : LANES * (at + 1)
                ]
    out_ref[...] = turn[...].reshape(WAVE, 1, 16, LANES).astype(BF16)


def direct_kernel(order_ref, r_ref, leg_ref, pick_ref, out_ref, turn, wide, packed, total):
    chunk = pl.program_id(0)
    turn[...] = r_ref[...].reshape(WAVE * 16, LANES).astype(F32)
    for c in range(2):
        for ab in range(2):
            for i in range(PAIRS):
                at = 2 * c + ab
                wide[WAVE * i : WAVE * (i + 1), LANES * at : LANES * (at + 1)] = turn[
                    pl.ds(c * 8 + ab * PAIRS + i, WAVE, stride=16), :
                ].astype(BF16)
    spread = jnp.dot(wide[...], pick_ref[...], preferred_element_type=F32)
    for i in range(PAIRS):
        q = order_ref[2 * PAIRS * chunk + 2 * i] >> 7
        load_packed(leg_ref, packed, i, q)
        values = jnp.concatenate(
            [
                spread[WAVE * i : WAVE * (i + 1), LANES * lat : LANES * (lat + 1)]
                for lat in range(LATS)
            ],
            axis=0,
        )
        values = values.T.astype(BF16)
        result = jnp.dot(values[: 2 * ROWS], packed[...], preferred_element_type=F32)
        for t in range(PB):
            span = slice(LANES * t, LANES * (t + 1))
            if t < NB:
                block = jnp.where(t >= q, result[:ROWS, span], result[ROWS:, span])
            else:
                block = result[ROWS:, span]
            total[t, pl.ds(i, ROWS, stride=PAIRS), :] = block
    for t in range(PB):
        for g in range(FLD):
            out_ref[g, 0, :, LANES * t : LANES * (t + 1)] = total[
                t, ROWS * g : ROWS * (g + 1)
            ].astype(BF16)


def table_kernel(col_ref, row_ref, base_ref, table_ref, turned_ref):
    step = 256
    for at in range(0, M, step):
        lane = lax.broadcasted_iota(I32, (step, BLOCK), 1)
        hot = (lane == (col_ref[at : at + step, :] & (BLOCK - 1))).astype(F32).astype(BF16)
        rows = jnp.dot(hot, base_ref[...], preferred_element_type=F32).astype(BF16)
        table_ref[at : at + step, :] = rows[:, :BLOCK]
        table_ref[M + at : M + at + step, :] = rows[:, BLOCK:]
    for at in range(0, M, step):
        sub = lax.broadcasted_iota(I32, (BLOCK, step), 0)
        hot = (sub == (row_ref[:, at : at + step] & (BLOCK - 1))).astype(F32).astype(BF16)
        for half in range(2):
            turned_ref[:, half * M + at : half * M + at + step] = jnp.dot(
                base_ref[:, half * BLOCK : (half + 1) * BLOCK], hot, preferred_element_type=F32
            ).astype(BF16)


def turn_pair(t):
    a = (t - 0.25) * (2.0 * math.pi)
    s = a * a
    sine = a * (
        1.0
        + s
        * (
            -1.0 / 6
            + s * (1.0 / 120 + s * (-1.0 / 5040 + s * (1.0 / 362880 - s * (1.0 / 39916800))))
        )
    )
    cosine = 1.0 + s * (
        -0.5
        + s
        * (
            1.0 / 24
            + s * (-1.0 / 720 + s * (1.0 / 40320 + s * (-1.0 / 3628800 + s * (1.0 / 479001600))))
        )
    )
    return -sine, cosine


def times(a, b):
    return a[0] * b[0] - a[1] * b[1], a[0] * b[1] + a[1] * b[0]


def back(a, b):
    return a[0] * b[0] + a[1] * b[1], a[1] * b[0] - a[0] * b[1]


def grid_kernel(
    r_ref, col_ref, length_ref, scale_ref, gain_ref, table_ref, turned_ref, out_ref,
    hr, hi, tr, ti, dr, di, hb, ub,
):
    length = length_ref[...]
    halfway = length >> 1
    inverse_length = 1.0 / length.astype(F32)
    srcs = 4
    step = srcs * CHUNKS * 8
    for s in range(0, WAVE, srcs):
        at = s * CHUNKS * 8
        rows = slice(at, at + step)
        m = col_ref[rows, :]
        keep = m < halfway
        t = jnp.where(keep, m.astype(F32) * inverse_length, 0.0)
        one = turn_pair(t)
        two = times(one, one)
        four = times(two, two)
        eight = times(four, four)
        eleven = times(times(eight, two), one)
        x = r_ref[s : s + srcs].reshape(srcs * CHUNKS, 16, LANES).astype(F32)
        x0 = jnp.where(keep, x[:, :8].reshape(step, LANES), 0.0)
        x1 = jnp.where(keep, x[:, 8:].reshape(step, LANES), 0.0)
        h = times((x0, x1), eleven)
        tr[rows], ti[rows] = one
        hr[rows], hi[rows] = h
        dr[rows] = jnp.zeros((step, LANES), F32)
        di[rows] = jnp.zeros((step, LANES), F32)

    count = length >> 9
    gain = gain_ref[...]
    gain2 = jnp.concatenate([gain, gain], axis=1)

    def body(s, carry):
        high = XMAX - 1 - 2 * s
        for at in range(0, M, step):
            rows = slice(at, at + step)
            low = slice(M + at, M + at + step)
            t = tr[rows], ti[rows]
            h = hr[rows], hi[rows]
            hb[rows, :LANES] = h[0].astype(BF16)
            hb[low, :LANES] = h[1].astype(BF16)
            h = back(h, t)
            hb[rows, LANES:] = h[0].astype(BF16)
            hb[low, LANES:] = h[1].astype(BF16)
            hr[rows], hi[rows] = back(h, t)
        live = jnp.concatenate(
            [(high < count).astype(F32), (high - 1 < count).astype(F32)], axis=1
        )
        for at in range(0, BLOCK, 128):
            g = jnp.dot(
                turned_ref[at : at + 128], hb[...], preferred_element_type=F32
            ) * float(M) ** (-0.5)
            ub[at : at + 128] = ((g + gain2 * g * g) * live).astype(BF16)
        for at in range(0, M, step):
            rows = slice(at, at + step)
            low = slice(M + at, M + at + step)
            vr = jnp.dot(table_ref[rows], ub[...], preferred_element_type=F32)
            vi = jnp.dot(table_ref[low], ub[...], preferred_element_type=F32)
            t = tr[rows], ti[rows]
            d = back((dr[rows], di[rows]), t)
            d = d[0] + vr[:, :LANES], d[1] + vi[:, :LANES]
            d = back(d, t)
            dr[rows] = d[0] + vr[:, LANES:]
            di[rows] = d[1] + vi[:, LANES:]
        return carry

    lax.fori_loop(0, XMAX // 2, body, 0)
    scale = scale_ref[...]
    for s in range(0, WAVE, srcs):
        at = s * CHUNKS * 8
        rows = slice(at, at + step)
        keep = col_ref[rows, :] < halfway
        d0 = jnp.where(keep, dr[rows] * scale, 0.0).reshape(srcs * CHUNKS, 8, LANES)
        d1 = jnp.where(keep, di[rows] * scale, 0.0).reshape(srcs * CHUNKS, 8, LANES)
        out_ref[s : s + srcs] = (
            jnp.concatenate([d0, d1], axis=1).reshape(srcs, CHUNKS, 16, LANES).astype(BF16)
        )


def params(mib):
    return pltpu.CompilerParams(vmem_limit_bytes=mib << 20)


SMEM = pl.BlockSpec(memory_space=pltpu.SMEM)
VMEM = pl.BlockSpec(memory_space=pltpu.VMEM)


def local(spec_in, legendre, wave_order, row_length, quad_weight, mixing, square_gain):
    same, pick, rows24, cols24 = lane_maps()
    w = lax.axis_index("wave")
    g = lax.axis_index("fld")
    own = lax.dynamic_slice_in_dim(wave_order, w * 2 * PAIRS * CHUNKS, 2 * PAIRS * CHUNKS)
    lead = own.reshape(CHUNKS, 1, PAIRS, 2)[..., 0]
    row_orders = jnp.broadcast_to(lead[..., None], (CHUNKS, 2 * FD, PAIRS, LANES)).reshape(
        CHUNKS, ROWS, LANES
    )
    x = spec_in.reshape(FD, CHUNKS, PAIRS, 2, 2, M).transpose(3, 1, 4, 0, 2, 5)
    x = x.reshape(2, CHUNKS, ROWS, M)

    chunked = lambda n, width: pl.BlockSpec((n, 1, ROWS, width), lambda i: (0, i, 0, 0))
    orders_spec = pl.BlockSpec((1, ROWS, LANES), lambda i: (i, 0, 0))
    packed = pl.pallas_call(
        pack_kernel,
        grid=(CHUNKS,),
        out_shape=jax.ShapeDtypeStruct((CHUNKS, ROWS, PACKED), BF16),
        in_specs=[chunked(2, M), orders_spec],
        out_specs=pl.BlockSpec((1, ROWS, PACKED), lambda i: (i, 0, 0)),
        compiler_params=params(24),
    )(x, row_orders)
    gathered = lax.all_gather(packed, "fld", axis=0)

    column = wave_order.reshape(WAVE, CHUNKS, PAIRS, 2).transpose(0, 1, 3, 2).reshape(M)
    table, turned = pl.pallas_call(
        table_kernel,
        out_shape=(
            jax.ShapeDtypeStruct((2 * M, BLOCK), BF16),
            jax.ShapeDtypeStruct((BLOCK, 2 * M), BF16),
        ),
        in_specs=[VMEM, VMEM, VMEM],
        out_specs=(VMEM, VMEM),
        compiler_params=params(32),
    )(column[:, None], column[None, :], jnp.asarray(wave_tables()))

    mix = jnp.dot(
        jnp.dot(jnp.asarray(rows24), mixing.T, precision=lax.Precision.HIGHEST),
        jnp.asarray(cols24),
        precision=lax.Precision.HIGHEST,
    ) * jnp.asarray(same)
    mix_high = mix.astype(BF16)
    mix_low = (mix - mix_high.astype(F32)).astype(BF16)
    mix_parts = jnp.stack([mix_high, mix_low])

    leg_spec = pl.BlockSpec((2 * PAIRS, FLD * WAVE, M), lambda i: (i, 0, 0))
    msg_spec = pl.BlockSpec((WAVE, 1, 16, LANES), lambda i: (0, i, 0, 0))
    msg_shape = jax.ShapeDtypeStruct((WAVE, CHUNKS, 16, LANES), BF16)
    sent = pl.pallas_call(
        inverse_kernel,
        grid=(CHUNKS,),
        out_shape=msg_shape,
        in_specs=[
            SMEM,
            chunked(FLD, PACKED),
            leg_spec,
            pl.BlockSpec((2, LATS * LANES, LATS * LANES), lambda i: (0, 0, 0)),
        ],
        out_specs=msg_spec,
        scratch_shapes=[
            pltpu.VMEM((PB, FLD * ROWS, LANES), F32),
            pltpu.VMEM((LANES, PACKED), BF16),
            pltpu.VMEM((PAIRS * WAVE, LATS * LANES), BF16),
            pltpu.VMEM((WAVE * 16, LANES), F32),
        ],
        compiler_params=params(48),
    )(own, gathered, legendre, mix_parts)
    arrived = lax.all_to_all(sent, "wave", split_axis=0, concat_axis=0, tiled=True)

    quarter = lambda a: lax.dynamic_index_in_dim(
        lax.dynamic_slice_in_dim(a, g * LATS * WAVE, LATS * WAVE).reshape(LATS, WAVE), w, 1, False
    )
    lanes = lambda a: jnp.pad(jnp.repeat(a, FL), (0, LANES - LATS * FL), mode="edge")[None, :]
    lengths = quarter(row_length)
    scale = quarter(quad_weight) * lax.rsqrt(lengths.astype(F32))
    gain = jnp.pad(jnp.tile(square_gain, LATS), (0, LANES - LATS * FL))[None, :]
    full = pltpu.VMEM((M, LANES), F32)
    direct = pl.pallas_call(
        grid_kernel,
        out_shape=msg_shape,
        in_specs=[VMEM] * 7,
        out_specs=VMEM,
        scratch_shapes=[full] * 6
        + [pltpu.VMEM((2 * M, 2 * LANES), BF16), pltpu.VMEM((BLOCK, 2 * LANES), BF16)],
        compiler_params=params(48),
    )(arrived, column[:, None], lanes(lengths), lanes(scale), gain, table, turned)
    returned = lax.all_to_all(direct, "wave", split_axis=0, concat_axis=0, tiled=True)

    parts = pl.pallas_call(
        direct_kernel,
        grid=(CHUNKS,),
        out_shape=jax.ShapeDtypeStruct((FLD, CHUNKS, ROWS, PACKED), BF16),
        in_specs=[
            SMEM,
            msg_spec,
            leg_spec,
            pl.BlockSpec((LATS * LANES, LATS * LANES), lambda i: (0, 0)),
        ],
        out_specs=chunked(FLD, PACKED),
        scratch_shapes=[
            pltpu.VMEM((WAVE * 16, LANES), F32),
            pltpu.VMEM((PAIRS * WAVE, LATS * LANES), BF16),
            pltpu.VMEM((LANES, PACKED), BF16),
            pltpu.VMEM((PB, FLD * ROWS, LANES), F32),
        ],
        compiler_params=params(48),
    )(own, returned, legendre, jnp.asarray(pick))
    parts = lax.all_to_all(parts, "fld", split_axis=0, concat_axis=0, tiled=True)

    result = pl.pallas_call(
        unpack_kernel,
        grid=(CHUNKS,),
        out_shape=jax.ShapeDtypeStruct((2, CHUNKS, ROWS, M), F32),
        in_specs=[chunked(FLD, PACKED), orders_spec],
        out_specs=chunked(2, M),
        compiler_params=params(24),
    )(parts, row_orders)
    result = result.reshape(2, CHUNKS, 2, FD, PAIRS, M).transpose(3, 1, 4, 0, 2, 5)
    return result.reshape(FD, 2 * PAIRS * CHUNKS, 2, M)


def solution(mesh):
    in_specs = (P("fld", "wave", None, None), P("wave", "fld", None), P(), P(), P(), P(), P())
    out_specs = P("fld", "wave", None, None)
    return jax.shard_map(local, mesh=mesh, in_specs=in_specs, out_specs=out_specs, check_vma=False)
```

```python
import functools
import math

import jax
import jax.numpy as jnp
import ml_dtypes
import numpy as np
from jax import lax
from jax.experimental import pallas as pl
from jax.experimental.pallas import tpu as pltpu
from jax.sharding import PartitionSpec as P

M = 1280
FL = 24
BLOCK = 512
LANES = 128
NB = M // LANES
PB = NB + 1
PACKED = PB * LANES
CHUNKS = 5
PAIRS = 4
WAVE = 32
FLD = 4
LATS = 4
FD = FL // FLD
ROWS = 2 * FD * PAIRS
XMAX = 12
F32, BF16, I32 = jnp.float32, jnp.bfloat16, jnp.int32


def wave_tables():
    v = np.arange(BLOCK)
    angle = (v[:, None] * v[None, :] % BLOCK) * (2.0 * math.pi / BLOCK)
    return np.concatenate([np.cos(angle), -np.sin(angle)], axis=1).astype(ml_dtypes.bfloat16)


def lane_maps():
    width = LATS * LANES
    lat_a, ab_a, level_a, half_a = (np.full(width, -1) for _ in range(4))
    for lat in range(LATS):
        for ab in range(2):
            for g in range(FLD):
                for c in range(2):
                    for f in range(FD):
                        at = LANES * lat + ((ab * FLD + g) * 2 + c) * FD + f
                        lat_a[at], ab_a[at], half_a[at], level_a[at] = lat, ab, c, FD * g + f
    lat_b, ab_b, level_b, half_b = (np.full(width, -2) for _ in range(4))
    for c in range(2):
        for ab in range(2):
            for lat in range(LATS):
                for f in range(FL):
                    at = LANES * (2 * c + ab) + FL * lat + f
                    lat_b[at], ab_b[at], half_b[at], level_b[at] = lat, ab, c, f
    same = (
        (lat_a[:, None] == lat_b[None, :])
        & (ab_a[:, None] == ab_b[None, :])
        & (half_a[:, None] == half_b[None, :])
    )
    pick = same & (level_a[:, None] == level_b[None, :])
    rows = (level_a[:, None] == np.arange(FL)[None, :]).astype(np.float32)
    cols = (np.arange(FL)[:, None] == level_b[None, :]).astype(np.float32)
    return same.astype(np.float32), pick.T.astype(ml_dtypes.bfloat16), rows, cols


def turn_pair(t):
    a = (t - 0.25) * (2.0 * math.pi)
    s = a * a
    sine = a * (
        1.0
        + s
        * (
            -1.0 / 6
            + s * (1.0 / 120 + s * (-1.0 / 5040 + s * (1.0 / 362880 - s * (1.0 / 39916800))))
        )
    )
    cosine = 1.0 + s * (
        -0.5
        + s
        * (
            1.0 / 24
            + s * (-1.0 / 720 + s * (1.0 / 40320 + s * (-1.0 / 3628800 + s * (1.0 / 479001600))))
        )
    )
    return -sine, cosine


def times(a, b):
    return a[0] * b[0] - a[1] * b[1], a[0] * b[1] + a[1] * b[0]


def back(a, b):
    return a[0] * b[0] + a[1] * b[1], a[1] * b[0] - a[0] * b[1]


LEFT_PART = 5 * LANES
GROUP = 8
MESH = pl.DeviceIdType.MESH


def load_packed(leg_ref, packed_ref, first, q):
    q = jnp.broadcast_to(q.astype(F32), (LANES, LANES)).astype(BF16)
    spare = None
    for t in range(NB):
        one = leg_ref[first, :, LANES * t : LANES * (t + 1)]
        at = NB - 1 - t
        two = leg_ref[first + 1, :, LANES * at : LANES * (at + 1)]
        packed_ref[:, LANES * t : LANES * (t + 1)] = jnp.where(q <= t, one, two)
        spare = two if t == 0 else jnp.where(q == t, two, spare)
    packed_ref[:, LANES * NB :] = spare


def kernel(
    x_ref, orders_ref, leg_ref, col_ref, row_ref, base_ref, mix_ref, pick_ref,
    length_ref, scale_ref, gain_ref, out_ref,
    legs, gathered, coeff, packed, wide, turn, sent, arrived, table, turned, waves, grid, update,
    tr, ti, sent_back, arrived_back, opposite, part_right, part_left, part_own, to_right, to_left,
    first_left, first_right, second_left, second_right,
    leg_sem, ag_send, ag_recv, a_send, a_recv, b_send, b_recv, rs_send, rs_recv,
):
    w = lax.axis_index("wave")
    g = lax.axis_index("fld")
    right, left, across = lax.rem(g + 1, FLD), lax.rem(g + 3, FLD), lax.rem(g + 2, FLD)

    def leg_copy(k):
        rows = pl.ds(k * GROUP, GROUP)
        return pltpu.make_async_copy(leg_ref.at[rows], legs.at[rows], leg_sem.at[k])

    def remote(src, dst, send, recv, to):
        return pltpu.make_async_remote_copy(
            src_ref=src, dst_ref=dst, send_sem=send, recv_sem=recv, device_id=to, device_id_type=MESH
        )

    to_r, to_l = (w, right), (w, left)
    head, rest = pl.ds(0, LEFT_PART), pl.ds(LEFT_PART, PACKED - LEFT_PART)

    def own_right(k):
        block = gathered.at[k, g]
        return remote(block, block, ag_send.at[0, k], ag_recv.at[0, k], to_r)

    def own_left(k):
        block = gathered.at[k, g]
        return remote(block, block, ag_send.at[1, k], ag_recv.at[1, k], to_l)

    def pass_right(k):
        block = gathered.at[k, left, :, head]
        return remote(block, block, ag_send.at[2, k], ag_recv.at[2, k], to_r)

    def pass_left(k):
        block = gathered.at[k, right, :, rest]
        return remote(block, block, ag_send.at[3, k], ag_recv.at[3, k], to_l)

    def sum_first_right(k):
        return remote(
            opposite.at[k, :, head], first_left.at[k], rs_send.at[0, k], rs_recv.at[0, k], to_r
        )

    def sum_first_left(k):
        return remote(
            opposite.at[k, :, rest], first_right.at[k], rs_send.at[1, k], rs_recv.at[1, k], to_l
        )

    def sum_second_right(k):
        return remote(to_right.at[k], second_left.at[k], rs_send.at[2, k], rs_recv.at[2, k], to_r)

    def sum_second_left(k):
        return remote(to_left.at[k], second_right.at[k], rs_send.at[3, k], rs_recv.at[3, k], to_l)

    def exchange_all(k, src, dst, send, recv):
        others = pl.ds(0, WAVE - 1)
        return remote(src.at[k, others], dst.at[k, others], send.at[k], recv.at[k], (w, g))

    def exchange(k, src, dst, send, recv):
        def one(d, carry):
            to = lax.rem(w + d, WAVE)
            remote(src.at[k, to], dst.at[k, w], send.at[k], recv.at[k], (to, g)).start()
            return carry

        lax.fori_loop(1, WAVE, one, 0)
        dst[k, w] = src[k, w]

    for k in range(CHUNKS):
        leg_copy(k).start()
    barrier = pltpu.get_barrier_semaphore()

    def greet(d, carry):
        pl.semaphore_signal(
            barrier, inc=1, device_id=(lax.rem(w + d, WAVE), g), device_id_type=MESH
        )
        return carry

    for to in (to_r, to_l):
        pl.semaphore_signal(barrier, inc=1, device_id=to, device_id_type=MESH)
    lax.fori_loop(1, WAVE, greet, 0)

    lane = lax.broadcasted_iota(I32, (ROWS, LANES), 1)

    def pack(k, carry):
        m = orders_ref[k]
        q = m >> 7
        first, second = [], []
        for t in range(NB):
            n = lane + LANES * t
            span = slice(LANES * t, LANES * (t + 1))
            first.append(jnp.where(n >= m, x_ref[0, k, :, span].astype(F32), 0.0))
            second.append(jnp.where(n >= M - 1 - m, x_ref[1, k, :, span].astype(F32), 0.0))
        spare = second[NB - 1]
        for t in range(NB):
            other = second[NB - 1 - t]
            gathered[k, g, :, LANES * t : LANES * (t + 1)] = jnp.where(
                t >= q, first[t], other
            ).astype(BF16)
            spare = jnp.where(q == t, other, spare)
        gathered[k, g, :, LANES * NB :] = spare.astype(BF16)
        return carry

    lax.fori_loop(0, CHUNKS, pack, 0)
    pl.semaphore_wait(barrier, WAVE + 1)
    for k in range(2):
        own_right(k).start()
        own_left(k).start()

    width = WAVE * GROUP
    half_length = length_ref[...] >> 1
    inverse_length = 1.0 / length_ref[...].astype(F32)
    count = length_ref[...] >> 9

    def tables(k, carry):
        at = pl.ds(pl.multiple_of(k * width, width), width)
        m = col_ref[at, :]
        spot = lax.broadcasted_iota(I32, (width, BLOCK), 1)
        hot = (spot == (m & (BLOCK - 1))).astype(F32).astype(BF16)
        rows = jnp.dot(hot, base_ref[...], preferred_element_type=F32).astype(BF16)
        table[k, :width] = rows[:, :BLOCK]
        table[k, width:] = rows[:, BLOCK:]
        spot = lax.broadcasted_iota(I32, (BLOCK, width), 0)
        hot = (spot == (row_ref[:, at] & (BLOCK - 1))).astype(F32).astype(BF16)
        for half in range(2):
            turned[k, :, half * width : (half + 1) * width] = jnp.dot(
                base_ref[:, half * BLOCK : (half + 1) * BLOCK], hot, preferred_element_type=F32
            ).astype(BF16)
        t = jnp.where(m < half_length, m.astype(F32) * inverse_length, 0.0)
        tr[k], ti[k] = turn_pair(t)
        return carry

    lax.fori_loop(0, CHUNKS, tables, 0)
    for s in range(XMAX // 2):
        grid[s] = jnp.zeros((BLOCK, 2 * LANES), F32)

    def legendre_sum(k):
        for t in range(PB):
            for d in range(FLD):
                coeff[t, ROWS * d : ROWS * (d + 1)] = gathered[
                    k, d, :, LANES * t : LANES * (t + 1)
                ].astype(F32)
        for i in range(PAIRS):
            q = orders_ref[k, i : i + 1, :] >> 7
            load_packed(legs, packed, GROUP * k + 2 * i, q)
            weights = []
            for t in range(PB):
                block = coeff[t, pl.ds(i, ROWS, stride=PAIRS), :]
                lead = jnp.where(q <= t, block, 0.0) if t < NB else jnp.zeros_like(block)
                weights.append(
                    jnp.concatenate([lead, block - lead, jnp.zeros((32, LANES), F32)], axis=0).astype(BF16)
                )
            fourier = lax.dot_general(
                packed[...],
                jnp.concatenate(weights, axis=1),
                (((1,), (1,)), ((), ())),
                preferred_element_type=F32,
            ).astype(BF16)
            for lat in range(LATS):
                wide[WAVE * i : WAVE * (i + 1), LANES * lat : LANES * (lat + 1)] = fourier[
                    WAVE * lat : WAVE * (lat + 1)
                ]
        mixed = jnp.dot(wide[...], mix_ref[0], preferred_element_type=F32) + jnp.dot(
            wide[...], mix_ref[1], preferred_element_type=F32
        )
        for c in range(2):
            for ab in range(2):
                for i in range(PAIRS):
                    at = 2 * c + ab
                    turn[pl.ds(c * 8 + ab * PAIRS + i, WAVE, stride=16), :] = mixed[
                        WAVE * i : WAVE * (i + 1), LANES * at : LANES * (at + 1)
                    ]
        sent[k] = turn[...].reshape(WAVE, 16, LANES).astype(BF16)

    def grid_sum(k):
        keep = col_ref[pl.ds(pl.multiple_of(k * width, width), width), :] < half_length
        one = tr[k], ti[k]
        two = times(one, one)
        four = times(two, two)
        eight = times(four, four)
        eleven = times(times(eight, two), one)
        x = arrived[k].astype(F32)
        x0 = jnp.where(keep, x[:, :8].reshape(width, LANES), 0.0)
        x1 = jnp.where(keep, x[:, 8:].reshape(width, LANES), 0.0)
        h = times((x0, x1), eleven)
        for s in range(XMAX // 2):
            for side in range(2):
                span = slice(LANES * side, LANES * (side + 1))
                waves[s, :width, span] = h[0].astype(BF16)
                waves[s, width:, span] = h[1].astype(BF16)
                h = back(h, one)
        for s in range(XMAX // 2):
            grid[s] += jnp.dot(turned[k], waves[s], preferred_element_type=F32)

    def gather_step(k, carry):
        @pl.when(k < CHUNKS)
        def _():
            own_right(k).wait_recv()
            pass_right(k).start()
            own_left(k).wait_recv()
            pass_left(k).start()

        @pl.when(k + 2 < CHUNKS)
        def _():
            own_right(k + 2).start()
            own_left(k + 2).start()

        @pl.when((k >= 1) & (k <= CHUNKS))
        def _():
            pass_right(k - 1).wait_recv()
            pass_left(k - 1).wait_recv()
            leg_copy(k - 1).wait()
            legendre_sum(k - 1)
            exchange(k - 1, sent, arrived, a_send, a_recv)

        @pl.when(k >= 2)
        def _():
            exchange_all(k - 2, sent, arrived, a_send, a_recv).wait_recv()
            grid_sum(k - 2)

        return carry

    lax.fori_loop(0, CHUNKS + 2, gather_step, 0)

    gain = gain_ref[...]
    gain = jnp.concatenate([gain, gain], axis=1)

    def column(s, carry):
        high = XMAX - 1 - 2 * s
        live = jnp.concatenate(
            [(high < count).astype(F32), (high - 1 < count).astype(F32)], axis=1
        )
        mixed = grid[s] * float(M) ** (-0.5)
        update[s] = ((mixed + gain * mixed * mixed) * live).astype(BF16)
        return carry

    lax.fori_loop(0, XMAX // 2, column, 0)

    def grid_back(k):
        t = tr[k], ti[k]
        d = jnp.zeros((width, LANES), F32), jnp.zeros((width, LANES), F32)
        for s in range(XMAX // 2):
            v = jnp.dot(table[k], update[s], preferred_element_type=F32)
            for side in range(2):
                span = slice(LANES * side, LANES * (side + 1))
                if s + side > 0:
                    d = back(d, t)
                d = d[0] + v[:width, span], d[1] + v[width:, span]
        keep = col_ref[pl.ds(pl.multiple_of(k * width, width), width), :] < half_length
        scale = scale_ref[...]
        d0 = jnp.where(keep, d[0] * scale, 0.0).reshape(WAVE, 8, LANES)
        d1 = jnp.where(keep, d[1] * scale, 0.0).reshape(WAVE, 8, LANES)
        sent_back[k] = jnp.concatenate([d0, d1], axis=1).astype(BF16)

    def legendre_back(k):
        turn[...] = arrived_back[k].reshape(WAVE * 16, LANES).astype(F32)
        for c in range(2):
            for ab in range(2):
                for i in range(PAIRS):
                    at = 2 * c + ab
                    wide[WAVE * i : WAVE * (i + 1), LANES * at : LANES * (at + 1)] = turn[
                        pl.ds(c * 8 + ab * PAIRS + i, WAVE, stride=16), :
                    ].astype(BF16)
        spread = jnp.dot(wide[...], pick_ref[...], preferred_element_type=F32)
        for i in range(PAIRS):
            q = orders_ref[k, i : i + 1, :] >> 7
            load_packed(legs, packed, GROUP * k + 2 * i, q)
            values = jnp.concatenate(
                [
                    spread[WAVE * i : WAVE * (i + 1), LANES * lat : LANES * (lat + 1)]
                    for lat in range(LATS)
                ],
                axis=0,
            )
            values = values.T.astype(BF16)
            result = jnp.dot(values[: 2 * ROWS], packed[...], preferred_element_type=F32)
            for t in range(PB):
                span = slice(LANES * t, LANES * (t + 1))
                if t < NB:
                    block = jnp.where(q <= t, result[:ROWS, span], result[ROWS:, span])
                else:
                    block = result[ROWS:, span]
                coeff[t, pl.ds(i, ROWS, stride=PAIRS), :] = block
        for t in range(PB):
            span = slice(LANES * t, LANES * (t + 1))
            part = lambda d: coeff[t, pl.ds(pl.multiple_of(d * ROWS, 16), ROWS), :]
            opposite[k, :, span] = part(across).astype(BF16)
            part_right[k, :, span] = part(right)
            part_left[k, :, span] = part(left)
            part_own[k, :, span] = part(g)

    def sum_second(k):
        cut = LEFT_PART
        to_right[k, :, :cut] = (part_right[k, :, :cut] + first_left[k].astype(F32)).astype(BF16)
        to_right[k, :, cut:] = part_right[k, :, cut:].astype(BF16)
        to_left[k, :, :cut] = part_left[k, :, :cut].astype(BF16)
        to_left[k, :, cut:] = (part_left[k, :, cut:] + first_right[k].astype(F32)).astype(BF16)

    def unpack(k):
        m = orders_ref[k]
        q = m >> 7
        total = []
        for t in range(PB):
            span = slice(LANES * t, LANES * (t + 1))
            total.append(
                part_own[k, :, span]
                + second_left[k, :, span].astype(F32)
                + second_right[k, :, span].astype(F32)
            )
        moved = [jnp.where(NB - 1 - t == q, total[NB], total[NB - 1 - t]) for t in range(NB)]
        for t in range(NB):
            n = lane + LANES * t
            span = slice(LANES * t, LANES * (t + 1))
            out_ref[0, k, :, span] = jnp.where(n >= m, total[t], 0.0)
            out_ref[1, k, :, span] = jnp.where(n >= M - 1 - m, moved[t], 0.0)

    def scatter_step(k, carry):
        @pl.when((k >= 2) & (k < CHUNKS + 2))
        def _():
            sum_first_right(k - 2).wait_recv()
            sum_first_left(k - 2).wait_recv()
            sum_second(k - 2)
            sum_second_right(k - 2).start()
            sum_second_left(k - 2).start()

        @pl.when(k < CHUNKS)
        def _():
            grid_back(k)
            exchange(k, sent_back, arrived_back, b_send, b_recv)

        @pl.when((k >= 1) & (k < CHUNKS + 1))
        def _():
            exchange_all(k - 1, sent_back, arrived_back, b_send, b_recv).wait_recv()
            legendre_back(k - 1)
            sum_first_right(k - 1).start()
            sum_first_left(k - 1).start()

        @pl.when(k >= 3)
        def _():
            sum_second_right(k - 3).wait_recv()
            sum_second_left(k - 3).wait_recv()
            unpack(k - 3)

        return carry

    lax.fori_loop(0, CHUNKS + 3, scatter_step, 0)

    def finish(k, carry):
        for copy in (own_right, own_left, pass_right, pass_left):
            copy(k).wait_send()
        for copy in (sum_first_right, sum_first_left, sum_second_right, sum_second_left):
            copy(k).wait_send()
        exchange_all(k, sent, arrived, a_send, a_recv).wait_send()
        exchange_all(k, sent_back, arrived_back, b_send, b_recv).wait_send()
        return carry

    lax.fori_loop(0, CHUNKS, finish, 0)


VMEM = pl.BlockSpec(memory_space=pltpu.VMEM)
ANY = pl.BlockSpec(memory_space=pl.ANY)


def local(spec_in, legendre, wave_order, row_length, quad_weight, mixing, square_gain):
    same, pick, rows24, cols24 = lane_maps()
    w = lax.axis_index("wave")
    g = lax.axis_index("fld")
    own = lax.dynamic_slice_in_dim(wave_order, w * GROUP * CHUNKS, GROUP * CHUNKS)
    lead = own.reshape(CHUNKS, 1, PAIRS, 2)[..., 0]
    row_orders = jnp.broadcast_to(lead[..., None], (CHUNKS, 2 * FD, PAIRS, LANES)).reshape(
        CHUNKS, ROWS, LANES
    )
    x = spec_in.reshape(FD, CHUNKS, PAIRS, 2, 2, M).transpose(3, 1, 4, 0, 2, 5)
    x = x.reshape(2, CHUNKS, ROWS, M)

    column = wave_order.reshape(WAVE, CHUNKS, PAIRS, 2).transpose(1, 0, 3, 2).reshape(M)

    mix = jnp.dot(
        jnp.dot(jnp.asarray(rows24), mixing.T, precision=lax.Precision.HIGHEST),
        jnp.asarray(cols24),
        precision=lax.Precision.HIGHEST,
    ) * jnp.asarray(same)
    mix_high = mix.astype(BF16)
    mix_low = (mix - mix_high.astype(F32)).astype(BF16)
    mix_parts = jnp.stack([mix_high, mix_low])

    quarter = lambda a: lax.dynamic_index_in_dim(
        lax.dynamic_slice_in_dim(a, g * LATS * WAVE, LATS * WAVE).reshape(LATS, WAVE), w, 1, False
    )
    lanes = lambda a: jnp.pad(jnp.repeat(a, FL), (0, LANES - LATS * FL), mode="edge")[None, :]
    lengths = quarter(row_length)
    scale = quarter(quad_weight) * lax.rsqrt(lengths.astype(F32))
    gain = jnp.pad(jnp.tile(square_gain, LATS), (0, LANES - LATS * FL))[None, :]

    width = WAVE * GROUP
    message = pltpu.VMEM((CHUNKS, WAVE, 16, LANES), BF16)
    full = pltpu.VMEM((CHUNKS, ROWS, PACKED), F32)
    short = pltpu.VMEM((CHUNKS, ROWS, PACKED), BF16)
    copies = pltpu.SemaphoreType.DMA((4, CHUNKS))
    each = pltpu.SemaphoreType.DMA((CHUNKS,))
    result = pl.pallas_call(
        kernel,
        out_shape=jax.ShapeDtypeStruct((2, CHUNKS, ROWS, M), F32),
        in_specs=[VMEM, VMEM, ANY] + [VMEM] * 8,
        out_specs=VMEM,
        scratch_shapes=[
            pltpu.VMEM((GROUP * CHUNKS, FLD * WAVE, M), BF16),
            pltpu.VMEM((CHUNKS, FLD, ROWS, PACKED), BF16),
            pltpu.VMEM((PB, FLD * ROWS, LANES), F32),
            pltpu.VMEM((LANES, PACKED), BF16),
            pltpu.VMEM((PAIRS * WAVE, LATS * LANES), BF16),
            pltpu.VMEM((WAVE * 16, LANES), F32),
            message,
            message,
            pltpu.VMEM((CHUNKS, 2 * width, BLOCK), BF16),
            pltpu.VMEM((CHUNKS, BLOCK, 2 * width), BF16),
            pltpu.VMEM((XMAX // 2, 2 * width, 2 * LANES), BF16),
            pltpu.VMEM((XMAX // 2, BLOCK, 2 * LANES), F32),
            pltpu.VMEM((XMAX // 2, BLOCK, 2 * LANES), BF16),
            pltpu.VMEM((CHUNKS, width, LANES), F32),
            pltpu.VMEM((CHUNKS, width, LANES), F32),
            message,
            message,
            short,
            full,
            full,
            full,
            short,
            short,
            pltpu.VMEM((CHUNKS, ROWS, LEFT_PART), BF16),
            pltpu.VMEM((CHUNKS, ROWS, PACKED - LEFT_PART), BF16),
            short,
            short,
            each,
            copies,
            copies,
            each,
            each,
            each,
            each,
            copies,
            copies,
        ],
        compiler_params=pltpu.CompilerParams(
            collective_id=0, has_side_effects=True, vmem_limit_bytes=58 << 20
        ),
    )(
        x, row_orders, legendre, column[:, None], column[None, :], jnp.asarray(wave_tables()),
        mix_parts, jnp.asarray(pick), lanes(lengths), lanes(scale), gain,
    )
    result = result.reshape(2, CHUNKS, 2, FD, PAIRS, M).transpose(3, 1, 4, 0, 2, 5)
    return result.reshape(FD, GROUP * CHUNKS, 2, M)


def solution(mesh):
    in_specs = (P("fld", "wave", None, None), P("wave", "fld", None), P(), P(), P(), P(), P())
    out_specs = P("fld", "wave", None, None)
    return jax.shard_map(local, mesh=mesh, in_specs=in_specs, out_specs=out_specs, check_vma=False)
```

```python
import functools
import math

import jax
import jax.numpy as jnp
import numpy as np
from jax import lax
from jax.experimental import pallas as pl
from jax.experimental.pallas import tpu as pltpu
from jax.sharding import PartitionSpec as P

M = 1280
FL = 24
BLOCK = 512
LANES = 128
NB = M // LANES
PB = NB + 1
PACKED = PB * LANES
CHUNKS = 5
PAIRS = 4
WAVE = 32
FLD = 4
LATS = 4
FD = FL // FLD
ROWS = 2 * FD * PAIRS
XMAX = 12
F32, BF16, I32 = jnp.float32, jnp.bfloat16, jnp.int32


def wave_tables():
    v = np.arange(BLOCK)
    angle = (v[:, None] * v[None, :] % BLOCK) * (2.0 * math.pi / BLOCK)
    return np.concatenate([np.cos(angle), -np.sin(angle)], axis=1).astype(np.float32)


def lane_maps():
    width = LATS * LANES
    lat_a, ab_a, level_a, half_a = (np.full(width, -1) for _ in range(4))
    for lat in range(LATS):
        for ab in range(2):
            for g in range(FLD):
                for c in range(2):
                    for f in range(FD):
                        at = LANES * lat + ((ab * FLD + g) * 2 + c) * FD + f
                        lat_a[at], ab_a[at], half_a[at], level_a[at] = lat, ab, c, FD * g + f
    lat_b, ab_b, level_b, half_b = (np.full(width, -2) for _ in range(4))
    for c in range(2):
        for ab in range(2):
            for lat in range(LATS):
                for f in range(FL):
                    at = LANES * (2 * c + ab) + FL * lat + f
                    lat_b[at], ab_b[at], half_b[at], level_b[at] = lat, ab, c, f
    same = (
        (lat_a[:, None] == lat_b[None, :])
        & (ab_a[:, None] == ab_b[None, :])
        & (half_a[:, None] == half_b[None, :])
    )
    pick = same & (level_a[:, None] == level_b[None, :])
    return pick.T.astype(np.float32)


def turn_pair(t):
    a = (t - 0.25) * (2.0 * math.pi)
    s = a * a
    sine = a * (
        1.0
        + s
        * (
            -1.0 / 6
            + s * (1.0 / 120 + s * (-1.0 / 5040 + s * (1.0 / 362880 - s * (1.0 / 39916800))))
        )
    )
    cosine = 1.0 + s * (
        -0.5
        + s
        * (
            1.0 / 24
            + s * (-1.0 / 720 + s * (1.0 / 40320 + s * (-1.0 / 3628800 + s * (1.0 / 479001600))))
        )
    )
    return -sine, cosine


def times(a, b):
    return a[0] * b[0] - a[1] * b[1], a[0] * b[1] + a[1] * b[0]


def back(a, b):
    return a[0] * b[0] + a[1] * b[1], a[1] * b[0] - a[0] * b[1]


LEFT_PART = 5 * LANES
GROUP = 8
MESH = pl.DeviceIdType.MESH


def load_packed(leg_ref, packed_ref, first, q):
    q = jnp.broadcast_to(q.astype(F32), (LANES, LANES)).astype(BF16)
    spare = None
    for t in range(NB):
        one = leg_ref[first, :, LANES * t : LANES * (t + 1)]
        at = NB - 1 - t
        two = leg_ref[first + 1, :, LANES * at : LANES * (at + 1)]
        packed_ref[:, LANES * t : LANES * (t + 1)] = jnp.where(q <= t, one, two)
        spare = two if t == 0 else jnp.where(q == t, two, spare)
    packed_ref[:, LANES * NB :] = spare


def kernel(
    spec_ref, leg_ref, fixed_ref, own_ref, lengths_ref, weights_ref, gains_ref,
    order_ref, mixing_ref, out_ref,
    legs, base_ref, pick_ref, turn_ref, spec, rows, orders, mix_ref, column_orders,
    gathered, coeff, packed, wide, turn, sent, arrived, table, turned, waves, grid, update,
    tr, ti, sent_back, arrived_back, opposite, part_right, part_left, part_own, to_right, to_left,
    first_left, first_right, second_left, second_right, results,
    leg_sem, spec_sem, const_sem, out_sem, ag_send, ag_recv, a_send, a_recv, b_send, b_recv,
    rs_send, rs_recv,
):
    w = lax.axis_index("wave")
    g = lax.axis_index("fld")
    right, left, across = lax.rem(g + 1, FLD), lax.rem(g + 3, FLD), lax.rem(g + 2, FLD)

    def spec_copy(k):
        return pltpu.make_async_copy(
            spec_ref.at[:, pl.ds(k * GROUP, GROUP)], spec.at[k], spec_sem.at[k]
        )

    def out_copy(k):
        return pltpu.make_async_copy(results.at[k], out_ref.at[:, k], out_sem.at[k])

    fixed_copy = pltpu.make_async_copy(fixed_ref, grid, const_sem)

    def leg_copy(k):
        rows = pl.ds(k * GROUP, GROUP)
        return pltpu.make_async_copy(leg_ref.at[rows], legs.at[rows], leg_sem.at[k])

    def remote(src, dst, send, recv, to):
        return pltpu.make_async_remote_copy(
            src_ref=src, dst_ref=dst, send_sem=send, recv_sem=recv, device_id=to, device_id_type=MESH
        )

    to_r, to_l = (w, right), (w, left)
    head, rest = pl.ds(0, LEFT_PART), pl.ds(LEFT_PART, PACKED - LEFT_PART)

    def own_right(k):
        block = gathered.at[k, g]
        return remote(block, block, ag_send.at[0, k], ag_recv.at[0, k], to_r)

    def own_left(k):
        block = gathered.at[k, g]
        return remote(block, block, ag_send.at[1, k], ag_recv.at[1, k], to_l)

    def pass_right(k):
        block = gathered.at[k, left, :, head]
        return remote(block, block, ag_send.at[2, k], ag_recv.at[2, k], to_r)

    def pass_left(k):
        block = gathered.at[k, right, :, rest]
        return remote(block, block, ag_send.at[3, k], ag_recv.at[3, k], to_l)

    def sum_first_right(k):
        return remote(
            opposite.at[k, :, head], first_left.at[k], rs_send.at[0, k], rs_recv.at[0, k], to_r
        )

    def sum_first_left(k):
        return remote(
            opposite.at[k, :, rest], first_right.at[k], rs_send.at[1, k], rs_recv.at[1, k], to_l
        )

    def sum_second_right(k):
        return remote(to_right.at[k], second_left.at[k], rs_send.at[2, k], rs_recv.at[2, k], to_r)

    def sum_second_left(k):
        return remote(to_left.at[k], second_right.at[k], rs_send.at[3, k], rs_recv.at[3, k], to_l)

    def exchange_all(k, src, dst, send, recv):
        others = pl.ds(0, WAVE - 1)
        return remote(src.at[k, others], dst.at[k, others], send.at[k], recv.at[k], (w, g))

    def exchange(k, src, dst, send, recv):
        def one(d, carry):
            to = lax.rem(w + d, WAVE)
            remote(src.at[k, to], dst.at[k, w], send.at[k], recv.at[k], (to, g)).start()
            return carry

        lax.fori_loop(1, WAVE, one, 0)
        dst[k, w] = src[k, w]

    for k in range(CHUNKS):
        spec_copy(k).start()
    fixed_copy.start()
    for k in range(CHUNKS):
        leg_copy(k).start()
    barrier = pltpu.get_barrier_semaphore()

    def greet(d, carry):
        pl.semaphore_signal(
            barrier, inc=1, device_id=(lax.rem(w + d, WAVE), g), device_id_type=MESH
        )
        return carry

    for to in (to_r, to_l):
        pl.semaphore_signal(barrier, inc=1, device_id=to, device_id_type=MESH)
    lax.fori_loop(1, WAVE, greet, 0)

    lane = lax.broadcasted_iota(I32, (ROWS, LANES), 1)
    pair_of_row = lax.broadcasted_iota(I32, (ROWS, LANES), 0) & (PAIRS - 1)

    def pack(k):
        first_row = (w * CHUNKS + k) * GROUP
        m = jnp.full((ROWS, LANES), own_ref[first_row], I32)
        for i in range(1, PAIRS):
            m = jnp.where(pair_of_row == i, own_ref[first_row + 2 * i], m)
        orders[k] = m
        q = m >> 7
        spec_copy(k).wait()
        for f in range(FD):
            for r in range(GROUP):
                values = spec[k, f, r].astype(F32)
                at = 2 * (f * GROUP + r)
                for t in range(NB):
                    rows[t, at : at + 2, :] = values[:, LANES * t : LANES * (t + 1)]
        first, second = [], []
        for t in range(NB):
            n = lane + LANES * t
            half = [
                jnp.concatenate(
                    [rows[t, pl.ds(2 * ab + c, FD * PAIRS, stride=4), :] for c in range(2)], axis=0
                )
                for ab in range(2)
            ]
            first.append(jnp.where(n >= m, half[0], 0.0))
            second.append(jnp.where(n >= M - 1 - m, half[1], 0.0))
        spare = second[NB - 1]
        for t in range(NB):
            other = second[NB - 1 - t]
            gathered[k, g, :, LANES * t : LANES * (t + 1)] = jnp.where(
                t >= q, first[t], other
            ).astype(BF16)
            spare = jnp.where(q == t, other, spare)
        gathered[k, g, :, LANES * NB :] = spare.astype(BF16)

    def first_pack(k, carry):
        pack(k)

        @pl.when(k == 0)
        def _():
            pl.semaphore_wait(barrier, WAVE + 1)

        own_right(k).start()
        own_left(k).start()
        return carry

    lax.fori_loop(0, 2, first_pack, 0)

    spot = lax.broadcasted_iota(I32, (1, LANES), 1)
    lat_of = lambda x: sum((x >= FL * n).astype(I32) for n in range(1, LATS))
    level_of = lambda x: x - FL * lat_of(x)
    length, weight = jnp.zeros((1, LANES), I32), jnp.zeros((1, LANES), F32)
    for lat in range(LATS):
        at = (g * LATS + lat) * WAVE + w
        length = jnp.where(spot >= FL * lat, lengths_ref[at], length)
        weight = jnp.where(spot >= FL * lat, weights_ref[at], weight)
    gain = jnp.zeros((1, LANES), F32)
    for f in range(FL):
        gain = jnp.where(level_of(spot) == f, gains_ref[f], gain)
    gain = jnp.concatenate([gain, gain], axis=1)
    real_length = length.astype(F32)
    root = lax.rsqrt(real_length)
    scale = weight * (root * (1.5 - 0.5 * real_length * root * root))
    half_length = length >> 1
    inverse_length = 1.0 / real_length
    count = length >> 9

    spot = lax.broadcasted_iota(I32, (FL, LANES), 1)
    level = lax.broadcasted_iota(I32, (FL, LANES), 0)
    hot = ((level_of(spot) == level) & (spot < LATS * FL)).astype(F32)
    across_levels = (((0,), (0,)), ((), ()))
    spread = lax.dot_general(
        mixing_ref[...], hot, across_levels, precision=lax.Precision.HIGHEST,
        preferred_element_type=F32,
    )
    spread = lax.dot_general(
        hot, spread, across_levels, precision=lax.Precision.HIGHEST, preferred_element_type=F32
    )
    lats = [lat_of(lax.broadcasted_iota(I32, (LANES, LANES), dim)) for dim in range(2)]
    spread = jnp.where(lats[0] == lats[1], spread, 0.0)
    high_part = spread.astype(BF16)
    mix_ref[:LANES] = high_part
    mix_ref[LANES:] = (spread - high_part.astype(F32)).astype(BF16)

    width = WAVE * GROUP

    def tables(k):
        spot = lax.broadcasted_iota(I32, (width, LANES), 1)
        row = lax.broadcasted_iota(I32, (width, LANES), 0)
        row = (row >> 3) * (CHUNKS * GROUP) + k * GROUP + (row & 7)
        m = jnp.broadcast_to(order_ref[0:1, :], (width, LANES))
        for n in range(1, NB):
            m = jnp.where((row >> 7) == n, order_ref[n : n + 1, :], m)
        m = jnp.where(spot == (row & 127), m, 0).astype(F32)
        m = jnp.broadcast_to(jnp.sum(m, axis=1, keepdims=True), (width, LANES))
        across_lanes = m.T[0:1, :].astype(I32)
        m = m.astype(I32)
        column_orders[k] = m
        t = jnp.where(m < half_length, m.astype(F32) * inverse_length, 0.0)
        tr[k], ti[k] = turn_pair(t)

        spot = lax.broadcasted_iota(I32, (width, BLOCK), 1)
        m = jnp.concatenate([m & (BLOCK - 1)] * (BLOCK // LANES), axis=1)
        hot = (spot == m).astype(F32).astype(BF16)
        lines = jnp.dot(hot, base_ref[...], preferred_element_type=F32).astype(BF16)
        table[k, :width] = lines[:, :BLOCK]
        table[k, width:] = lines[:, BLOCK:]
        spot = lax.broadcasted_iota(I32, (BLOCK, width), 0)
        hot = (spot == (across_lanes & (BLOCK - 1))).astype(F32).astype(BF16)
        for half in range(2):
            turned[k, :, half * width : (half + 1) * width] = jnp.dot(
                base_ref[:, half * BLOCK : (half + 1) * BLOCK], hot, preferred_element_type=F32
            ).astype(BF16)

    fixed_copy.wait()
    side = 2 * LANES
    for n in range(4):
        base_ref[:, side * n : side * (n + 1)] = grid[n].astype(BF16)
    for n in range(2):
        pick_ref[:, side * n : side * (n + 1)] = grid[4 + n].astype(BF16)
        turn_ref[side * n : side * (n + 1), :] = grid[4 + n].T.astype(BF16)
    for s in range(XMAX // 2):
        grid[s] = jnp.zeros((BLOCK, side), F32)

    def legendre_sum(k):
        for t in range(PB):
            for d in range(FLD):
                coeff[t, ROWS * d : ROWS * (d + 1)] = gathered[
                    k, d, :, LANES * t : LANES * (t + 1)
                ].astype(F32)
        for i in range(PAIRS):
            q = orders[k, i : i + 1, :] >> 7
            load_packed(legs, packed, GROUP * k + 2 * i, q)
            weights = []
            for t in range(PB):
                block = coeff[t, pl.ds(i, ROWS, stride=PAIRS), :]
                lead = jnp.where(q <= t, block, 0.0) if t < NB else jnp.zeros_like(block)
                weights.append(
                    jnp.concatenate([lead, block - lead, jnp.zeros((32, LANES), F32)], axis=0).astype(BF16)
                )
            fourier = lax.dot_general(
                packed[...],
                jnp.concatenate(weights, axis=1),
                (((1,), (1,)), ((), ())),
                preferred_element_type=F32,
            ).astype(BF16)
            for lat in range(LATS):
                wide[WAVE * i : WAVE * (i + 1), LANES * lat : LANES * (lat + 1)] = fourier[
                    WAVE * lat : WAVE * (lat + 1)
                ]
        placed = jnp.dot(wide[...], turn_ref[...], preferred_element_type=F32)
        for c in range(2):
            for ab in range(2):
                for i in range(PAIRS):
                    at = 2 * c + ab
                    turn[pl.ds(c * 8 + 2 * i + ab, WAVE, stride=16), :] = placed[
                        WAVE * i : WAVE * (i + 1), LANES * at : LANES * (at + 1)
                    ]
        sent[k] = turn[...].reshape(WAVE, 16, LANES).astype(BF16)

    def grid_sum(k):
        keep = column_orders[k] < half_length
        one = tr[k], ti[k]
        two = times(one, one)
        four = times(two, two)
        eight = times(four, four)
        eleven = times(times(eight, two), one)
        x = arrived[k].astype(F32)
        x = jnp.concatenate(
            [x[:, :8].reshape(width, LANES), x[:, 8:].reshape(width, LANES)], axis=0
        ).astype(BF16)
        x = jnp.dot(
            jnp.concatenate([x, x], axis=1), mix_ref[...], preferred_element_type=F32
        )
        x0 = jnp.where(keep, x[:width], 0.0)
        x1 = jnp.where(keep, x[width:], 0.0)
        h = times((x0, x1), eleven)
        for s in range(XMAX // 2):
            for side in range(2):
                span = slice(LANES * side, LANES * (side + 1))
                waves[s, :width, span] = h[0].astype(BF16)
                waves[s, width:, span] = h[1].astype(BF16)
                h = back(h, one)
        for s in range(XMAX // 2):
            grid[s] += jnp.dot(turned[k], waves[s], preferred_element_type=F32)

    def gather_step(k, carry):
        @pl.when(k < CHUNKS)
        def _():
            tables(k)

        @pl.when(k + 2 < CHUNKS)
        def _():
            pack(k + 2)

        @pl.when(k < CHUNKS)
        def _():
            own_right(k).wait_recv()
            pass_right(k).start()
            own_left(k).wait_recv()
            pass_left(k).start()

        @pl.when(k + 2 < CHUNKS)
        def _():
            own_right(k + 2).start()
            own_left(k + 2).start()

        @pl.when((k >= 1) & (k <= CHUNKS))
        def _():
            pass_right(k - 1).wait_recv()
            pass_left(k - 1).wait_recv()
            leg_copy(k - 1).wait()
            legendre_sum(k - 1)
            exchange(k - 1, sent, arrived, a_send, a_recv)

        @pl.when(k >= 2)
        def _():
            exchange_all(k - 2, sent, arrived, a_send, a_recv).wait_recv()
            grid_sum(k - 2)

        return carry

    lax.fori_loop(0, CHUNKS + 2, gather_step, 0)

    def column(s, carry):
        high = XMAX - 1 - 2 * s
        live = jnp.concatenate(
            [(high < count).astype(F32), (high - 1 < count).astype(F32)], axis=1
        )
        mixed = grid[s] * float(M) ** (-0.5)
        update[s] = ((mixed + gain * mixed * mixed) * live).astype(BF16)
        return carry

    lax.fori_loop(0, XMAX // 2, column, 0)

    def grid_back(k):
        t = tr[k], ti[k]
        d = jnp.zeros((width, LANES), F32), jnp.zeros((width, LANES), F32)
        for s in range(XMAX // 2):
            v = jnp.dot(table[k], update[s], preferred_element_type=F32)
            for side in range(2):
                span = slice(LANES * side, LANES * (side + 1))
                if s + side > 0:
                    d = back(d, t)
                d = d[0] + v[:width, span], d[1] + v[width:, span]
        keep = column_orders[k] < half_length
        d0 = jnp.where(keep, d[0] * scale, 0.0).reshape(WAVE, 8, LANES)
        d1 = jnp.where(keep, d[1] * scale, 0.0).reshape(WAVE, 8, LANES)
        sent_back[k] = jnp.concatenate([d0, d1], axis=1).astype(BF16)

    def legendre_back(k):
        turn[...] = arrived_back[k].reshape(WAVE * 16, LANES).astype(F32)
        for c in range(2):
            for ab in range(2):
                for i in range(PAIRS):
                    at = 2 * c + ab
                    wide[WAVE * i : WAVE * (i + 1), LANES * at : LANES * (at + 1)] = turn[
                        pl.ds(c * 8 + 2 * i + ab, WAVE, stride=16), :
                    ].astype(BF16)
        spread = jnp.dot(wide[...], pick_ref[...], preferred_element_type=F32)
        for i in range(PAIRS):
            q = orders[k, i : i + 1, :] >> 7
            load_packed(legs, packed, GROUP * k + 2 * i, q)
            values = jnp.concatenate(
                [
                    spread[WAVE * i : WAVE * (i + 1), LANES * lat : LANES * (lat + 1)]
                    for lat in range(LATS)
                ],
                axis=0,
            )
            values = values.T.astype(BF16)
            result = jnp.dot(values[: 2 * ROWS], packed[...], preferred_element_type=F32)
            for t in range(PB):
                span = slice(LANES * t, LANES * (t + 1))
                if t < NB:
                    block = jnp.where(q <= t, result[:ROWS, span], result[ROWS:, span])
                else:
                    block = result[ROWS:, span]
                coeff[t, pl.ds(i, ROWS, stride=PAIRS), :] = block
        for t in range(PB):
            span = slice(LANES * t, LANES * (t + 1))
            part = lambda d: coeff[t, pl.ds(pl.multiple_of(d * ROWS, 16), ROWS), :]
            opposite[k, :, span] = part(across).astype(BF16)
            part_right[k, :, span] = part(right)
            part_left[k, :, span] = part(left)
            part_own[k, :, span] = part(g)

    def sum_second(k):
        cut = LEFT_PART
        to_right[k, :, :cut] = (part_right[k, :, :cut] + first_left[k].astype(F32)).astype(BF16)
        to_right[k, :, cut:] = part_right[k, :, cut:].astype(BF16)
        to_left[k, :, :cut] = part_left[k, :, :cut].astype(BF16)
        to_left[k, :, cut:] = (part_left[k, :, cut:] + first_right[k].astype(F32)).astype(BF16)

    def unpack(k):
        m = orders[k]
        q = m >> 7
        total = []
        for t in range(PB):
            span = slice(LANES * t, LANES * (t + 1))
            total.append(
                part_own[k, :, span]
                + second_left[k, :, span].astype(F32)
                + second_right[k, :, span].astype(F32)
            )
        for t in range(NB):
            n = lane + LANES * t
            other = jnp.where(NB - 1 - t == q, total[NB], total[NB - 1 - t])
            both = jnp.where(n >= m, total[t], 0.0), jnp.where(n >= M - 1 - m, other, 0.0)
            count = FD * PAIRS
            for ab in range(2):
                for c in range(2):
                    rows[t, pl.ds(2 * ab + c, count, stride=4), :] = both[ab][count * c : count * (c + 1)]
            for f in range(FD):
                results[k, f, :, LANES * t : LANES * (t + 1)] = rows[t, 16 * f : 16 * (f + 1), :]

    def back_step(k):
        grid_back(k)
        exchange(k, sent_back, arrived_back, b_send, b_recv)

    def ahead(k, carry):
        back_step(k)
        return carry

    lax.fori_loop(0, 3, ahead, 0)

    def scatter_step(k, carry):
        @pl.when(k < CHUNKS)
        def _():
            exchange_all(k, sent_back, arrived_back, b_send, b_recv).wait_recv()
            legendre_back(k)
            sum_first_right(k).start()
            sum_first_left(k).start()

        @pl.when((k >= 1) & (k <= CHUNKS))
        def _():
            sum_first_right(k - 1).wait_recv()
            sum_first_left(k - 1).wait_recv()
            sum_second(k - 1)
            sum_second_right(k - 1).start()
            sum_second_left(k - 1).start()

        @pl.when((k >= 1) & (k + 2 < CHUNKS))
        def _():
            back_step(k + 2)

        @pl.when(k >= 4)
        def _():
            sum_second_right(k - 4).wait_recv()
            sum_second_left(k - 4).wait_recv()
            unpack(k - 4)
            out_copy(k - 4).start()

        return carry

    lax.fori_loop(0, CHUNKS + 4, scatter_step, 0)

    def finish(k, carry):
        for copy in (own_right, own_left, pass_right, pass_left):
            copy(k).wait_send()
        for copy in (sum_first_right, sum_first_left, sum_second_right, sum_second_left):
            copy(k).wait_send()
        exchange_all(k, sent, arrived, a_send, a_recv).wait_send()
        exchange_all(k, sent_back, arrived_back, b_send, b_recv).wait_send()
        out_copy(k).wait()
        return carry

    lax.fori_loop(0, CHUNKS, finish, 0)


VMEM = pl.BlockSpec(memory_space=pltpu.VMEM)
SMEM = pl.BlockSpec(memory_space=pltpu.SMEM)
ANY = pl.BlockSpec(memory_space=pl.ANY)


def local(spec_in, legendre, wave_order, row_length, quad_weight, mixing, square_gain):
    fixed = np.concatenate([wave_tables(), lane_maps()], axis=1)
    fixed = fixed.reshape(BLOCK, XMAX // 2, 2 * LANES).transpose(1, 0, 2)
    width = WAVE * GROUP
    message = pltpu.VMEM((CHUNKS, WAVE, 16, LANES), BF16)
    full = pltpu.VMEM((CHUNKS, ROWS, PACKED), F32)
    short = pltpu.VMEM((CHUNKS, ROWS, PACKED), BF16)
    turns = pltpu.VMEM((CHUNKS, width, LANES), F32)
    places = pltpu.VMEM((LATS * LANES, LATS * LANES), BF16)
    copies = pltpu.SemaphoreType.DMA((4, CHUNKS))
    each = pltpu.SemaphoreType.DMA((CHUNKS,))
    result = pl.pallas_call(
        kernel,
        out_shape=jax.ShapeDtypeStruct((FD, CHUNKS, 4 * PAIRS, M), F32),
        in_specs=[ANY] * 3 + [SMEM] * 4 + [VMEM] * 2,
        out_specs=ANY,
        scratch_shapes=[
            pltpu.VMEM((GROUP * CHUNKS, FLD * WAVE, M), BF16),
            pltpu.VMEM((BLOCK, 2 * BLOCK), BF16),
            places,
            places,
            pltpu.VMEM((CHUNKS, FD, GROUP, 2, M), BF16),
            pltpu.VMEM((NB, 2 * ROWS, LANES), F32),
            pltpu.VMEM((CHUNKS, ROWS, LANES), I32),
            pltpu.VMEM((2 * LANES, LANES), BF16),
            pltpu.VMEM((CHUNKS, width, LANES), I32),
            pltpu.VMEM((CHUNKS, FLD, ROWS, PACKED), BF16),
            pltpu.VMEM((PB, FLD * ROWS, LANES), F32),
            pltpu.VMEM((LANES, PACKED), BF16),
            pltpu.VMEM((PAIRS * WAVE, LATS * LANES), BF16),
            pltpu.VMEM((WAVE * 16, LANES), F32),
            message,
            message,
            pltpu.VMEM((CHUNKS, 2 * width, BLOCK), BF16),
            pltpu.VMEM((CHUNKS, BLOCK, 2 * width), BF16),
            pltpu.VMEM((XMAX // 2, 2 * width, 2 * LANES), BF16),
            pltpu.VMEM((XMAX // 2, BLOCK, 2 * LANES), F32),
            pltpu.VMEM((XMAX // 2, BLOCK, 2 * LANES), BF16),
            turns,
            turns,
            message,
            message,
            short,
            full,
            full,
            full,
            short,
            short,
            pltpu.VMEM((CHUNKS, ROWS, LEFT_PART), BF16),
            pltpu.VMEM((CHUNKS, ROWS, PACKED - LEFT_PART), BF16),
            short,
            short,
            pltpu.VMEM((CHUNKS, FD, 4 * PAIRS, M), F32),
            each,
            each,
            pltpu.SemaphoreType.DMA,
            each,
            copies,
            copies,
            each,
            each,
            each,
            each,
            copies,
            copies,
        ],
        compiler_params=pltpu.CompilerParams(
            collective_id=0, has_side_effects=True, vmem_limit_bytes=60 << 20
        ),
    )(
        spec_in, legendre, jnp.asarray(fixed),
        wave_order, row_length, quad_weight, square_gain,
        wave_order.reshape(NB, LANES), mixing,
    )
    return result.reshape(FD, GROUP * CHUNKS, 2, M)


def solution(mesh):
    in_specs = (P("fld", "wave", None, None), P("wave", "fld", None), P(), P(), P(), P(), P())
    out_specs = P("fld", "wave", None, None)
    return jax.shard_map(local, mesh=mesh, in_specs=in_specs, out_specs=out_specs, check_vma=False)
```

```python
import functools
import math

import jax
import jax.numpy as jnp
import numpy as np
from jax import lax
from jax.experimental import pallas as pl
from jax.experimental.pallas import tpu as pltpu
from jax.sharding import PartitionSpec as P

M = 1280
FL = 24
BLOCK = 512
LANES = 128
NB = M // LANES
PB = NB + 1
PACKED = PB * LANES
CHUNKS = 5
PAIRS = 4
WAVE = 32
FLD = 4
LATS = 4
FD = FL // FLD
ROWS = 2 * FD * PAIRS
XMAX = 12
F32, BF16, I32 = jnp.float32, jnp.bfloat16, jnp.int32


def wave_tables():
    v = np.arange(BLOCK)
    angle = (v[:, None] * v[None, :] % BLOCK) * (2.0 * math.pi / BLOCK)
    return np.concatenate([np.cos(angle), -np.sin(angle)], axis=1).astype(np.float32)


def lane_maps():
    width = LATS * LANES
    lat_a, ab_a, level_a, half_a = (np.full(width, -1) for _ in range(4))
    for lat in range(LATS):
        for ab in range(2):
            for g in range(FLD):
                for c in range(2):
                    for f in range(FD):
                        at = LANES * lat + ((ab * FLD + g) * 2 + c) * FD + f
                        lat_a[at], ab_a[at], half_a[at], level_a[at] = lat, ab, c, FD * g + f
    lat_b, ab_b, level_b, half_b = (np.full(width, -2) for _ in range(4))
    for c in range(2):
        for ab in range(2):
            for lat in range(LATS):
                for f in range(FL):
                    at = LANES * (2 * c + ab) + FL * lat + f
                    lat_b[at], ab_b[at], half_b[at], level_b[at] = lat, ab, c, f
    same = (
        (lat_a[:, None] == lat_b[None, :])
        & (ab_a[:, None] == ab_b[None, :])
        & (half_a[:, None] == half_b[None, :])
    )
    pick = same & (level_a[:, None] == level_b[None, :])
    return pick.T.astype(np.float32)


def turn_pair(t):
    a = (t - 0.25) * (2.0 * math.pi)
    s = a * a
    sine = a * (
        1.0
        + s
        * (
            -1.0 / 6
            + s * (1.0 / 120 + s * (-1.0 / 5040 + s * (1.0 / 362880 - s * (1.0 / 39916800))))
        )
    )
    cosine = 1.0 + s * (
        -0.5
        + s
        * (
            1.0 / 24
            + s * (-1.0 / 720 + s * (1.0 / 40320 + s * (-1.0 / 3628800 + s * (1.0 / 479001600))))
        )
    )
    return -sine, cosine


def times(a, b):
    return a[0] * b[0] - a[1] * b[1], a[0] * b[1] + a[1] * b[0]


def back(a, b):
    return a[0] * b[0] + a[1] * b[1], a[1] * b[0] - a[0] * b[1]


LEFT_PART = 5 * LANES
GROUP = 8
MESH = pl.DeviceIdType.MESH
OTHERS = sorted(
    ((dz, dx, dc) for dz in range(4) for dx in range(4) for dc in range(2) if dz + dx + dc > 0),
    key=lambda d: -(min(d[0], 4 - d[0]) + min(d[1], 4 - d[1])),
)


def load_packed(leg_ref, packed_ref, first, q):
    q = jnp.broadcast_to(q.astype(F32), (LANES, LANES)).astype(BF16)
    spare = None
    for t in range(NB):
        one = leg_ref[first, :, LANES * t : LANES * (t + 1)]
        at = NB - 1 - t
        two = leg_ref[first + 1, :, LANES * at : LANES * (at + 1)]
        packed_ref[:, LANES * t : LANES * (t + 1)] = jnp.where(q <= t, one, two)
        spare = two if t == 0 else jnp.where(q == t, two, spare)
    packed_ref[:, LANES * NB :] = spare


def kernel(
    spec_ref, leg_ref, fixed_ref, own_ref, lengths_ref, weights_ref, gains_ref,
    order_ref, mixing_ref, out_ref,
    legs, base_ref, pick_ref, turn_ref, spec, rows, orders, mix_ref, column_orders,
    gathered, coeff, packed, wide, turn, sent, arrived, table, turned, waves, grid, update,
    tr, ti, sent_back, arrived_back, opposite, part_right, part_left, part_own, to_right, to_left,
    first_left, first_right, second_left, second_right, results,
    leg_sem, spec_sem, const_sem, out_sem, ag_send, ag_recv, a_send, a_recv, b_send, b_recv,
    rs_send, rs_recv,
):
    w = lax.axis_index("wave")
    g = lax.axis_index("fld")
    right, left, across = lax.rem(g + 1, FLD), lax.rem(g + 3, FLD), lax.rem(g + 2, FLD)

    def spec_copy(k):
        return pltpu.make_async_copy(
            spec_ref.at[:, pl.ds(k * GROUP, GROUP)], spec.at[k], spec_sem.at[k]
        )

    def out_copy(k):
        return pltpu.make_async_copy(
            results.at[k], out_ref.at[:, pl.ds(k * GROUP, GROUP)], out_sem.at[k]
        )

    fixed_copy = pltpu.make_async_copy(fixed_ref, grid, const_sem)

    def leg_copy(k):
        rows = pl.ds(k * GROUP, GROUP)
        return pltpu.make_async_copy(leg_ref.at[rows], legs.at[rows], leg_sem.at[k])

    def remote(src, dst, send, recv, to):
        return pltpu.make_async_remote_copy(
            src_ref=src, dst_ref=dst, send_sem=send, recv_sem=recv, device_id=to, device_id_type=MESH
        )

    to_r, to_l = (w, right), (w, left)
    head, rest = pl.ds(0, LEFT_PART), pl.ds(LEFT_PART, PACKED - LEFT_PART)

    def own_right(k):
        block = gathered.at[k, g]
        return remote(block, block, ag_send.at[0, k], ag_recv.at[0, k], to_r)

    def own_left(k):
        block = gathered.at[k, g]
        return remote(block, block, ag_send.at[1, k], ag_recv.at[1, k], to_l)

    def pass_right(k):
        block = gathered.at[k, left, :, head]
        return remote(block, block, ag_send.at[2, k], ag_recv.at[2, k], to_r)

    def pass_left(k):
        block = gathered.at[k, right, :, rest]
        return remote(block, block, ag_send.at[3, k], ag_recv.at[3, k], to_l)

    def sum_first_right(k):
        return remote(
            opposite.at[k, :, head], first_left.at[k], rs_send.at[0, k], rs_recv.at[0, k], to_r
        )

    def sum_first_left(k):
        return remote(
            opposite.at[k, :, rest], first_right.at[k], rs_send.at[1, k], rs_recv.at[1, k], to_l
        )

    def sum_second_right(k):
        return remote(to_right.at[k], second_left.at[k], rs_send.at[2, k], rs_recv.at[2, k], to_r)

    def sum_second_left(k):
        return remote(to_left.at[k], second_right.at[k], rs_send.at[3, k], rs_recv.at[3, k], to_l)

    def exchange_all(k, count, src, dst, send, recv):
        some, others = pl.ds(k, count), pl.ds(0, WAVE - 1)
        return remote(src.at[some, others], dst.at[some, others], send.at[k], recv.at[k], (w, g))

    z, x, core = w // 8, lax.rem(w // 2, 4), lax.rem(w, 2)

    def exchange(k, count, src, dst, send, recv):
        some = pl.ds(k, count)
        for dz, dx, dc in OTHERS:
            to = lax.rem(z + dz, 4) * 8 + lax.rem(x + dx, 4) * 2 + lax.rem(core + dc, 2)
            remote(src.at[some, to], dst.at[some, w], send.at[k], recv.at[k], (to, g)).start()
        for n in range(count):
            dst[k + n, w] = src[k + n, w]

    for k in range(CHUNKS):
        spec_copy(k).start()
    fixed_copy.start()
    for k in range(CHUNKS):
        leg_copy(k).start()
    barrier = pltpu.get_barrier_semaphore()

    def greet(d, carry):
        pl.semaphore_signal(
            barrier, inc=1, device_id=(lax.rem(w + d, WAVE), g), device_id_type=MESH
        )
        return carry

    for to in (to_r, to_l):
        pl.semaphore_signal(barrier, inc=1, device_id=to, device_id_type=MESH)
    lax.fori_loop(1, WAVE, greet, 0)

    lane = lax.broadcasted_iota(I32, (ROWS, LANES), 1)
    pair_of_row = lax.broadcasted_iota(I32, (ROWS, LANES), 0) & (PAIRS - 1)

    def pack(k):
        first_row = (w * CHUNKS + k) * GROUP
        m = jnp.full((ROWS, LANES), own_ref[first_row], I32)
        for i in range(1, PAIRS):
            m = jnp.where(pair_of_row == i, own_ref[first_row + 2 * i], m)
        orders[k] = m
        q = m >> 7
        spec_copy(k).wait()
        for f in range(FD):
            for r in range(GROUP):
                values = spec[k, f, r].astype(F32)
                at = 2 * (f * GROUP + r)
                for t in range(NB):
                    rows[t, at : at + 2, :] = values[:, LANES * t : LANES * (t + 1)]
        first, second = [], []
        for t in range(NB):
            n = lane + LANES * t
            half = [
                jnp.concatenate(
                    [rows[t, pl.ds(2 * ab + c, FD * PAIRS, stride=4), :] for c in range(2)], axis=0
                )
                for ab in range(2)
            ]
            first.append(jnp.where(n >= m, half[0], 0.0))
            second.append(jnp.where(n >= M - 1 - m, half[1], 0.0))
        spare = second[NB - 1]
        for t in range(NB):
            other = second[NB - 1 - t]
            gathered[k, g, :, LANES * t : LANES * (t + 1)] = jnp.where(
                t >= q, first[t], other
            ).astype(BF16)
            spare = jnp.where(q == t, other, spare)
        gathered[k, g, :, LANES * NB :] = spare.astype(BF16)

    def first_pack(k, carry):
        pack(k)

        @pl.when(k == 0)
        def _():
            pl.semaphore_wait(barrier, WAVE + 1)
            own_right(0).start()
            own_left(0).start()

        return carry

    lax.fori_loop(0, 2, first_pack, 0)

    spot = lax.broadcasted_iota(I32, (1, LANES), 1)
    lat_of = lambda x: sum((x >= FL * n).astype(I32) for n in range(1, LATS))
    level_of = lambda x: x - FL * lat_of(x)
    length, weight = jnp.zeros((1, LANES), I32), jnp.zeros((1, LANES), F32)
    for lat in range(LATS):
        at = (g * LATS + lat) * WAVE + w
        length = jnp.where(spot >= FL * lat, lengths_ref[at], length)
        weight = jnp.where(spot >= FL * lat, weights_ref[at], weight)
    gain = jnp.zeros((1, LANES), F32)
    for f in range(FL):
        gain = jnp.where(level_of(spot) == f, gains_ref[f], gain)
    gain = jnp.concatenate([gain, gain], axis=1)
    real_length = length.astype(F32)
    root = lax.rsqrt(real_length)
    scale = weight * (root * (1.5 - 0.5 * real_length * root * root))
    half_length = length >> 1
    inverse_length = 1.0 / real_length
    count = length >> 9

    spot = lax.broadcasted_iota(I32, (FL, LANES), 1)
    level = lax.broadcasted_iota(I32, (FL, LANES), 0)
    hot = ((level_of(spot) == level) & (spot < LATS * FL)).astype(F32)
    across_levels = (((0,), (0,)), ((), ()))
    spread = lax.dot_general(
        mixing_ref[...], hot, across_levels, precision=lax.Precision.HIGHEST,
        preferred_element_type=F32,
    )
    spread = lax.dot_general(
        hot, spread, across_levels, precision=lax.Precision.HIGHEST, preferred_element_type=F32
    )
    lats = [lat_of(lax.broadcasted_iota(I32, (LANES, LANES), dim)) for dim in range(2)]
    spread = jnp.where(lats[0] == lats[1], spread, 0.0)
    high_part = spread.astype(BF16)
    mix_ref[:LANES] = high_part
    mix_ref[LANES:] = (spread - high_part.astype(F32)).astype(BF16)

    width = WAVE * GROUP

    def tables(k):
        spot = lax.broadcasted_iota(I32, (width, LANES), 1)
        row = lax.broadcasted_iota(I32, (width, LANES), 0)
        row = (row >> 3) * (CHUNKS * GROUP) + k * GROUP + (row & 7)
        m = jnp.broadcast_to(order_ref[0:1, :], (width, LANES))
        for n in range(1, NB):
            m = jnp.where((row >> 7) == n, order_ref[n : n + 1, :], m)
        m = jnp.where(spot == (row & 127), m, 0).astype(F32)
        m = jnp.broadcast_to(jnp.sum(m, axis=1, keepdims=True), (width, LANES))
        across_lanes = m.T[0:1, :].astype(I32)
        m = m.astype(I32)
        column_orders[k] = m
        t = jnp.where(m < half_length, m.astype(F32) * inverse_length, 0.0)
        tr[k], ti[k] = turn_pair(t)

        spot = lax.broadcasted_iota(I32, (width, BLOCK), 1)
        m = jnp.concatenate([m & (BLOCK - 1)] * (BLOCK // LANES), axis=1)
        hot = (spot == m).astype(F32).astype(BF16)
        lines = jnp.dot(hot, base_ref[...], preferred_element_type=F32).astype(BF16)
        table[k, :width] = lines[:, :BLOCK]
        table[k, width:] = lines[:, BLOCK:]
        spot = lax.broadcasted_iota(I32, (BLOCK, width), 0)
        hot = (spot == (across_lanes & (BLOCK - 1))).astype(F32).astype(BF16)
        for half in range(2):
            turned[k, :, half * width : (half + 1) * width] = jnp.dot(
                base_ref[:, half * BLOCK : (half + 1) * BLOCK], hot, preferred_element_type=F32
            ).astype(BF16)

    fixed_copy.wait()
    side = 2 * LANES
    for n in range(4):
        base_ref[:, side * n : side * (n + 1)] = grid[n].astype(BF16)
    for n in range(2):
        pick_ref[:, side * n : side * (n + 1)] = grid[4 + n].astype(BF16)
        turn_ref[side * n : side * (n + 1), :] = grid[4 + n].T.astype(BF16)
    for s in range(XMAX // 2):
        grid[s] = jnp.zeros((BLOCK, side), F32)

    def legendre_sum(k):
        for t in range(PB):
            for d in range(FLD):
                coeff[t, ROWS * d : ROWS * (d + 1)] = gathered[
                    k, d, :, LANES * t : LANES * (t + 1)
                ].astype(F32)
        for i in range(PAIRS):
            q = orders[k, i : i + 1, :] >> 7
            load_packed(legs, packed, GROUP * k + 2 * i, q)
            weights = []
            for t in range(PB):
                block = coeff[t, pl.ds(i, ROWS, stride=PAIRS), :]
                lead = jnp.where(q <= t, block, 0.0) if t < NB else jnp.zeros_like(block)
                weights.append(
                    jnp.concatenate([lead, block - lead, jnp.zeros((32, LANES), F32)], axis=0).astype(BF16)
                )
            fourier = lax.dot_general(
                packed[...],
                jnp.concatenate(weights, axis=1),
                (((1,), (1,)), ((), ())),
                preferred_element_type=F32,
            ).astype(BF16)
            for lat in range(LATS):
                wide[WAVE * i : WAVE * (i + 1), LANES * lat : LANES * (lat + 1)] = fourier[
                    WAVE * lat : WAVE * (lat + 1)
                ]
        placed = jnp.dot(wide[...], turn_ref[...], preferred_element_type=F32)
        for c in range(2):
            for ab in range(2):
                for i in range(PAIRS):
                    at = 2 * c + ab
                    turn[pl.ds(c * 8 + 2 * i + ab, WAVE, stride=16), :] = placed[
                        WAVE * i : WAVE * (i + 1), LANES * at : LANES * (at + 1)
                    ]
        sent[k] = turn[...].reshape(WAVE, 16, LANES).astype(BF16)

    def grid_sum(k, last):
        keep = column_orders[k] < half_length
        one = tr[k], ti[k]
        two = times(one, one)
        four = times(two, two)
        eight = times(four, four)
        eleven = times(times(eight, two), one)
        x = arrived[k].astype(F32)
        x = jnp.concatenate(
            [x[:, :8].reshape(width, LANES), x[:, 8:].reshape(width, LANES)], axis=0
        ).astype(BF16)
        x = jnp.dot(
            jnp.concatenate([x, x], axis=1), mix_ref[...], preferred_element_type=F32
        )
        x0 = jnp.where(keep, x[:width], 0.0)
        x1 = jnp.where(keep, x[width:], 0.0)
        h = times((x0, x1), eleven)
        for s in range(XMAX // 2):
            for side in range(2):
                span = slice(LANES * side, LANES * (side + 1))
                waves[s, :width, span] = h[0].astype(BF16)
                waves[s, width:, span] = h[1].astype(BF16)
                h = back(h, one)
        for s in range(XMAX // 2):
            part = grid[s] + jnp.dot(turned[k], waves[s], preferred_element_type=F32)
            if not last:
                grid[s] = part
                continue
            high = XMAX - 1 - 2 * s
            live = jnp.concatenate(
                [(high < count).astype(F32), (high - 1 < count).astype(F32)], axis=1
            )
            mixed = part * float(M) ** (-0.5)
            update[s] = ((mixed + gain * mixed * mixed) * live).astype(BF16)

    own_right(1).start()
    own_left(1).start()
    pack(2)
    tables(0)

    def some_tables(k, carry):
        tables(k)
        return carry

    def gather_step(k, carry):
        @pl.when(k < CHUNKS)
        def _():
            own_right(k).wait_recv()
            pass_right(k).start()
            own_left(k).wait_recv()
            pass_left(k).start()

        @pl.when(k + 3 < CHUNKS)
        def _():
            pack(k + 3)
            lax.fori_loop(2 * k + 1, 2 * k + 3, some_tables, 0)

        @pl.when(k + 2 < CHUNKS)
        def _():
            own_right(k + 2).start()
            own_left(k + 2).start()

        @pl.when((k >= 1) & (k <= CHUNKS))
        def _():
            pass_right(k - 1).wait_recv()
            pass_left(k - 1).wait_recv()
            leg_copy(k - 1).wait()
            legendre_sum(k - 1)

        @pl.when(k == 2)
        def _():
            exchange(0, 2, sent, arrived, a_send, a_recv)

        @pl.when(k >= 3)
        def _():
            exchange(k - 1, 1, sent, arrived, a_send, a_recv)

        @pl.when(k == 3)
        def _():
            exchange_all(0, 2, sent, arrived, a_send, a_recv).wait_recv()

        @pl.when(k == 4)
        def _():
            grid_sum(0, False)

        return carry

    lax.fori_loop(0, CHUNKS + 1, gather_step, 0)

    def late_sum(k, carry):
        @pl.when(k >= 2)
        def _():
            exchange_all(k, 1, sent, arrived, a_send, a_recv).wait_recv()

        grid_sum(k, False)
        return carry

    lax.fori_loop(1, CHUNKS - 1, late_sum, 0)
    exchange_all(CHUNKS - 1, 1, sent, arrived, a_send, a_recv).wait_recv()
    grid_sum(CHUNKS - 1, True)

    def grid_back(k):
        t = tr[k], ti[k]
        d = jnp.zeros((width, LANES), F32), jnp.zeros((width, LANES), F32)
        for s in range(XMAX // 2):
            v = jnp.dot(table[k], update[s], preferred_element_type=F32)
            for side in range(2):
                span = slice(LANES * side, LANES * (side + 1))
                if s + side > 0:
                    d = back(d, t)
                d = d[0] + v[:width, span], d[1] + v[width:, span]
        keep = column_orders[k] < half_length
        d0 = jnp.where(keep, d[0] * scale, 0.0).reshape(WAVE, 8, LANES)
        d1 = jnp.where(keep, d[1] * scale, 0.0).reshape(WAVE, 8, LANES)
        sent_back[k] = jnp.concatenate([d0, d1], axis=1).astype(BF16)

    def legendre_back(k):
        turn[...] = arrived_back[k].reshape(WAVE * 16, LANES).astype(F32)
        for c in range(2):
            for ab in range(2):
                for i in range(PAIRS):
                    at = 2 * c + ab
                    wide[WAVE * i : WAVE * (i + 1), LANES * at : LANES * (at + 1)] = turn[
                        pl.ds(c * 8 + 2 * i + ab, WAVE, stride=16), :
                    ].astype(BF16)
        spread = jnp.dot(wide[...], pick_ref[...], preferred_element_type=F32)
        for i in range(PAIRS):
            q = orders[k, i : i + 1, :] >> 7
            load_packed(legs, packed, GROUP * k + 2 * i, q)
            values = jnp.concatenate(
                [
                    spread[WAVE * i : WAVE * (i + 1), LANES * lat : LANES * (lat + 1)]
                    for lat in range(LATS)
                ],
                axis=0,
            )
            values = values.T.astype(BF16)
            result = jnp.dot(values[: 2 * ROWS], packed[...], preferred_element_type=F32)
            for t in range(PB):
                span = slice(LANES * t, LANES * (t + 1))
                if t < NB:
                    block = jnp.where(q <= t, result[:ROWS, span], result[ROWS:, span])
                else:
                    block = result[ROWS:, span]
                coeff[t, pl.ds(i, ROWS, stride=PAIRS), :] = block
        for t in range(PB):
            span = slice(LANES * t, LANES * (t + 1))
            part = lambda d: coeff[t, pl.ds(pl.multiple_of(d * ROWS, 16), ROWS), :]
            opposite[k, :, span] = part(across).astype(BF16)
            part_right[k, :, span] = part(right)
            part_left[k, :, span] = part(left)
            part_own[k, :, span] = part(g)

    def sum_second(k):
        cut = LEFT_PART
        to_right[k, :, :cut] = (part_right[k, :, :cut] + first_left[k].astype(F32)).astype(BF16)
        to_right[k, :, cut:] = part_right[k, :, cut:].astype(BF16)
        to_left[k, :, :cut] = part_left[k, :, :cut].astype(BF16)
        to_left[k, :, cut:] = (part_left[k, :, cut:] + first_right[k].astype(F32)).astype(BF16)

    def unpack(k):
        m = orders[k]
        q = m >> 7
        total = []
        for t in range(PB):
            span = slice(LANES * t, LANES * (t + 1))
            total.append(
                part_own[k, :, span]
                + second_left[k, :, span].astype(F32)
                + second_right[k, :, span].astype(F32)
            )
        for t in range(NB):
            n = lane + LANES * t
            other = jnp.where(NB - 1 - t == q, total[NB], total[NB - 1 - t])
            both = jnp.where(n >= m, total[t], 0.0), jnp.where(n >= M - 1 - m, other, 0.0)
            count = FD * PAIRS
            for ab in range(2):
                for c in range(2):
                    rows[t, pl.ds(2 * ab + c, count, stride=4), :] = both[ab][count * c : count * (c + 1)]
        for f in range(FD):
            for r in range(GROUP):
                at = 2 * (f * GROUP + r)
                results[k, f, r] = jnp.concatenate(
                    [rows[t, at : at + 2, :] for t in range(NB)], axis=1
                )

    def back_step(k):
        grid_back(k)
        exchange(k, 1, sent_back, arrived_back, b_send, b_recv)

    def ahead(k, carry):
        back_step(k)
        return carry

    lax.fori_loop(0, 3, ahead, 0)

    def scatter_step(k, carry):
        @pl.when(k < CHUNKS)
        def _():
            exchange_all(k, 1, sent_back, arrived_back, b_send, b_recv).wait_recv()
            legendre_back(k)
            sum_first_right(k).start()
            sum_first_left(k).start()

        @pl.when((k >= 1) & (k <= CHUNKS))
        def _():
            sum_first_right(k - 1).wait_recv()
            sum_first_left(k - 1).wait_recv()
            sum_second(k - 1)
            sum_second_right(k - 1).start()
            sum_second_left(k - 1).start()

        @pl.when((k >= 1) & (k + 2 < CHUNKS))
        def _():
            back_step(k + 2)

        @pl.when(k >= 4)
        def _():
            sum_second_right(k - 4).wait_recv()
            sum_second_left(k - 4).wait_recv()
            unpack(k - 4)
            out_copy(k - 4).start()

        return carry

    lax.fori_loop(0, CHUNKS + 4, scatter_step, 0)

    def finish(k, carry):
        for copy in (own_right, own_left, pass_right, pass_left):
            copy(k).wait_send()
        for copy in (sum_first_right, sum_first_left, sum_second_right, sum_second_left):
            copy(k).wait_send()
        exchange_all(k, 1, sent_back, arrived_back, b_send, b_recv).wait_send()
        out_copy(k).wait()
        return carry

    lax.fori_loop(0, CHUNKS, finish, 0)
    for k, count in ((0, 2), (2, 1), (3, 1), (4, 1)):
        exchange_all(k, count, sent, arrived, a_send, a_recv).wait_send()


PIECES = 5


def hand_over(src_ref, dst_ref, held, sem_in, sem_out):
    count = src_ref.shape[1] // PIECES
    spans = [pl.ds(n * count, count) for n in range(PIECES)]
    reads = [
        pltpu.make_async_copy(src_ref.at[:, at], held.at[:, at], sem_in.at[n])
        for n, at in enumerate(spans)
    ]
    writes = [
        pltpu.make_async_copy(held.at[:, at], dst_ref.at[:, at], sem_out.at[n])
        for n, at in enumerate(spans)
    ]
    for read in reads:
        read.start()
    for read, write in zip(reads, writes):
        read.wait()
        write.start()
    for write in writes:
        write.wait()


VMEM = pl.BlockSpec(memory_space=pltpu.VMEM)
SMEM = pl.BlockSpec(memory_space=pltpu.SMEM)
ANY = pl.BlockSpec(memory_space=pl.ANY)


def local(spec_in, legendre, wave_order, row_length, quad_weight, mixing, square_gain):
    fixed = np.concatenate([wave_tables(), lane_maps()], axis=1)
    fixed = fixed.reshape(BLOCK, XMAX // 2, 2 * LANES).transpose(1, 0, 2)
    width = WAVE * GROUP
    message = pltpu.VMEM((CHUNKS, WAVE, 16, LANES), BF16)
    full = pltpu.VMEM((CHUNKS, ROWS, PACKED), F32)
    short = pltpu.VMEM((CHUNKS, ROWS, PACKED), BF16)
    turns = pltpu.VMEM((CHUNKS, width, LANES), F32)
    places = pltpu.VMEM((LATS * LANES, LATS * LANES), BF16)
    copies = pltpu.SemaphoreType.DMA((4, CHUNKS))
    each = pltpu.SemaphoreType.DMA((CHUNKS,))
    result = pl.pallas_call(
        kernel,
        out_shape=jax.ShapeDtypeStruct((FD, GROUP * CHUNKS, 2, M), F32),
        in_specs=[ANY] * 3 + [SMEM] * 4 + [VMEM] * 2,
        out_specs=ANY,
        scratch_shapes=[
            pltpu.VMEM((GROUP * CHUNKS, FLD * WAVE, M), BF16),
            pltpu.VMEM((BLOCK, 2 * BLOCK), BF16),
            places,
            places,
            pltpu.VMEM((CHUNKS, FD, GROUP, 2, M), BF16),
            pltpu.VMEM((NB, 2 * ROWS, LANES), F32),
            pltpu.VMEM((CHUNKS, ROWS, LANES), I32),
            pltpu.VMEM((2 * LANES, LANES), BF16),
            pltpu.VMEM((CHUNKS, width, LANES), I32),
            pltpu.VMEM((CHUNKS, FLD, ROWS, PACKED), BF16),
            pltpu.VMEM((PB, FLD * ROWS, LANES), F32),
            pltpu.VMEM((LANES, PACKED), BF16),
            pltpu.VMEM((PAIRS * WAVE, LATS * LANES), BF16),
            pltpu.VMEM((WAVE * 16, LANES), F32),
            message,
            message,
            pltpu.VMEM((CHUNKS, 2 * width, BLOCK), BF16),
            pltpu.VMEM((CHUNKS, BLOCK, 2 * width), BF16),
            pltpu.VMEM((XMAX // 2, 2 * width, 2 * LANES), BF16),
            pltpu.VMEM((XMAX // 2, BLOCK, 2 * LANES), F32),
            pltpu.VMEM((XMAX // 2, BLOCK, 2 * LANES), BF16),
            turns,
            turns,
            message,
            message,
            short,
            full,
            full,
            full,
            short,
            short,
            pltpu.VMEM((CHUNKS, ROWS, LEFT_PART), BF16),
            pltpu.VMEM((CHUNKS, ROWS, PACKED - LEFT_PART), BF16),
            short,
            short,
            pltpu.VMEM((CHUNKS, FD, GROUP, 2, M), F32),
            each,
            each,
            pltpu.SemaphoreType.DMA,
            each,
            copies,
            copies,
            each,
            each,
            each,
            each,
            copies,
            copies,
        ],
        compiler_params=pltpu.CompilerParams(
            collective_id=0, has_side_effects=True, vmem_limit_bytes=60 << 20
        ),
    )(
        spec_in, legendre, jnp.asarray(fixed),
        wave_order, row_length, quad_weight, square_gain,
        wave_order.reshape(NB, LANES), mixing,
    )
    return pl.pallas_call(
        hand_over,
        out_shape=jax.ShapeDtypeStruct(result.shape, F32),
        in_specs=[ANY],
        out_specs=ANY,
        scratch_shapes=[
            pltpu.VMEM(result.shape, F32),
            pltpu.SemaphoreType.DMA((PIECES,)),
            pltpu.SemaphoreType.DMA((PIECES,)),
        ],
        compiler_params=pltpu.CompilerParams(vmem_limit_bytes=60 << 20),
    )(result)

def solution(mesh):
    in_specs = (P("fld", "wave", None, None), P("wave", "fld", None), P(), P(), P(), P(), P())
    out_specs = P("fld", "wave", None, None)
    return jax.shard_map(local, mesh=mesh, in_specs=in_specs, out_specs=out_specs, check_vma=False)
```

```python
import functools
import math

import jax
import jax.numpy as jnp
import numpy as np
from jax import lax
from jax.experimental import pallas as pl
from jax.experimental.pallas import tpu as pltpu
from jax.sharding import PartitionSpec as P

M = 1280
FL = 24
BLOCK = 512
LANES = 128
NB = M // LANES
PB = NB + 1
PACKED = PB * LANES
CHUNKS = 5
PAIRS = 4
WAVE = 32
FLD = 4
LATS = 4
FD = FL // FLD
ROWS = 2 * FD * PAIRS
XMAX = 12
F32, BF16, I32 = jnp.float32, jnp.bfloat16, jnp.int32


def wave_tables():
    v = np.arange(BLOCK)
    angle = (v[:, None] * v[None, :] % BLOCK) * (2.0 * math.pi / BLOCK)
    return np.concatenate([np.cos(angle), -np.sin(angle)], axis=1).astype(np.float32)


def lane_maps():
    width = LATS * LANES
    lat_a, ab_a, level_a, half_a = (np.full(width, -1) for _ in range(4))
    for lat in range(LATS):
        for ab in range(2):
            for g in range(FLD):
                for c in range(2):
                    for f in range(FD):
                        at = LANES * lat + ((ab * FLD + g) * 2 + c) * FD + f
                        lat_a[at], ab_a[at], half_a[at], level_a[at] = lat, ab, c, FD * g + f
    lat_b, ab_b, level_b, half_b = (np.full(width, -2) for _ in range(4))
    for c in range(2):
        for ab in range(2):
            for lat in range(LATS):
                for f in range(FL):
                    at = LANES * (2 * c + ab) + FL * lat + f
                    lat_b[at], ab_b[at], half_b[at], level_b[at] = lat, ab, c, f
    same = (
        (lat_a[:, None] == lat_b[None, :])
        & (ab_a[:, None] == ab_b[None, :])
        & (half_a[:, None] == half_b[None, :])
    )
    pick = same & (level_a[:, None] == level_b[None, :])
    return pick.T.astype(np.float32)


def turn_pair(t):
    a = (t - 0.25) * (2.0 * math.pi)
    s = a * a
    sine = a * (
        1.0
        + s
        * (
            -1.0 / 6
            + s * (1.0 / 120 + s * (-1.0 / 5040 + s * (1.0 / 362880 - s * (1.0 / 39916800))))
        )
    )
    cosine = 1.0 + s * (
        -0.5
        + s
        * (
            1.0 / 24
            + s * (-1.0 / 720 + s * (1.0 / 40320 + s * (-1.0 / 3628800 + s * (1.0 / 479001600))))
        )
    )
    return -sine, cosine


def times(a, b):
    return a[0] * b[0] - a[1] * b[1], a[0] * b[1] + a[1] * b[0]


def back(a, b):
    return a[0] * b[0] + a[1] * b[1], a[1] * b[0] - a[0] * b[1]


SENT = NB * ROWS + 16
LEFT_PART = SENT // 32 * 16
GROUP = 8
MESH = pl.DeviceIdType.MESH
OTHERS = sorted(
    ((dz, dx, dc) for dz in range(4) for dx in range(4) for dc in range(2) if dz + dx + dc > 0),
    key=lambda d: -(min(d[0], 4 - d[0]) + min(d[1], 4 - d[1])),
)


def load_packed(leg_ref, packed_ref, first, q):
    q = jnp.broadcast_to(q.astype(F32), (LANES, LANES)).astype(BF16)
    spare = None
    for t in range(NB):
        one = leg_ref[first, :, LANES * t : LANES * (t + 1)]
        at = NB - 1 - t
        two = leg_ref[first + 1, :, LANES * at : LANES * (at + 1)]
        packed_ref[:, LANES * t : LANES * (t + 1)] = jnp.where(q <= t, one, two)
        spare = two if t == 0 else jnp.where(q == t, two, spare)
    packed_ref[:, LANES * NB :] = spare


def kernel(
    spec_ref, leg_ref, fixed_ref, own_ref, lengths_ref, weights_ref, gains_ref,
    order_ref, mixing_ref, out_ref,
    legs, base_ref, pick_ref, turn_ref, spec, rows, orders, mix_ref, column_orders,
    gathered, coeff, flipped, packed, wide, turn, sent, arrived, table, turned, waves, grid, update,
    tr, ti, sent_back, arrived_back, opposite, part_right, part_left, part_own, to_right, to_left,
    first_left, first_right, second_left, second_right, results,
    leg_sem, spec_sem, const_sem, out_sem, ag_send, ag_recv, a_send, a_recv, b_send, b_recv,
    rs_send, rs_recv,
):
    w = lax.axis_index("wave")
    g = lax.axis_index("fld")
    right, left, across = lax.rem(g + 1, FLD), lax.rem(g + 3, FLD), lax.rem(g + 2, FLD)

    def spec_copy(k):
        return pltpu.make_async_copy(
            spec_ref.at[:, pl.ds(k * GROUP, GROUP)], spec.at[k], spec_sem.at[k]
        )

    def out_copy(k):
        return pltpu.make_async_copy(
            results.at[k], out_ref.at[:, pl.ds(k * GROUP, GROUP)], out_sem.at[k]
        )

    fixed_copy = pltpu.make_async_copy(fixed_ref, grid, const_sem)

    def leg_copy(k):
        rows = pl.ds(k * GROUP, GROUP)
        return pltpu.make_async_copy(leg_ref.at[rows], legs.at[rows], leg_sem.at[k])

    def remote(src, dst, send, recv, to):
        return pltpu.make_async_remote_copy(
            src_ref=src, dst_ref=dst, send_sem=send, recv_sem=recv, device_id=to, device_id_type=MESH
        )

    to_r, to_l = (w, right), (w, left)
    head, rest = pl.ds(0, LEFT_PART), pl.ds(LEFT_PART, SENT - LEFT_PART)

    def own_right(k):
        block = gathered.at[k, g]
        return remote(block, block, ag_send.at[0, k], ag_recv.at[0, k], to_r)

    def own_left(k):
        block = gathered.at[k, g]
        return remote(block, block, ag_send.at[1, k], ag_recv.at[1, k], to_l)

    def pass_right(k):
        block = gathered.at[k, left, head]
        return remote(block, block, ag_send.at[2, k], ag_recv.at[2, k], to_r)

    def pass_left(k):
        block = gathered.at[k, right, rest]
        return remote(block, block, ag_send.at[3, k], ag_recv.at[3, k], to_l)

    def sum_first_right(k):
        return remote(
            opposite.at[k, head], first_left.at[k], rs_send.at[0, k], rs_recv.at[0, k], to_r
        )

    def sum_first_left(k):
        return remote(
            opposite.at[k, rest], first_right.at[k], rs_send.at[1, k], rs_recv.at[1, k], to_l
        )

    def sum_second_right(k):
        return remote(to_right.at[k], second_left.at[k], rs_send.at[2, k], rs_recv.at[2, k], to_r)

    def sum_second_left(k):
        return remote(to_left.at[k], second_right.at[k], rs_send.at[3, k], rs_recv.at[3, k], to_l)

    def exchange_all(k, count, src, dst, send, recv):
        some, others = pl.ds(k, count), pl.ds(0, WAVE - 1)
        return remote(src.at[some, others], dst.at[some, others], send.at[k], recv.at[k], (w, g))

    z, x, core = w // 8, lax.rem(w // 2, 4), lax.rem(w, 2)

    def exchange(k, count, src, dst, send, recv):
        some = pl.ds(k, count)
        for dz, dx, dc in OTHERS:
            to = lax.rem(z + dz, 4) * 8 + lax.rem(x + dx, 4) * 2 + lax.rem(core + dc, 2)
            remote(src.at[some, to], dst.at[some, w], send.at[k], recv.at[k], (to, g)).start()
        for n in range(count):
            dst[k + n, w] = src[k + n, w]

    for k in range(CHUNKS):
        spec_copy(k).start()
    fixed_copy.start()
    for k in range(CHUNKS):
        leg_copy(k).start()
    barrier = pltpu.get_barrier_semaphore()

    def greet(d, carry):
        pl.semaphore_signal(
            barrier, inc=1, device_id=(lax.rem(w + d, WAVE), g), device_id_type=MESH
        )
        return carry

    for to in (to_r, to_l):
        pl.semaphore_signal(barrier, inc=1, device_id=to, device_id_type=MESH)
    lax.fori_loop(1, WAVE, greet, 0)

    lane = lax.broadcasted_iota(I32, (ROWS, LANES), 1)
    pair_of_row = lax.broadcasted_iota(I32, (ROWS, LANES), 0) & (PAIRS - 1)

    def reverse(values):
        places = [lax.broadcasted_iota(I32, (LANES, LANES), dim) for dim in range(2)]
        flip = (places[0] + places[1] == LANES - 1).astype(F32)
        if values.dtype == BF16:
            return jnp.dot(values, flip.astype(BF16), preferred_element_type=F32)
        return jnp.dot(
            values, flip, precision=lax.Precision.HIGHEST, preferred_element_type=F32
        )

    def fold(spare, s):
        value = jnp.sum(jnp.where(lane == LANES - 1 - s, spare, 0.0), axis=1, keepdims=True)
        value = jnp.broadcast_to(value, (ROWS, LANES))
        spot = lane[:16]
        out = jnp.zeros((16, LANES), F32)
        for n in range(ROWS // 16):
            out = jnp.where(spot == n, value[16 * n : 16 * (n + 1)], out)
        return out

    def unfold(extras):
        spot = lane[:16]
        return jnp.concatenate(
            [
                jnp.broadcast_to(
                    jnp.sum(jnp.where(spot == n, extras, 0.0), axis=1, keepdims=True), (16, LANES)
                )
                for n in range(ROWS // 16)
            ],
            axis=0,
        )

    def recover(blocks, extras, m, kind):
        q, s = m >> 7, m & (LANES - 1)
        shared = blocks[0]
        for t in range(1, NB):
            shared = jnp.where(q == t, blocks[t], shared)
        back_again = reverse(shared.astype(kind))
        spot = LANES - 1 - s
        return jnp.where(lane > spot, back_again, jnp.where(lane == spot, unfold(extras), 0.0))

    def pack(k):
        first_row = (w * CHUNKS + k) * GROUP
        m = jnp.full((ROWS, LANES), own_ref[first_row], I32)
        for i in range(1, PAIRS):
            m = jnp.where(pair_of_row == i, own_ref[first_row + 2 * i], m)
        orders[k] = m
        q = m >> 7
        spec_copy(k).wait()
        for f in range(FD):
            for r in range(GROUP):
                values = spec[k, f, r].astype(F32)
                at = 2 * (f * GROUP + r)
                for t in range(NB):
                    rows[t, at : at + 2, :] = values[:, LANES * t : LANES * (t + 1)]
        first, second = [], []
        for t in range(NB):
            n = lane + LANES * t
            half = [
                jnp.concatenate(
                    [rows[t, pl.ds(2 * ab + c, FD * PAIRS, stride=4), :] for c in range(2)], axis=0
                )
                for ab in range(2)
            ]
            first.append(jnp.where(n >= m, half[0], 0.0))
            second.append(jnp.where(n >= M - 1 - m, half[1], 0.0))
        s = m & (LANES - 1)
        spare = second[NB - 1]
        for t in range(1, NB):
            spare = jnp.where(q == t, second[NB - 1 - t], spare)
        turned_round = reverse(spare.astype(BF16))
        for t in range(NB):
            shared = jnp.where(lane >= s, first[t], turned_round)
            block = jnp.where(q < t, first[t], jnp.where(q == t, shared, second[NB - 1 - t]))
            gathered[k, g, ROWS * t : ROWS * (t + 1), :] = block.astype(BF16)
        gathered[k, g, NB * ROWS :, :] = fold(spare, s).astype(BF16)

    def first_pack(k, carry):
        pack(k)

        @pl.when(k == 0)
        def _():
            pl.semaphore_wait(barrier, WAVE + 1)
            own_right(0).start()
            own_left(0).start()

        return carry

    lax.fori_loop(0, 2, first_pack, 0)

    spot = lax.broadcasted_iota(I32, (1, LANES), 1)
    lat_of = lambda x: sum((x >= FL * n).astype(I32) for n in range(1, LATS))
    level_of = lambda x: x - FL * lat_of(x)
    length, weight = jnp.zeros((1, LANES), I32), jnp.zeros((1, LANES), F32)
    for lat in range(LATS):
        at = (g * LATS + lat) * WAVE + w
        length = jnp.where(spot >= FL * lat, lengths_ref[at], length)
        weight = jnp.where(spot >= FL * lat, weights_ref[at], weight)
    gain = jnp.zeros((1, LANES), F32)
    for f in range(FL):
        gain = jnp.where(level_of(spot) == f, gains_ref[f], gain)
    gain = jnp.concatenate([gain, gain], axis=1)
    real_length = length.astype(F32)
    root = lax.rsqrt(real_length)
    scale = weight * (root * (1.5 - 0.5 * real_length * root * root))
    half_length = length >> 1
    inverse_length = 1.0 / real_length
    count = length >> 9

    spot = lax.broadcasted_iota(I32, (FL, LANES), 1)
    level = lax.broadcasted_iota(I32, (FL, LANES), 0)
    hot = ((level_of(spot) == level) & (spot < LATS * FL)).astype(F32)
    across_levels = (((0,), (0,)), ((), ()))
    spread = lax.dot_general(
        mixing_ref[...], hot, across_levels, precision=lax.Precision.HIGHEST,
        preferred_element_type=F32,
    )
    spread = lax.dot_general(
        hot, spread, across_levels, precision=lax.Precision.HIGHEST, preferred_element_type=F32
    )
    lats = [lat_of(lax.broadcasted_iota(I32, (LANES, LANES), dim)) for dim in range(2)]
    spread = jnp.where(lats[0] == lats[1], spread, 0.0)
    high_part = spread.astype(BF16)
    mix_ref[:LANES] = high_part
    mix_ref[LANES:] = (spread - high_part.astype(F32)).astype(BF16)

    width = WAVE * GROUP

    def tables(k):
        spot = lax.broadcasted_iota(I32, (width, LANES), 1)
        row = lax.broadcasted_iota(I32, (width, LANES), 0)
        row = (row >> 3) * (CHUNKS * GROUP) + k * GROUP + (row & 7)
        m = jnp.broadcast_to(order_ref[0:1, :], (width, LANES))
        for n in range(1, NB):
            m = jnp.where((row >> 7) == n, order_ref[n : n + 1, :], m)
        m = jnp.where(spot == (row & 127), m, 0).astype(F32)
        m = jnp.broadcast_to(jnp.sum(m, axis=1, keepdims=True), (width, LANES))
        across_lanes = m.T[0:1, :].astype(I32)
        m = m.astype(I32)
        column_orders[k] = m
        t = jnp.where(m < half_length, m.astype(F32) * inverse_length, 0.0)
        tr[k], ti[k] = turn_pair(t)

        spot = lax.broadcasted_iota(I32, (width, BLOCK), 1)
        m = jnp.concatenate([m & (BLOCK - 1)] * (BLOCK // LANES), axis=1)
        hot = (spot == m).astype(F32).astype(BF16)
        lines = jnp.dot(hot, base_ref[...], preferred_element_type=F32).astype(BF16)
        table[k, :width] = lines[:, :BLOCK]
        table[k, width:] = lines[:, BLOCK:]
        spot = lax.broadcasted_iota(I32, (BLOCK, width), 0)
        hot = (spot == (across_lanes & (BLOCK - 1))).astype(F32).astype(BF16)
        for half in range(2):
            turned[k, :, half * width : (half + 1) * width] = jnp.dot(
                base_ref[:, half * BLOCK : (half + 1) * BLOCK], hot, preferred_element_type=F32
            ).astype(BF16)

    fixed_copy.wait()
    side = 2 * LANES
    for n in range(4):
        base_ref[:, side * n : side * (n + 1)] = grid[n].astype(BF16)
    for n in range(2):
        pick_ref[:, side * n : side * (n + 1)] = grid[4 + n].astype(BF16)
        turn_ref[side * n : side * (n + 1), :] = grid[4 + n].T.astype(BF16)
    for s in range(XMAX // 2):
        grid[s] = jnp.zeros((BLOCK, side), F32)

    def legendre_sum(k):
        for d in range(FLD):
            group = slice(ROWS * d, ROWS * (d + 1))
            blocks = [gathered[k, d, ROWS * t : ROWS * (t + 1), :] for t in range(NB)]
            for t in range(NB):
                coeff[t, group] = blocks[t].astype(F32)
            extras = gathered[k, d, NB * ROWS :, :].astype(F32)
            coeff[NB, group] = recover([coeff[t, group] for t in range(NB)], extras, orders[k], BF16)
        for i in range(PAIRS):
            m = orders[k, i : i + 1, :]
            q = m >> 7
            load_packed(legs, packed, GROUP * k + 2 * i, q)
            spot = lax.broadcasted_iota(I32, (1, LANES), 1)
            weights = []
            for t in range(PB):
                block = coeff[t, pl.ds(i, ROWS, stride=PAIRS), :]
                if t < NB:
                    lead = jnp.where(spot + LANES * t >= m, block, 0.0)
                    other = jnp.where(q > t, block, 0.0)
                else:
                    lead, other = jnp.zeros_like(block), block
                weights.append(
                    jnp.concatenate([lead, other, jnp.zeros((32, LANES), F32)], axis=0).astype(BF16)
                )
            fourier = lax.dot_general(
                packed[...],
                jnp.concatenate(weights, axis=1),
                (((1,), (1,)), ((), ())),
                preferred_element_type=F32,
            ).astype(BF16)
            for lat in range(LATS):
                wide[WAVE * i : WAVE * (i + 1), LANES * lat : LANES * (lat + 1)] = fourier[
                    WAVE * lat : WAVE * (lat + 1)
                ]
        placed = jnp.dot(wide[...], turn_ref[...], preferred_element_type=F32)
        for c in range(2):
            for ab in range(2):
                for i in range(PAIRS):
                    at = 2 * c + ab
                    turn[pl.ds(c * 8 + 2 * i + ab, WAVE, stride=16), :] = placed[
                        WAVE * i : WAVE * (i + 1), LANES * at : LANES * (at + 1)
                    ]
        sent[k] = turn[...].reshape(WAVE, 16, LANES).astype(BF16)

    def grid_sum(k, last):
        keep = column_orders[k] < half_length
        one = tr[k], ti[k]
        two = times(one, one)
        four = times(two, two)
        eight = times(four, four)
        eleven = times(times(eight, two), one)
        x = arrived[k].astype(F32)
        x = jnp.concatenate(
            [x[:, :8].reshape(width, LANES), x[:, 8:].reshape(width, LANES)], axis=0
        ).astype(BF16)
        x = jnp.dot(
            jnp.concatenate([x, x], axis=1), mix_ref[...], preferred_element_type=F32
        )
        x0 = jnp.where(keep, x[:width], 0.0)
        x1 = jnp.where(keep, x[width:], 0.0)
        h = times((x0, x1), eleven)
        for s in range(XMAX // 2):
            for side in range(2):
                span = slice(LANES * side, LANES * (side + 1))
                waves[s, :width, span] = h[0].astype(BF16)
                waves[s, width:, span] = h[1].astype(BF16)
                h = back(h, one)
        for s in range(XMAX // 2):
            part = grid[s] + jnp.dot(turned[k], waves[s], preferred_element_type=F32)
            if not last:
                grid[s] = part
                continue
            high = XMAX - 1 - 2 * s
            live = jnp.concatenate(
                [(high < count).astype(F32), (high - 1 < count).astype(F32)], axis=1
            )
            mixed = part * float(M) ** (-0.5)
            update[s] = ((mixed + gain * mixed * mixed) * live).astype(BF16)

    own_right(1).start()
    own_left(1).start()
    pack(2)
    tables(0)

    def some_tables(k, carry):
        tables(k)
        return carry

    def gather_step(k, carry):
        @pl.when(k < CHUNKS)
        def _():
            own_right(k).wait_recv()
            pass_right(k).start()
            own_left(k).wait_recv()
            pass_left(k).start()

        @pl.when(k + 3 < CHUNKS)
        def _():
            pack(k + 3)
            lax.fori_loop(2 * k + 1, 2 * k + 3, some_tables, 0)

        @pl.when(k + 2 < CHUNKS)
        def _():
            own_right(k + 2).start()
            own_left(k + 2).start()

        @pl.when((k >= 1) & (k <= CHUNKS))
        def _():
            pass_right(k - 1).wait_recv()
            pass_left(k - 1).wait_recv()
            leg_copy(k - 1).wait()
            legendre_sum(k - 1)

        @pl.when(k == 2)
        def _():
            exchange(0, 2, sent, arrived, a_send, a_recv)

        @pl.when(k >= 3)
        def _():
            exchange(k - 1, 1, sent, arrived, a_send, a_recv)

        @pl.when(k == 3)
        def _():
            exchange_all(0, 2, sent, arrived, a_send, a_recv).wait_recv()

        @pl.when(k == 4)
        def _():
            grid_sum(0, False)

        return carry

    lax.fori_loop(0, CHUNKS + 1, gather_step, 0)

    def late_sum(k, carry):
        @pl.when(k >= 2)
        def _():
            exchange_all(k, 1, sent, arrived, a_send, a_recv).wait_recv()

        grid_sum(k, False)
        return carry

    lax.fori_loop(1, CHUNKS - 1, late_sum, 0)
    exchange_all(CHUNKS - 1, 1, sent, arrived, a_send, a_recv).wait_recv()
    grid_sum(CHUNKS - 1, True)

    def grid_back(k):
        t = tr[k], ti[k]
        d = jnp.zeros((width, LANES), F32), jnp.zeros((width, LANES), F32)
        for s in range(XMAX // 2):
            v = jnp.dot(table[k], update[s], preferred_element_type=F32)
            for side in range(2):
                span = slice(LANES * side, LANES * (side + 1))
                if s + side > 0:
                    d = back(d, t)
                d = d[0] + v[:width, span], d[1] + v[width:, span]
        keep = column_orders[k] < half_length
        d0 = jnp.where(keep, d[0] * scale, 0.0).reshape(WAVE, 8, LANES)
        d1 = jnp.where(keep, d[1] * scale, 0.0).reshape(WAVE, 8, LANES)
        sent_back[k] = jnp.concatenate([d0, d1], axis=1).astype(BF16)

    def legendre_back(k):
        turn[...] = arrived_back[k].reshape(WAVE * 16, LANES).astype(F32)
        for c in range(2):
            for ab in range(2):
                for i in range(PAIRS):
                    at = 2 * c + ab
                    wide[WAVE * i : WAVE * (i + 1), LANES * at : LANES * (at + 1)] = turn[
                        pl.ds(c * 8 + 2 * i + ab, WAVE, stride=16), :
                    ].astype(BF16)
        spread = jnp.dot(wide[...], pick_ref[...], preferred_element_type=F32)
        for i in range(PAIRS):
            q = orders[k, i : i + 1, :] >> 7
            load_packed(legs, packed, GROUP * k + 2 * i, q)
            values = jnp.concatenate(
                [
                    spread[WAVE * i : WAVE * (i + 1), LANES * lat : LANES * (lat + 1)]
                    for lat in range(LATS)
                ],
                axis=0,
            )
            values = values.T.astype(BF16)
            result = jnp.dot(values[: 2 * ROWS], packed[...], preferred_element_type=F32)
            for t in range(PB):
                span = slice(LANES * t, LANES * (t + 1))
                if t < NB:
                    block = jnp.where(q <= t, result[:ROWS, span], result[ROWS:, span])
                else:
                    block = result[ROWS:, span]
                coeff[t, pl.ds(i, ROWS, stride=PAIRS), :] = block
        m = orders[k]
        q, s = m >> 7, m & (LANES - 1)
        flipped[...] = reverse(coeff[NB].astype(BF16))
        own_rows = lambda d: pl.ds(pl.multiple_of(d * ROWS, 16), ROWS)
        places = (
            (opposite, across, BF16), (part_right, right, F32), (part_left, left, F32), (part_own, g, F32)
        )
        for place, d, kind in places:
            for t in range(NB):
                shared = (q == t) & (lane < s)
                block = jnp.where(shared, flipped[own_rows(d), :], coeff[t, own_rows(d), :])
                place[k, ROWS * t : ROWS * (t + 1), :] = block.astype(kind)
            place[k, NB * ROWS :, :] = fold(coeff[NB, own_rows(d), :], s).astype(kind)

    def sum_second(k):
        cut = LEFT_PART
        to_right[k, :cut] = (part_right[k, :cut] + first_left[k].astype(F32)).astype(BF16)
        to_right[k, cut:] = part_right[k, cut:].astype(BF16)
        to_left[k, :cut] = part_left[k, :cut].astype(BF16)
        to_left[k, cut:] = (part_left[k, cut:] + first_right[k].astype(F32)).astype(BF16)

    def unpack(k):
        m = orders[k]
        q = m >> 7
        whole = lambda at: (
            part_own[k, at, :] + second_left[k, at, :].astype(F32) + second_right[k, at, :].astype(F32)
        )
        total = [whole(slice(ROWS * t, ROWS * (t + 1))) for t in range(NB)]
        total.append(recover(total, whole(slice(NB * ROWS, SENT)), m, F32))
        for t in range(NB):
            n = lane + LANES * t
            other = jnp.where(NB - 1 - t == q, total[NB], total[NB - 1 - t])
            both = jnp.where(n >= m, total[t], 0.0), jnp.where(n >= M - 1 - m, other, 0.0)
            count = FD * PAIRS
            for ab in range(2):
                for c in range(2):
                    rows[t, pl.ds(2 * ab + c, count, stride=4), :] = both[ab][count * c : count * (c + 1)]
        for f in range(FD):
            for r in range(GROUP):
                at = 2 * (f * GROUP + r)
                results[k, f, r] = jnp.concatenate(
                    [rows[t, at : at + 2, :] for t in range(NB)], axis=1
                )

    def back_step(k):
        grid_back(k)
        exchange(k, 1, sent_back, arrived_back, b_send, b_recv)

    def ahead(k, carry):
        back_step(k)
        return carry

    lax.fori_loop(0, 3, ahead, 0)

    def scatter_step(k, carry):
        @pl.when(k < CHUNKS)
        def _():
            exchange_all(k, 1, sent_back, arrived_back, b_send, b_recv).wait_recv()
            legendre_back(k)
            sum_first_right(k).start()
            sum_first_left(k).start()

        @pl.when((k >= 1) & (k <= CHUNKS))
        def _():
            sum_first_right(k - 1).wait_recv()
            sum_first_left(k - 1).wait_recv()
            sum_second(k - 1)
            sum_second_right(k - 1).start()
            sum_second_left(k - 1).start()

        @pl.when((k >= 1) & (k + 2 < CHUNKS))
        def _():
            back_step(k + 2)

        @pl.when(k >= 4)
        def _():
            sum_second_right(k - 4).wait_recv()
            sum_second_left(k - 4).wait_recv()
            unpack(k - 4)
            out_copy(k - 4).start()

        return carry

    lax.fori_loop(0, CHUNKS + 4, scatter_step, 0)

    def finish(k, carry):
        for copy in (own_right, own_left, pass_right, pass_left):
            copy(k).wait_send()
        for copy in (sum_first_right, sum_first_left, sum_second_right, sum_second_left):
            copy(k).wait_send()
        exchange_all(k, 1, sent_back, arrived_back, b_send, b_recv).wait_send()
        out_copy(k).wait()
        return carry

    lax.fori_loop(0, CHUNKS, finish, 0)
    for k, count in ((0, 2), (2, 1), (3, 1), (4, 1)):
        exchange_all(k, count, sent, arrived, a_send, a_recv).wait_send()


PIECES = 5


def hand_over(src_ref, dst_ref, held, sem_in, sem_out):
    count = src_ref.shape[1] // PIECES
    spans = [pl.ds(n * count, count) for n in range(PIECES)]
    reads = [
        pltpu.make_async_copy(src_ref.at[:, at], held.at[:, at], sem_in.at[n])
        for n, at in enumerate(spans)
    ]
    writes = [
        pltpu.make_async_copy(held.at[:, at], dst_ref.at[:, at], sem_out.at[n])
        for n, at in enumerate(spans)
    ]
    for read in reads:
        read.start()
    for read, write in zip(reads, writes):
        read.wait()
        write.start()
    for write in writes:
        write.wait()


VMEM = pl.BlockSpec(memory_space=pltpu.VMEM)
SMEM = pl.BlockSpec(memory_space=pltpu.SMEM)
ANY = pl.BlockSpec(memory_space=pl.ANY)


def local(spec_in, legendre, wave_order, row_length, quad_weight, mixing, square_gain):
    fixed = np.concatenate([wave_tables(), lane_maps()], axis=1)
    fixed = fixed.reshape(BLOCK, XMAX // 2, 2 * LANES).transpose(1, 0, 2)
    width = WAVE * GROUP
    message = pltpu.VMEM((CHUNKS, WAVE, 16, LANES), BF16)
    full = pltpu.VMEM((CHUNKS, SENT, LANES), F32)
    short = pltpu.VMEM((CHUNKS, SENT, LANES), BF16)
    turns = pltpu.VMEM((CHUNKS, width, LANES), F32)
    places = pltpu.VMEM((LATS * LANES, LATS * LANES), BF16)
    copies = pltpu.SemaphoreType.DMA((4, CHUNKS))
    each = pltpu.SemaphoreType.DMA((CHUNKS,))
    result = pl.pallas_call(
        kernel,
        out_shape=jax.ShapeDtypeStruct((FD, GROUP * CHUNKS, 2, M), F32),
        in_specs=[ANY] * 3 + [SMEM] * 4 + [VMEM] * 2,
        out_specs=ANY,
        scratch_shapes=[
            pltpu.VMEM((GROUP * CHUNKS, FLD * WAVE, M), BF16),
            pltpu.VMEM((BLOCK, 2 * BLOCK), BF16),
            places,
            places,
            pltpu.VMEM((CHUNKS, FD, GROUP, 2, M), BF16),
            pltpu.VMEM((NB, 2 * ROWS, LANES), F32),
            pltpu.VMEM((CHUNKS, ROWS, LANES), I32),
            pltpu.VMEM((2 * LANES, LANES), BF16),
            pltpu.VMEM((CHUNKS, width, LANES), I32),
            pltpu.VMEM((CHUNKS, FLD, SENT, LANES), BF16),
            pltpu.VMEM((PB, FLD * ROWS, LANES), F32),
            pltpu.VMEM((FLD * ROWS, LANES), F32),
            pltpu.VMEM((LANES, PACKED), BF16),
            pltpu.VMEM((PAIRS * WAVE, LATS * LANES), BF16),
            pltpu.VMEM((WAVE * 16, LANES), F32),
            message,
            message,
            pltpu.VMEM((CHUNKS, 2 * width, BLOCK), BF16),
            pltpu.VMEM((CHUNKS, BLOCK, 2 * width), BF16),
            pltpu.VMEM((XMAX // 2, 2 * width, 2 * LANES), BF16),
            pltpu.VMEM((XMAX // 2, BLOCK, 2 * LANES), F32),
            pltpu.VMEM((XMAX // 2, BLOCK, 2 * LANES), BF16),
            turns,
            turns,
            message,
            message,
            short,
            full,
            full,
            full,
            short,
            short,
            pltpu.VMEM((CHUNKS, LEFT_PART, LANES), BF16),
            pltpu.VMEM((CHUNKS, SENT - LEFT_PART, LANES), BF16),
            short,
            short,
            pltpu.VMEM((CHUNKS, FD, GROUP, 2, M), F32),
            each,
            each,
            pltpu.SemaphoreType.DMA,
            each,
            copies,
            copies,
            each,
            each,
            each,
            each,
            copies,
            copies,
        ],
        compiler_params=pltpu.CompilerParams(
            collective_id=0, has_side_effects=True, vmem_limit_bytes=60 << 20
        ),
    )(
        spec_in, legendre, jnp.asarray(fixed),
        wave_order, row_length, quad_weight, square_gain,
        wave_order.reshape(NB, LANES), mixing,
    )
    return pl.pallas_call(
        hand_over,
        out_shape=jax.ShapeDtypeStruct(result.shape, F32),
        in_specs=[ANY],
        out_specs=ANY,
        scratch_shapes=[
            pltpu.VMEM(result.shape, F32),
            pltpu.SemaphoreType.DMA((PIECES,)),
            pltpu.SemaphoreType.DMA((PIECES,)),
        ],
        compiler_params=pltpu.CompilerParams(vmem_limit_bytes=60 << 20),
    )(result)

def solution(mesh):
    in_specs = (P("fld", "wave", None, None), P("wave", "fld", None), P(), P(), P(), P(), P())
    out_specs = P("fld", "wave", None, None)
    return jax.shard_map(local, mesh=mesh, in_specs=in_specs, out_specs=out_specs, check_vma=False)
```

```python
import functools
import math

import jax
import jax.numpy as jnp
import numpy as np
from jax import lax
from jax.experimental import pallas as pl
from jax.experimental.pallas import tpu as pltpu
from jax.sharding import PartitionSpec as P

M = 1280
FL = 24
BLOCK = 512
LANES = 128
NB = M // LANES
PB = NB + 1
PACKED = PB * LANES
CHUNKS = 5
PAIRS = 4
WAVE = 32
FLD = 4
LATS = 4
FD = FL // FLD
ROWS = 2 * FD * PAIRS
HALF = BLOCK // 2
EVEN = HALF + 16
XMAX = 12
F32, BF16, I32 = jnp.float32, jnp.bfloat16, jnp.int32


def wave_tables():
    v = np.arange(BLOCK)
    angle = (v[:, None] * v[None, :] % BLOCK) * (2.0 * math.pi / BLOCK)
    return np.concatenate([np.cos(angle), -np.sin(angle)], axis=1).astype(np.float32)


def lane_maps():
    width = LATS * LANES
    lat_a, ab_a, level_a, half_a = (np.full(width, -1) for _ in range(4))
    for lat in range(LATS):
        for ab in range(2):
            for g in range(FLD):
                for c in range(2):
                    for f in range(FD):
                        at = LANES * lat + ((ab * FLD + g) * 2 + c) * FD + f
                        lat_a[at], ab_a[at], half_a[at], level_a[at] = lat, ab, c, FD * g + f
    lat_b, ab_b, level_b, half_b = (np.full(width, -2) for _ in range(4))
    for c in range(2):
        for ab in range(2):
            for lat in range(LATS):
                for f in range(FL):
                    at = LANES * (2 * c + ab) + FL * lat + f
                    lat_b[at], ab_b[at], half_b[at], level_b[at] = lat, ab, c, f
    same = (
        (lat_a[:, None] == lat_b[None, :])
        & (ab_a[:, None] == ab_b[None, :])
        & (half_a[:, None] == half_b[None, :])
    )
    pick = same & (level_a[:, None] == level_b[None, :])
    return pick.T.astype(np.float32)


def turn_pair(t):
    a = (t - 0.25) * (2.0 * math.pi)
    s = a * a
    sine = a * (
        1.0
        + s
        * (
            -1.0 / 6
            + s * (1.0 / 120 + s * (-1.0 / 5040 + s * (1.0 / 362880 - s * (1.0 / 39916800))))
        )
    )
    cosine = 1.0 + s * (
        -0.5
        + s
        * (
            1.0 / 24
            + s * (-1.0 / 720 + s * (1.0 / 40320 + s * (-1.0 / 3628800 + s * (1.0 / 479001600))))
        )
    )
    return -sine, cosine


def times(a, b):
    return a[0] * b[0] - a[1] * b[1], a[0] * b[1] + a[1] * b[0]


def back(a, b):
    return a[0] * b[0] + a[1] * b[1], a[1] * b[0] - a[0] * b[1]


SENT = NB * ROWS + 16
LEFT_PART = SENT // 32 * 16
GROUP = 8
MESH = pl.DeviceIdType.MESH
OTHERS = sorted(
    ((dz, dx, dc) for dz in range(4) for dx in range(4) for dc in range(2) if dz + dx + dc > 0),
    key=lambda d: -(min(d[0], 4 - d[0]) + min(d[1], 4 - d[1])),
)


def load_packed(leg_ref, packed_ref, first, q):
    q = jnp.broadcast_to(q.astype(F32), (LANES, LANES)).astype(BF16)
    spare = None
    for t in range(NB):
        one = leg_ref[first, :, LANES * t : LANES * (t + 1)]
        at = NB - 1 - t
        two = leg_ref[first + 1, :, LANES * at : LANES * (at + 1)]
        packed_ref[:, LANES * t : LANES * (t + 1)] = jnp.where(q <= t, one, two)
        spare = two if t == 0 else jnp.where(q == t, two, spare)
    packed_ref[:, LANES * NB :] = spare


def kernel(
    spec_ref, leg_ref, fixed_ref, own_ref, lengths_ref, weights_ref, gains_ref,
    order_ref, mixing_ref, out_ref,
    legs, base_ref, pick_ref, turn_ref, spec, rows, orders, mix_ref, column_orders,
    gathered, coeff, flipped, packed, wide, turn, sent, arrived, table, turned, waves, grid, update, edge,
    tr, ti, sent_back, arrived_back, opposite, part_right, part_left, part_own, to_right, to_left,
    first_left, first_right, second_left, second_right, results,
    leg_sem, spec_sem, const_sem, out_sem, ag_send, ag_recv, a_send, a_recv, b_send, b_recv,
    rs_send, rs_recv,
):
    w = lax.axis_index("wave")
    g = lax.axis_index("fld")
    right, left, across = lax.rem(g + 1, FLD), lax.rem(g + 3, FLD), lax.rem(g + 2, FLD)

    def spec_copy(k):
        return pltpu.make_async_copy(
            spec_ref.at[:, pl.ds(k * GROUP, GROUP)], spec.at[k], spec_sem.at[k]
        )

    def out_copy(k):
        return pltpu.make_async_copy(
            results.at[k], out_ref.at[:, pl.ds(k * GROUP, GROUP)], out_sem.at[k]
        )

    fixed_copy = pltpu.make_async_copy(fixed_ref, grid.at[:, pl.ds(0, BLOCK)], const_sem)

    def leg_copy(k):
        rows = pl.ds(k * GROUP, GROUP)
        return pltpu.make_async_copy(leg_ref.at[rows], legs.at[rows], leg_sem.at[k])

    def remote(src, dst, send, recv, to):
        return pltpu.make_async_remote_copy(
            src_ref=src, dst_ref=dst, send_sem=send, recv_sem=recv, device_id=to, device_id_type=MESH
        )

    to_r, to_l = (w, right), (w, left)
    head, rest = pl.ds(0, LEFT_PART), pl.ds(LEFT_PART, SENT - LEFT_PART)

    def own_right(k):
        block = gathered.at[k, g]
        return remote(block, block, ag_send.at[0, k], ag_recv.at[0, k], to_r)

    def own_left(k):
        block = gathered.at[k, g]
        return remote(block, block, ag_send.at[1, k], ag_recv.at[1, k], to_l)

    def pass_right(k):
        block = gathered.at[k, left, head]
        return remote(block, block, ag_send.at[2, k], ag_recv.at[2, k], to_r)

    def pass_left(k):
        block = gathered.at[k, right, rest]
        return remote(block, block, ag_send.at[3, k], ag_recv.at[3, k], to_l)

    def sum_first_right(k):
        return remote(
            opposite.at[k, head], first_left.at[k], rs_send.at[0, k], rs_recv.at[0, k], to_r
        )

    def sum_first_left(k):
        return remote(
            opposite.at[k, rest], first_right.at[k], rs_send.at[1, k], rs_recv.at[1, k], to_l
        )

    def sum_second_right(k):
        return remote(to_right.at[k], second_left.at[k], rs_send.at[2, k], rs_recv.at[2, k], to_r)

    def sum_second_left(k):
        return remote(to_left.at[k], second_right.at[k], rs_send.at[3, k], rs_recv.at[3, k], to_l)

    def exchange_all(k, count, src, dst, send, recv):
        some, others = pl.ds(k, count), pl.ds(0, WAVE - 1)
        return remote(src.at[some, others], dst.at[some, others], send.at[k], recv.at[k], (w, g))

    z, x, core = w // 8, lax.rem(w // 2, 4), lax.rem(w, 2)

    def exchange(k, count, src, dst, send, recv):
        some = pl.ds(k, count)
        for dz, dx, dc in OTHERS:
            to = lax.rem(z + dz, 4) * 8 + lax.rem(x + dx, 4) * 2 + lax.rem(core + dc, 2)
            remote(src.at[some, to], dst.at[some, w], send.at[k], recv.at[k], (to, g)).start()
        for n in range(count):
            dst[k + n, w] = src[k + n, w]

    for k in range(CHUNKS):
        spec_copy(k).start()
    fixed_copy.start()
    for k in range(CHUNKS):
        leg_copy(k).start()
    barrier = pltpu.get_barrier_semaphore()

    def greet(d, carry):
        pl.semaphore_signal(
            barrier, inc=1, device_id=(lax.rem(w + d, WAVE), g), device_id_type=MESH
        )
        return carry

    for to in (to_r, to_l):
        pl.semaphore_signal(barrier, inc=1, device_id=to, device_id_type=MESH)
    lax.fori_loop(1, WAVE, greet, 0)

    lane = lax.broadcasted_iota(I32, (ROWS, LANES), 1)
    pair_of_row = lax.broadcasted_iota(I32, (ROWS, LANES), 0) & (PAIRS - 1)

    def reverse(values):
        places = [lax.broadcasted_iota(I32, (LANES, LANES), dim) for dim in range(2)]
        flip = (places[0] + places[1] == LANES - 1).astype(F32)
        if values.dtype == BF16:
            return jnp.dot(values, flip.astype(BF16), preferred_element_type=F32)
        return jnp.dot(
            values, flip, precision=lax.Precision.HIGHEST, preferred_element_type=F32
        )

    def fold(spare, s):
        value = jnp.sum(jnp.where(lane == LANES - 1 - s, spare, 0.0), axis=1, keepdims=True)
        value = jnp.broadcast_to(value, (ROWS, LANES))
        spot = lane[:16]
        out = jnp.zeros((16, LANES), F32)
        for n in range(ROWS // 16):
            out = jnp.where(spot == n, value[16 * n : 16 * (n + 1)], out)
        return out

    def unfold(extras):
        spot = lane[:16]
        return jnp.concatenate(
            [
                jnp.broadcast_to(
                    jnp.sum(jnp.where(spot == n, extras, 0.0), axis=1, keepdims=True), (16, LANES)
                )
                for n in range(ROWS // 16)
            ],
            axis=0,
        )

    def recover(blocks, extras, m, kind):
        q, s = m >> 7, m & (LANES - 1)
        shared = blocks[0]
        for t in range(1, NB):
            shared = jnp.where(q == t, blocks[t], shared)
        back_again = reverse(shared.astype(kind))
        spot = LANES - 1 - s
        return jnp.where(lane > spot, back_again, jnp.where(lane == spot, unfold(extras), 0.0))

    def pack(k):
        first_row = (w * CHUNKS + k) * GROUP
        m = jnp.full((ROWS, LANES), own_ref[first_row], I32)
        for i in range(1, PAIRS):
            m = jnp.where(pair_of_row == i, own_ref[first_row + 2 * i], m)
        orders[k] = m
        q = m >> 7
        spec_copy(k).wait()
        for f in range(FD):
            for r in range(GROUP):
                values = spec[k, f, r].astype(F32)
                at = 2 * (f * GROUP + r)
                for t in range(NB):
                    rows[t, at : at + 2, :] = values[:, LANES * t : LANES * (t + 1)]
        first, second = [], []
        for t in range(NB):
            n = lane + LANES * t
            half = [
                jnp.concatenate(
                    [rows[t, pl.ds(2 * ab + c, FD * PAIRS, stride=4), :] for c in range(2)], axis=0
                )
                for ab in range(2)
            ]
            first.append(jnp.where(n >= m, half[0], 0.0))
            second.append(jnp.where(n >= M - 1 - m, half[1], 0.0))
        s = m & (LANES - 1)
        spare = second[NB - 1]
        for t in range(1, NB):
            spare = jnp.where(q == t, second[NB - 1 - t], spare)
        turned_round = reverse(spare.astype(BF16))
        for t in range(NB):
            shared = jnp.where(lane >= s, first[t], turned_round)
            block = jnp.where(q < t, first[t], jnp.where(q == t, shared, second[NB - 1 - t]))
            gathered[k, g, ROWS * t : ROWS * (t + 1), :] = block.astype(BF16)
        gathered[k, g, NB * ROWS :, :] = fold(spare, s).astype(BF16)

    def first_pack(k, carry):
        pack(k)

        @pl.when(k == 0)
        def _():
            pl.semaphore_wait(barrier, WAVE + 1)
            own_right(0).start()
            own_left(0).start()

        return carry

    lax.fori_loop(0, 2, first_pack, 0)

    spot = lax.broadcasted_iota(I32, (1, LANES), 1)
    lat_of = lambda x: sum((x >= FL * n).astype(I32) for n in range(1, LATS))
    level_of = lambda x: x - FL * lat_of(x)
    length, weight = jnp.zeros((1, LANES), I32), jnp.zeros((1, LANES), F32)
    for lat in range(LATS):
        at = (g * LATS + lat) * WAVE + w
        length = jnp.where(spot >= FL * lat, lengths_ref[at], length)
        weight = jnp.where(spot >= FL * lat, weights_ref[at], weight)
    gain = jnp.zeros((1, LANES), F32)
    for f in range(FL):
        gain = jnp.where(level_of(spot) == f, gains_ref[f], gain)
    gain = jnp.concatenate([gain, gain], axis=1)
    real_length = length.astype(F32)
    root = lax.rsqrt(real_length)
    scale = weight * (root * (1.5 - 0.5 * real_length * root * root))
    half_length = length >> 1
    inverse_length = 1.0 / real_length
    count = length >> 9

    spot = lax.broadcasted_iota(I32, (FL, LANES), 1)
    level = lax.broadcasted_iota(I32, (FL, LANES), 0)
    hot = ((level_of(spot) == level) & (spot < LATS * FL)).astype(F32)
    across_levels = (((0,), (0,)), ((), ()))
    spread = lax.dot_general(
        mixing_ref[...], hot, across_levels, precision=lax.Precision.HIGHEST,
        preferred_element_type=F32,
    )
    spread = lax.dot_general(
        hot, spread, across_levels, precision=lax.Precision.HIGHEST, preferred_element_type=F32
    )
    lats = [lat_of(lax.broadcasted_iota(I32, (LANES, LANES), dim)) for dim in range(2)]
    spread = jnp.where(lats[0] == lats[1], spread, 0.0)
    high_part = spread.astype(BF16)
    mix_ref[:LANES] = high_part
    mix_ref[LANES:] = (spread - high_part.astype(F32)).astype(BF16)

    width = WAVE * GROUP

    def tables(k):
        spot = lax.broadcasted_iota(I32, (width, LANES), 1)
        row = lax.broadcasted_iota(I32, (width, LANES), 0)
        row = (row >> 3) * (CHUNKS * GROUP) + k * GROUP + (row & 7)
        m = jnp.broadcast_to(order_ref[0:1, :], (width, LANES))
        for n in range(1, NB):
            m = jnp.where((row >> 7) == n, order_ref[n : n + 1, :], m)
        m = jnp.where(spot == (row & 127), m, 0).astype(F32)
        m = jnp.broadcast_to(jnp.sum(m, axis=1, keepdims=True), (width, LANES))
        across_lanes = m.T[0:1, :].astype(I32)
        m = m.astype(I32)
        column_orders[k] = m
        t = jnp.where(m < half_length, m.astype(F32) * inverse_length, 0.0)
        tr[k], ti[k] = turn_pair(t)

        spot = lax.broadcasted_iota(I32, (width, BLOCK), 1)
        m = jnp.concatenate([m & (BLOCK - 1)] * (BLOCK // LANES), axis=1)
        hot = (spot == m).astype(F32).astype(BF16)
        for half in range(2):
            table[k, half * width : (half + 1) * width] = jnp.dot(
                hot, base_ref[:, half * BLOCK : half * BLOCK + HALF], preferred_element_type=F32
            ).astype(BF16)
        spot = lax.broadcasted_iota(I32, (BLOCK, width), 0)
        hot = (spot == (across_lanes & (BLOCK - 1))).astype(F32).astype(BF16)
        turned[k, :EVEN] = jnp.dot(
            base_ref[:EVEN, :BLOCK], hot, preferred_element_type=F32
        ).astype(BF16)
        turned[k, EVEN:] = jnp.dot(
            base_ref[:HALF, BLOCK:], hot, preferred_element_type=F32
        ).astype(BF16)

    fixed_copy.wait()
    side = 2 * LANES
    for n in range(4):
        base_ref[:, side * n : side * (n + 1)] = grid[n, :BLOCK].astype(BF16)
    for n in range(2):
        pick_ref[:, side * n : side * (n + 1)] = grid[4 + n, :BLOCK].astype(BF16)
        turn_ref[side * n : side * (n + 1), :] = grid[4 + n, :BLOCK].T.astype(BF16)
    for s in range(XMAX // 2):
        grid[s] = jnp.zeros((EVEN + HALF, side), F32)

    def legendre_sum(k):
        for d in range(FLD):
            group = slice(ROWS * d, ROWS * (d + 1))
            blocks = [gathered[k, d, ROWS * t : ROWS * (t + 1), :] for t in range(NB)]
            for t in range(NB):
                coeff[t, group] = blocks[t].astype(F32)
            extras = gathered[k, d, NB * ROWS :, :].astype(F32)
            coeff[NB, group] = recover([coeff[t, group] for t in range(NB)], extras, orders[k], BF16)
        for i in range(PAIRS):
            m = orders[k, i : i + 1, :]
            q = m >> 7
            load_packed(legs, packed, GROUP * k + 2 * i, q)
            spot = lax.broadcasted_iota(I32, (1, LANES), 1)
            weights = []
            for t in range(PB):
                block = coeff[t, pl.ds(i, ROWS, stride=PAIRS), :]
                if t < NB:
                    lead = jnp.where(spot + LANES * t >= m, block, 0.0)
                    other = jnp.where(q > t, block, 0.0)
                else:
                    lead, other = jnp.zeros_like(block), block
                weights.append(
                    jnp.concatenate([lead, other, jnp.zeros((32, LANES), F32)], axis=0).astype(BF16)
                )
            fourier = lax.dot_general(
                packed[...],
                jnp.concatenate(weights, axis=1),
                (((1,), (1,)), ((), ())),
                preferred_element_type=F32,
            ).astype(BF16)
            for lat in range(LATS):
                wide[WAVE * i : WAVE * (i + 1), LANES * lat : LANES * (lat + 1)] = fourier[
                    WAVE * lat : WAVE * (lat + 1)
                ]
        placed = jnp.dot(wide[...], turn_ref[...], preferred_element_type=F32)
        for c in range(2):
            for ab in range(2):
                for i in range(PAIRS):
                    at = 2 * c + ab
                    turn[pl.ds(c * 8 + 2 * i + ab, WAVE, stride=16), :] = placed[
                        WAVE * i : WAVE * (i + 1), LANES * at : LANES * (at + 1)
                    ]
        sent[k] = turn[...].reshape(WAVE, 16, LANES).astype(BF16)

    def grid_sum(k, last):
        keep = column_orders[k] < half_length
        one = tr[k], ti[k]
        two = times(one, one)
        four = times(two, two)
        eight = times(four, four)
        eleven = times(times(eight, two), one)
        x = arrived[k].astype(F32)
        x = jnp.concatenate(
            [x[:, :8].reshape(width, LANES), x[:, 8:].reshape(width, LANES)], axis=0
        ).astype(BF16)
        x = jnp.dot(
            jnp.concatenate([x, x], axis=1), mix_ref[...], preferred_element_type=F32
        )
        x0 = jnp.where(keep, x[:width], 0.0)
        x1 = jnp.where(keep, x[width:], 0.0)
        h = times((x0, x1), eleven)
        for s in range(XMAX // 2):
            for side in range(2):
                span = slice(LANES * side, LANES * (side + 1))
                waves[s, :width, span] = h[0].astype(BF16)
                waves[s, width:, span] = h[1].astype(BF16)
                h = back(h, one)
        for s in range(XMAX // 2):
            even = grid[s, :EVEN] + jnp.dot(
                turned[k, :EVEN], waves[s, :width], preferred_element_type=F32
            )
            odd = grid[s, EVEN:] + jnp.dot(
                turned[k, EVEN:], waves[s, width:], preferred_element_type=F32
            )
            if not last:
                grid[s, :EVEN] = even
                grid[s, EVEN:] = odd
                continue
            high = XMAX - 1 - 2 * s
            live = jnp.concatenate(
                [(high < count).astype(F32), (high - 1 < count).astype(F32)], axis=1
            )

            def column(values):
                mixed = values * float(M) ** (-0.5)
                return (mixed + gain * mixed * mixed) * live

            one = column(even[:HALF] + odd)
            two = column(even[:HALF] - odd)
            two = jnp.where(lax.broadcasted_iota(I32, two.shape, 0) == 0, 0.0, two)
            update[s, :HALF] = (one + two).astype(BF16)
            update[s, HALF:] = (one - two).astype(BF16)
            edge[s] = column(even[HALF : HALF + 8])

    own_right(1).start()
    own_left(1).start()
    pack(2)
    tables(0)

    def some_tables(k, carry):
        tables(k)
        return carry

    def gather_step(k, carry):
        @pl.when(k < CHUNKS)
        def _():
            own_right(k).wait_recv()
            pass_right(k).start()
            own_left(k).wait_recv()
            pass_left(k).start()

        @pl.when(k + 3 < CHUNKS)
        def _():
            pack(k + 3)
            lax.fori_loop(2 * k + 1, 2 * k + 3, some_tables, 0)

        @pl.when(k + 2 < CHUNKS)
        def _():
            own_right(k + 2).start()
            own_left(k + 2).start()

        @pl.when((k >= 1) & (k <= CHUNKS))
        def _():
            pass_right(k - 1).wait_recv()
            pass_left(k - 1).wait_recv()
            leg_copy(k - 1).wait()
            legendre_sum(k - 1)

        @pl.when(k == 2)
        def _():
            exchange(0, 2, sent, arrived, a_send, a_recv)

        @pl.when(k >= 3)
        def _():
            exchange(k - 1, 1, sent, arrived, a_send, a_recv)

        @pl.when(k == 3)
        def _():
            exchange_all(0, 2, sent, arrived, a_send, a_recv).wait_recv()

        @pl.when(k == 4)
        def _():
            grid_sum(0, False)

        return carry

    lax.fori_loop(0, CHUNKS + 1, gather_step, 0)

    def late_sum(k, carry):
        @pl.when(k >= 2)
        def _():
            exchange_all(k, 1, sent, arrived, a_send, a_recv).wait_recv()

        grid_sum(k, False)
        return carry

    lax.fori_loop(1, CHUNKS - 1, late_sum, 0)
    exchange_all(CHUNKS - 1, 1, sent, arrived, a_send, a_recv).wait_recv()
    grid_sum(CHUNKS - 1, True)

    def grid_back(k):
        t = tr[k], ti[k]
        d = jnp.zeros((width, LANES), F32), jnp.zeros((width, LANES), F32)
        sign = 1.0 - 2.0 * (column_orders[k] & 1).astype(F32)
        for s in range(XMAX // 2):
            even = jnp.dot(table[k, :width], update[s, :HALF], preferred_element_type=F32)
            odd = jnp.dot(table[k, width:], update[s, HALF:], preferred_element_type=F32)
            for side in range(2):
                span = slice(LANES * side, LANES * (side + 1))
                if s + side > 0:
                    d = back(d, t)
                d = d[0] + (even[:, span] + sign * edge[s, 0:1, span]), d[1] + odd[:, span]
        keep = column_orders[k] < half_length
        d0 = jnp.where(keep, d[0] * scale, 0.0).reshape(WAVE, 8, LANES)
        d1 = jnp.where(keep, d[1] * scale, 0.0).reshape(WAVE, 8, LANES)
        sent_back[k] = jnp.concatenate([d0, d1], axis=1).astype(BF16)

    def legendre_back(k):
        turn[...] = arrived_back[k].reshape(WAVE * 16, LANES).astype(F32)
        for c in range(2):
            for ab in range(2):
                for i in range(PAIRS):
                    at = 2 * c + ab
                    wide[WAVE * i : WAVE * (i + 1), LANES * at : LANES * (at + 1)] = turn[
                        pl.ds(c * 8 + 2 * i + ab, WAVE, stride=16), :
                    ].astype(BF16)
        spread = jnp.dot(wide[...], pick_ref[...], preferred_element_type=F32)
        for i in range(PAIRS):
            q = orders[k, i : i + 1, :] >> 7
            load_packed(legs, packed, GROUP * k + 2 * i, q)
            values = jnp.concatenate(
                [
                    spread[WAVE * i : WAVE * (i + 1), LANES * lat : LANES * (lat + 1)]
                    for lat in range(LATS)
                ],
                axis=0,
            )
            values = values.T.astype(BF16)
            result = jnp.dot(values[: 2 * ROWS], packed[...], preferred_element_type=F32)
            for t in range(PB):
                span = slice(LANES * t, LANES * (t + 1))
                if t < NB:
                    block = jnp.where(q <= t, result[:ROWS, span], result[ROWS:, span])
                else:
                    block = result[ROWS:, span]
                coeff[t, pl.ds(i, ROWS, stride=PAIRS), :] = block
        m = orders[k]
        q, s = m >> 7, m & (LANES - 1)
        flipped[...] = reverse(coeff[NB].astype(BF16))
        own_rows = lambda d: pl.ds(pl.multiple_of(d * ROWS, 16), ROWS)
        places = (
            (opposite, across, BF16), (part_right, right, F32), (part_left, left, F32), (part_own, g, F32)
        )
        for place, d, kind in places:
            for t in range(NB):
                shared = (q == t) & (lane < s)
                block = jnp.where(shared, flipped[own_rows(d), :], coeff[t, own_rows(d), :])
                place[k, ROWS * t : ROWS * (t + 1), :] = block.astype(kind)
            place[k, NB * ROWS :, :] = fold(coeff[NB, own_rows(d), :], s).astype(kind)

    def sum_second(k):
        cut = LEFT_PART
        to_right[k, :cut] = (part_right[k, :cut] + first_left[k].astype(F32)).astype(BF16)
        to_right[k, cut:] = part_right[k, cut:].astype(BF16)
        to_left[k, :cut] = part_left[k, :cut].astype(BF16)
        to_left[k, cut:] = (part_left[k, cut:] + first_right[k].astype(F32)).astype(BF16)

    def unpack(k):
        m = orders[k]
        q = m >> 7
        whole = lambda at: (
            part_own[k, at, :] + second_left[k, at, :].astype(F32) + second_right[k, at, :].astype(F32)
        )
        total = [whole(slice(ROWS * t, ROWS * (t + 1))) for t in range(NB)]
        total.append(recover(total, whole(slice(NB * ROWS, SENT)), m, F32))
        for t in range(NB):
            n = lane + LANES * t
            other = jnp.where(NB - 1 - t == q, total[NB], total[NB - 1 - t])
            both = jnp.where(n >= m, total[t], 0.0), jnp.where(n >= M - 1 - m, other, 0.0)
            count = FD * PAIRS
            for ab in range(2):
                for c in range(2):
                    rows[t, pl.ds(2 * ab + c, count, stride=4), :] = both[ab][count * c : count * (c + 1)]
        for f in range(FD):
            for r in range(GROUP):
                at = 2 * (f * GROUP + r)
                results[k, f, r] = jnp.concatenate(
                    [rows[t, at : at + 2, :] for t in range(NB)], axis=1
                )

    def back_step(k):
        grid_back(k)
        exchange(k, 1, sent_back, arrived_back, b_send, b_recv)

    def ahead(k, carry):
        back_step(k)
        return carry

    lax.fori_loop(0, 3, ahead, 0)

    def scatter_step(k, carry):
        @pl.when(k < CHUNKS)
        def _():
            exchange_all(k, 1, sent_back, arrived_back, b_send, b_recv).wait_recv()
            legendre_back(k)
            sum_first_right(k).start()
            sum_first_left(k).start()

        @pl.when((k >= 1) & (k <= CHUNKS))
        def _():
            sum_first_right(k - 1).wait_recv()
            sum_first_left(k - 1).wait_recv()
            sum_second(k - 1)
            sum_second_right(k - 1).start()
            sum_second_left(k - 1).start()

        @pl.when((k >= 1) & (k + 2 < CHUNKS))
        def _():
            back_step(k + 2)

        @pl.when(k >= 4)
        def _():
            sum_second_right(k - 4).wait_recv()
            sum_second_left(k - 4).wait_recv()
            unpack(k - 4)
            out_copy(k - 4).start()

        return carry

    lax.fori_loop(0, CHUNKS + 4, scatter_step, 0)

    def finish(k, carry):
        for copy in (own_right, own_left, pass_right, pass_left):
            copy(k).wait_send()
        for copy in (sum_first_right, sum_first_left, sum_second_right, sum_second_left):
            copy(k).wait_send()
        exchange_all(k, 1, sent_back, arrived_back, b_send, b_recv).wait_send()
        out_copy(k).wait()
        return carry

    lax.fori_loop(0, CHUNKS, finish, 0)
    for k, count in ((0, 2), (2, 1), (3, 1), (4, 1)):
        exchange_all(k, count, sent, arrived, a_send, a_recv).wait_send()


PIECES = 5


def hand_over(src_ref, dst_ref, held, sem_in, sem_out):
    count = src_ref.shape[1] // PIECES
    spans = [pl.ds(n * count, count) for n in range(PIECES)]
    reads = [
        pltpu.make_async_copy(src_ref.at[:, at], held.at[:, at], sem_in.at[n])
        for n, at in enumerate(spans)
    ]
    writes = [
        pltpu.make_async_copy(held.at[:, at], dst_ref.at[:, at], sem_out.at[n])
        for n, at in enumerate(spans)
    ]
    for read in reads:
        read.start()
    for read, write in zip(reads, writes):
        read.wait()
        write.start()
    for write in writes:
        write.wait()


VMEM = pl.BlockSpec(memory_space=pltpu.VMEM)
SMEM = pl.BlockSpec(memory_space=pltpu.SMEM)
ANY = pl.BlockSpec(memory_space=pl.ANY)


def local(spec_in, legendre, wave_order, row_length, quad_weight, mixing, square_gain):
    fixed = np.concatenate([wave_tables(), lane_maps()], axis=1)
    fixed = fixed.reshape(BLOCK, XMAX // 2, 2 * LANES).transpose(1, 0, 2)
    width = WAVE * GROUP
    message = pltpu.VMEM((CHUNKS, WAVE, 16, LANES), BF16)
    full = pltpu.VMEM((CHUNKS, SENT, LANES), F32)
    short = pltpu.VMEM((CHUNKS, SENT, LANES), BF16)
    turns = pltpu.VMEM((CHUNKS, width, LANES), F32)
    places = pltpu.VMEM((LATS * LANES, LATS * LANES), BF16)
    copies = pltpu.SemaphoreType.DMA((4, CHUNKS))
    each = pltpu.SemaphoreType.DMA((CHUNKS,))
    result = pl.pallas_call(
        kernel,
        out_shape=jax.ShapeDtypeStruct((FD, GROUP * CHUNKS, 2, M), F32),
        in_specs=[ANY] * 3 + [SMEM] * 4 + [VMEM] * 2,
        out_specs=ANY,
        scratch_shapes=[
            pltpu.VMEM((GROUP * CHUNKS, FLD * WAVE, M), BF16),
            pltpu.VMEM((BLOCK, 2 * BLOCK), BF16),
            places,
            places,
            pltpu.VMEM((CHUNKS, FD, GROUP, 2, M), BF16),
            pltpu.VMEM((NB, 2 * ROWS, LANES), F32),
            pltpu.VMEM((CHUNKS, ROWS, LANES), I32),
            pltpu.VMEM((2 * LANES, LANES), BF16),
            pltpu.VMEM((CHUNKS, width, LANES), I32),
            pltpu.VMEM((CHUNKS, FLD, SENT, LANES), BF16),
            pltpu.VMEM((PB, FLD * ROWS, LANES), F32),
            pltpu.VMEM((FLD * ROWS, LANES), F32),
            pltpu.VMEM((LANES, PACKED), BF16),
            pltpu.VMEM((PAIRS * WAVE, LATS * LANES), BF16),
            pltpu.VMEM((WAVE * 16, LANES), F32),
            message,
            message,
            pltpu.VMEM((CHUNKS, 2 * width, HALF), BF16),
            pltpu.VMEM((CHUNKS, EVEN + HALF, width), BF16),
            pltpu.VMEM((XMAX // 2, 2 * width, 2 * LANES), BF16),
            pltpu.VMEM((XMAX // 2, EVEN + HALF, 2 * LANES), F32),
            pltpu.VMEM((XMAX // 2, BLOCK, 2 * LANES), BF16),
            pltpu.VMEM((XMAX // 2, 8, 2 * LANES), F32),
            turns,
            turns,
            message,
            message,
            short,
            full,
            full,
            full,
            short,
            short,
            pltpu.VMEM((CHUNKS, LEFT_PART, LANES), BF16),
            pltpu.VMEM((CHUNKS, SENT - LEFT_PART, LANES), BF16),
            short,
            short,
            pltpu.VMEM((CHUNKS, FD, GROUP, 2, M), F32),
            each,
            each,
            pltpu.SemaphoreType.DMA,
            each,
            copies,
            copies,
            each,
            each,
            each,
            each,
            copies,
            copies,
        ],
        compiler_params=pltpu.CompilerParams(
            collective_id=0, has_side_effects=True, vmem_limit_bytes=60 << 20
        ),
    )(
        spec_in, legendre, jnp.asarray(fixed),
        wave_order, row_length, quad_weight, square_gain,
        wave_order.reshape(NB, LANES), mixing,
    )
    return pl.pallas_call(
        hand_over,
        out_shape=jax.ShapeDtypeStruct(result.shape, F32),
        in_specs=[ANY],
        out_specs=ANY,
        scratch_shapes=[
            pltpu.VMEM(result.shape, F32),
            pltpu.SemaphoreType.DMA((PIECES,)),
            pltpu.SemaphoreType.DMA((PIECES,)),
        ],
        compiler_params=pltpu.CompilerParams(vmem_limit_bytes=60 << 20),
    )(result)

def solution(mesh):
    in_specs = (P("fld", "wave", None, None), P("wave", "fld", None), P(), P(), P(), P(), P())
    out_specs = P("fld", "wave", None, None)
    return jax.shard_map(local, mesh=mesh, in_specs=in_specs, out_specs=out_specs, check_vma=False)
```

```python
import functools
import math

import jax
import jax.numpy as jnp
import numpy as np
from jax import lax
from jax.experimental import pallas as pl
from jax.experimental.pallas import tpu as pltpu
from jax.sharding import PartitionSpec as P

M = 1280
FL = 24
BLOCK = 512
LANES = 128
NB = M // LANES
PB = NB + 1
PACKED = PB * LANES
CHUNKS = 5
PAIRS = 4
WAVE = 32
FLD = 4
LATS = 4
FD = FL // FLD
ROWS = 2 * FD * PAIRS
HALF = BLOCK // 2
EVEN = HALF + 16
XMAX = 12
F32, BF16, I32 = jnp.float32, jnp.bfloat16, jnp.int32


def wave_tables():
    v = np.arange(BLOCK)
    angle = (v[:, None] * v[None, :] % BLOCK) * (2.0 * math.pi / BLOCK)
    return np.concatenate([np.cos(angle), -np.sin(angle)], axis=1).astype(np.float32)


def lane_maps():
    width = LATS * LANES
    lat_a, ab_a, level_a, half_a = (np.full(width, -1) for _ in range(4))
    for lat in range(LATS):
        for ab in range(2):
            for g in range(FLD):
                for c in range(2):
                    for f in range(FD):
                        at = LANES * lat + ((ab * FLD + g) * 2 + c) * FD + f
                        lat_a[at], ab_a[at], half_a[at], level_a[at] = lat, ab, c, FD * g + f
    lat_b, ab_b, level_b, half_b = (np.full(width, -2) for _ in range(4))
    for c in range(2):
        for ab in range(2):
            for lat in range(LATS):
                for f in range(FL):
                    at = LANES * (2 * c + ab) + FL * lat + f
                    lat_b[at], ab_b[at], half_b[at], level_b[at] = lat, ab, c, f
    same = (
        (lat_a[:, None] == lat_b[None, :])
        & (ab_a[:, None] == ab_b[None, :])
        & (half_a[:, None] == half_b[None, :])
    )
    pick = same & (level_a[:, None] == level_b[None, :])
    return pick.T.astype(np.float32)


def turn_pair(t):
    a = (t - 0.25) * (2.0 * math.pi)
    s = a * a
    sine = a * (
        1.0
        + s
        * (
            -1.0 / 6
            + s * (1.0 / 120 + s * (-1.0 / 5040 + s * (1.0 / 362880 - s * (1.0 / 39916800))))
        )
    )
    cosine = 1.0 + s * (
        -0.5
        + s
        * (
            1.0 / 24
            + s * (-1.0 / 720 + s * (1.0 / 40320 + s * (-1.0 / 3628800 + s * (1.0 / 479001600))))
        )
    )
    return -sine, cosine


def times(a, b):
    return a[0] * b[0] - a[1] * b[1], a[0] * b[1] + a[1] * b[0]


def back(a, b):
    return a[0] * b[0] + a[1] * b[1], a[1] * b[0] - a[0] * b[1]


SENT = NB * ROWS + 16
LEFT_PART = SENT // 32 * 16
GROUP = 8
MESH = pl.DeviceIdType.MESH
OTHERS = sorted(
    ((dz, dx, dc) for dz in range(4) for dx in range(4) for dc in range(2) if dz + dx + dc > 0),
    key=lambda d: -(min(d[0], 4 - d[0]) + min(d[1], 4 - d[1])),
)


def load_packed(leg_ref, packed_ref, first, q):
    q = jnp.broadcast_to(q.astype(F32), (LANES, LANES)).astype(BF16)
    spare = None
    for t in range(NB):
        one = leg_ref[first, :, LANES * t : LANES * (t + 1)]
        at = NB - 1 - t
        two = leg_ref[first + 1, :, LANES * at : LANES * (at + 1)]
        packed_ref[:, LANES * t : LANES * (t + 1)] = jnp.where(q <= t, one, two)
        spare = two if t == 0 else jnp.where(q == t, two, spare)
    packed_ref[:, LANES * NB :] = spare


def kernel(
    spec_ref, leg_ref, fixed_ref, own_ref, lengths_ref, weights_ref, gains_ref,
    order_ref, mixing_ref, out_ref,
    legs, base_ref, pick_ref, turn_ref, spec, rows, orders, mix_ref, column_orders,
    gathered, coeff, flipped, packed, wide, turn, sent, arrived, table, turned, waves, grid, update, edge,
    tr, ti, sent_back, arrived_back, opposite, part_right, part_left, part_own, to_right, to_left,
    first_left, first_right, second_left, second_right, results,
    leg_sem, spec_sem, const_sem, out_sem, ag_send, ag_recv, a_send, a_recv, b_send, b_recv,
    rs_send, rs_recv,
):
    w = lax.axis_index("wave")
    g = lax.axis_index("fld")
    right, left, across = lax.rem(g + 1, FLD), lax.rem(g + 3, FLD), lax.rem(g + 2, FLD)

    def spec_copy(k):
        return pltpu.make_async_copy(
            spec_ref.at[:, pl.ds(k * GROUP, GROUP)], spec.at[k], spec_sem.at[k]
        )

    def out_copy(k):
        return pltpu.make_async_copy(
            results.at[k], out_ref.at[:, pl.ds(k * GROUP, GROUP)], out_sem.at[k]
        )

    fixed_copy = pltpu.make_async_copy(fixed_ref, grid.at[:, pl.ds(0, BLOCK)], const_sem)

    def leg_copy(k):
        rows = pl.ds(k * GROUP, GROUP)
        return pltpu.make_async_copy(leg_ref.at[rows], legs.at[rows], leg_sem.at[k])

    def remote(src, dst, send, recv, to):
        return pltpu.make_async_remote_copy(
            src_ref=src, dst_ref=dst, send_sem=send, recv_sem=recv, device_id=to, device_id_type=MESH
        )

    to_r, to_l = (w, right), (w, left)
    head, rest = pl.ds(0, LEFT_PART), pl.ds(LEFT_PART, SENT - LEFT_PART)

    def own_right(k):
        block = gathered.at[k, g]
        return remote(block, block, ag_send.at[0, k], ag_recv.at[0, k], to_r)

    def own_left(k):
        block = gathered.at[k, g]
        return remote(block, block, ag_send.at[1, k], ag_recv.at[1, k], to_l)

    def pass_right(k):
        block = gathered.at[k, left, head]
        return remote(block, block, ag_send.at[2, k], ag_recv.at[2, k], to_r)

    def pass_left(k):
        block = gathered.at[k, right, rest]
        return remote(block, block, ag_send.at[3, k], ag_recv.at[3, k], to_l)

    def sum_first_right(k):
        return remote(
            opposite.at[k, head], first_left.at[k], rs_send.at[0, k], rs_recv.at[0, k], to_r
        )

    def sum_first_left(k):
        return remote(
            opposite.at[k, rest], first_right.at[k], rs_send.at[1, k], rs_recv.at[1, k], to_l
        )

    def sum_second_right(k):
        return remote(to_right.at[k], second_left.at[k], rs_send.at[2, k], rs_recv.at[2, k], to_r)

    def sum_second_left(k):
        return remote(to_left.at[k], second_right.at[k], rs_send.at[3, k], rs_recv.at[3, k], to_l)

    def exchange_all(k, count, src, dst, send, recv):
        some, others = pl.ds(k, count), pl.ds(0, WAVE - 1)
        return remote(src.at[some, others], dst.at[some, others], send.at[k], recv.at[k], (w, g))

    z, x, core = w // 8, lax.rem(w // 2, 4), lax.rem(w, 2)

    def exchange(k, count, src, dst, send, recv):
        some = pl.ds(k, count)
        for dz, dx, dc in OTHERS:
            to = lax.rem(z + dz, 4) * 8 + lax.rem(x + dx, 4) * 2 + lax.rem(core + dc, 2)
            remote(src.at[some, to], dst.at[some, w], send.at[k], recv.at[k], (to, g)).start()
        for n in range(count):
            dst[k + n, w] = src[k + n, w]

    for k in range(CHUNKS):
        spec_copy(k).start()
    fixed_copy.start()
    for k in range(CHUNKS):
        leg_copy(k).start()
    barrier = pltpu.get_barrier_semaphore()

    def greet(d, carry):
        pl.semaphore_signal(
            barrier, inc=1, device_id=(lax.rem(w + d, WAVE), g), device_id_type=MESH
        )
        return carry

    for to in (to_r, to_l):
        pl.semaphore_signal(barrier, inc=1, device_id=to, device_id_type=MESH)
    lax.fori_loop(1, WAVE, greet, 0)

    lane = lax.broadcasted_iota(I32, (ROWS, LANES), 1)
    pair_of_row = lax.broadcasted_iota(I32, (ROWS, LANES), 0) & (PAIRS - 1)

    def reverse(values):
        places = [lax.broadcasted_iota(I32, (LANES, LANES), dim) for dim in range(2)]
        flip = (places[0] + places[1] == LANES - 1).astype(F32)
        if values.dtype == BF16:
            return jnp.dot(values, flip.astype(BF16), preferred_element_type=F32)
        return jnp.dot(
            values, flip, precision=lax.Precision.HIGHEST, preferred_element_type=F32
        )

    def fold(spare, s):
        value = jnp.sum(jnp.where(lane == LANES - 1 - s, spare, 0.0), axis=1, keepdims=True)
        value = jnp.broadcast_to(value, (ROWS, LANES))
        spot = lane[:16]
        out = jnp.zeros((16, LANES), F32)
        for n in range(ROWS // 16):
            out = jnp.where(spot == n, value[16 * n : 16 * (n + 1)], out)
        return out

    def unfold(extras):
        spot = lane[:16]
        return jnp.concatenate(
            [
                jnp.broadcast_to(
                    jnp.sum(jnp.where(spot == n, extras, 0.0), axis=1, keepdims=True), (16, LANES)
                )
                for n in range(ROWS // 16)
            ],
            axis=0,
        )

    def recover(blocks, extras, m, kind):
        q, s = m >> 7, m & (LANES - 1)
        shared = blocks[0]
        for t in range(1, NB):
            shared = jnp.where(q == t, blocks[t], shared)
        back_again = reverse(shared.astype(kind))
        spot = LANES - 1 - s
        return jnp.where(lane > spot, back_again, jnp.where(lane == spot, unfold(extras), 0.0))

    def pack(k):
        first_row = (w * CHUNKS + k) * GROUP
        m = jnp.full((ROWS, LANES), own_ref[first_row], I32)
        for i in range(1, PAIRS):
            m = jnp.where(pair_of_row == i, own_ref[first_row + 2 * i], m)
        orders[k] = m
        q = m >> 7
        spec_copy(k).wait()
        for f in range(FD):
            for r in range(GROUP):
                values = spec[k, f, r].astype(F32)
                at = 2 * (f * GROUP + r)
                for t in range(NB):
                    rows[t, at : at + 2, :] = values[:, LANES * t : LANES * (t + 1)]
        first, second = [], []
        for t in range(NB):
            n = lane + LANES * t
            half = [
                jnp.concatenate(
                    [rows[t, pl.ds(2 * ab + c, FD * PAIRS, stride=4), :] for c in range(2)], axis=0
                )
                for ab in range(2)
            ]
            first.append(jnp.where(n >= m, half[0], 0.0))
            second.append(jnp.where(n >= M - 1 - m, half[1], 0.0))
        s = m & (LANES - 1)
        spare = second[NB - 1]
        for t in range(1, NB):
            spare = jnp.where(q == t, second[NB - 1 - t], spare)
        turned_round = reverse(spare.astype(BF16))
        for t in range(NB):
            shared = jnp.where(lane >= s, first[t], turned_round)
            block = jnp.where(q < t, first[t], jnp.where(q == t, shared, second[NB - 1 - t]))
            gathered[k, g, ROWS * t : ROWS * (t + 1), :] = block.astype(BF16)
        gathered[k, g, NB * ROWS :, :] = fold(spare, s).astype(BF16)

    def first_pack(k, carry):
        pack(k)

        @pl.when(k == 0)
        def _():
            pl.semaphore_wait(barrier, WAVE + 1)
            own_right(0).start()
            own_left(0).start()

        return carry

    lax.fori_loop(0, 2, first_pack, 0)

    spot = lax.broadcasted_iota(I32, (1, LANES), 1)
    lat_of = lambda x: sum((x >= FL * n).astype(I32) for n in range(1, LATS))
    level_of = lambda x: x - FL * lat_of(x)
    length, weight = jnp.zeros((1, LANES), I32), jnp.zeros((1, LANES), F32)
    for lat in range(LATS):
        at = (g * LATS + lat) * WAVE + w
        length = jnp.where(spot >= FL * lat, lengths_ref[at], length)
        weight = jnp.where(spot >= FL * lat, weights_ref[at], weight)
    gain = jnp.zeros((1, LANES), F32)
    for f in range(FL):
        gain = jnp.where(level_of(spot) == f, gains_ref[f], gain)
    gain = jnp.concatenate([gain, gain], axis=1)
    real_length = length.astype(F32)
    root = lax.rsqrt(real_length)
    scale = weight * (root * (1.5 - 0.5 * real_length * root * root))
    half_length = length >> 1
    inverse_length = 1.0 / real_length
    count = length >> 9

    spot = lax.broadcasted_iota(I32, (FL, LANES), 1)
    level = lax.broadcasted_iota(I32, (FL, LANES), 0)
    hot = ((level_of(spot) == level) & (spot < LATS * FL)).astype(F32)
    across_levels = (((0,), (0,)), ((), ()))
    spread = lax.dot_general(
        mixing_ref[...], hot, across_levels, precision=lax.Precision.HIGHEST,
        preferred_element_type=F32,
    )
    spread = lax.dot_general(
        hot, spread, across_levels, precision=lax.Precision.HIGHEST, preferred_element_type=F32
    )
    lats = [lat_of(lax.broadcasted_iota(I32, (LANES, LANES), dim)) for dim in range(2)]
    spread = jnp.where(lats[0] == lats[1], spread, 0.0)
    high_part = spread.astype(BF16)
    mix_ref[:LANES] = high_part
    mix_ref[LANES:] = (spread - high_part.astype(F32)).astype(BF16)

    width = WAVE * GROUP

    def tables(k):
        spot = lax.broadcasted_iota(I32, (width, LANES), 1)
        row = lax.broadcasted_iota(I32, (width, LANES), 0)
        row = (row >> 3) * (CHUNKS * GROUP) + k * GROUP + (row & 7)
        m = jnp.broadcast_to(order_ref[0:1, :], (width, LANES))
        for n in range(1, NB):
            m = jnp.where((row >> 7) == n, order_ref[n : n + 1, :], m)
        m = jnp.where(spot == (row & 127), m, 0).astype(F32)
        m = jnp.broadcast_to(jnp.sum(m, axis=1, keepdims=True), (width, LANES))
        across_lanes = m.T[0:1, :].astype(I32)
        m = m.astype(I32)
        column_orders[k] = m
        t = jnp.where(m < half_length, m.astype(F32) * inverse_length, 0.0)
        tr[k], ti[k] = turn_pair(t)

        spot = lax.broadcasted_iota(I32, (width, BLOCK), 1)
        m = jnp.concatenate([m & (BLOCK - 1)] * (BLOCK // LANES), axis=1)
        hot = (spot == m).astype(F32).astype(BF16)
        for half in range(2):
            table[k, half * width : (half + 1) * width] = jnp.dot(
                hot, base_ref[:, half * BLOCK : half * BLOCK + HALF], preferred_element_type=F32
            ).astype(BF16)
        spot = lax.broadcasted_iota(I32, (BLOCK, width), 0)
        hot = (spot == (across_lanes & (BLOCK - 1))).astype(F32).astype(BF16)
        turned[k, :EVEN] = jnp.dot(
            base_ref[:EVEN, :BLOCK], hot, preferred_element_type=F32
        ).astype(BF16)
        turned[k, EVEN:] = jnp.dot(
            base_ref[:HALF, BLOCK:], hot, preferred_element_type=F32
        ).astype(BF16)

    fixed_copy.wait()
    side = 2 * LANES
    for n in range(4):
        base_ref[:, side * n : side * (n + 1)] = grid[n, :BLOCK].astype(BF16)
    for n in range(2):
        pick_ref[:, side * n : side * (n + 1)] = grid[4 + n, :BLOCK].astype(BF16)
        turn_ref[side * n : side * (n + 1), :] = grid[4 + n, :BLOCK].T.astype(BF16)
    for s in range(XMAX // 2):
        grid[s] = jnp.zeros((EVEN + HALF, side), F32)

    def pack_legendre(k):
        for i in range(PAIRS):
            load_packed(legs, packed.at[i], GROUP * k + 2 * i, orders[k, i : i + 1, :] >> 7)

    def spread_group(k, d):
        group = pl.ds(pl.multiple_of(d * ROWS, 16), ROWS)
        blocks = []
        for t in range(NB):
            blocks.append(gathered[k, d, ROWS * t : ROWS * (t + 1), :].astype(F32))
            coeff[t, group, :] = blocks[t]
        extras = gathered[k, d, NB * ROWS :, :].astype(F32)
        coeff[NB, group, :] = recover(blocks, extras, orders[k], BF16)

    def legendre_sum(k):
        spread_group(k, across)
        for i in range(PAIRS):
            m = orders[k, i : i + 1, :]
            q = m >> 7
            spot = lax.broadcasted_iota(I32, (1, LANES), 1)
            weights = []
            for t in range(PB):
                block = coeff[t, pl.ds(i, ROWS, stride=PAIRS), :]
                if t < NB:
                    lead = jnp.where(spot + LANES * t >= m, block, 0.0)
                    other = jnp.where(q > t, block, 0.0)
                else:
                    lead, other = jnp.zeros_like(block), block
                weights.append(
                    jnp.concatenate([lead, other, jnp.zeros((32, LANES), F32)], axis=0).astype(BF16)
                )
            fourier = lax.dot_general(
                packed[i],
                jnp.concatenate(weights, axis=1),
                (((1,), (1,)), ((), ())),
                preferred_element_type=F32,
            ).astype(BF16)
            for lat in range(LATS):
                wide[WAVE * i : WAVE * (i + 1), LANES * lat : LANES * (lat + 1)] = fourier[
                    WAVE * lat : WAVE * (lat + 1)
                ]
        placed = jnp.dot(wide[...], turn_ref[...], preferred_element_type=F32)
        for c in range(2):
            for ab in range(2):
                for i in range(PAIRS):
                    at = 2 * c + ab
                    turn[pl.ds(c * 8 + 2 * i + ab, WAVE, stride=16), :] = placed[
                        WAVE * i : WAVE * (i + 1), LANES * at : LANES * (at + 1)
                    ]
        sent[k] = turn[...].reshape(WAVE, 16, LANES).astype(BF16)

    def grid_sum(k, last):
        keep = column_orders[k] < half_length
        one = tr[k], ti[k]
        two = times(one, one)
        four = times(two, two)
        eight = times(four, four)
        eleven = times(times(eight, two), one)
        x = arrived[k].astype(F32)
        x = jnp.concatenate(
            [x[:, :8].reshape(width, LANES), x[:, 8:].reshape(width, LANES)], axis=0
        ).astype(BF16)
        x = jnp.dot(
            jnp.concatenate([x, x], axis=1), mix_ref[...], preferred_element_type=F32
        )
        x0 = jnp.where(keep, x[:width], 0.0)
        x1 = jnp.where(keep, x[width:], 0.0)
        h = times((x0, x1), eleven)
        for s in range(XMAX // 2):
            for side in range(2):
                span = slice(LANES * side, LANES * (side + 1))
                waves[s, :width, span] = h[0].astype(BF16)
                waves[s, width:, span] = h[1].astype(BF16)
                h = back(h, one)
        for s in range(XMAX // 2):
            even = grid[s, :EVEN] + jnp.dot(
                turned[k, :EVEN], waves[s, :width], preferred_element_type=F32
            )
            odd = grid[s, EVEN:] + jnp.dot(
                turned[k, EVEN:], waves[s, width:], preferred_element_type=F32
            )
            if not last:
                grid[s, :EVEN] = even
                grid[s, EVEN:] = odd
                continue
            high = XMAX - 1 - 2 * s
            live = jnp.concatenate(
                [(high < count).astype(F32), (high - 1 < count).astype(F32)], axis=1
            )

            def column(values):
                mixed = values * float(M) ** (-0.5)
                return (mixed + gain * mixed * mixed) * live

            one = column(even[:HALF] + odd)
            two = column(even[:HALF] - odd)
            two = jnp.where(lax.broadcasted_iota(I32, two.shape, 0) == 0, 0.0, two)
            update[s, :HALF] = (one + two).astype(BF16)
            update[s, HALF:] = (one - two).astype(BF16)
            edge[s] = column(even[HALF : HALF + 8])

    own_right(1).start()
    own_left(1).start()
    pack(2)
    tables(0)

    def some_tables(k, carry):
        tables(k)
        return carry

    def gather_step(k, carry):
        @pl.when(k < CHUNKS)
        def _():
            own_right(k).wait_recv()
            pass_right(k).start()
            own_left(k).wait_recv()
            pass_left(k).start()

        @pl.when(k + 3 < CHUNKS)
        def _():
            pack(k + 3)
            lax.fori_loop(2 * k + 1, 2 * k + 3, some_tables, 0)

        @pl.when(k + 2 < CHUNKS)
        def _():
            own_right(k + 2).start()
            own_left(k + 2).start()

        @pl.when((k >= 1) & (k <= CHUNKS))
        def _():
            leg_copy(k - 1).wait()
            pack_legendre(k - 1)
            for d in (g, left, right):
                spread_group(k - 1, d)
            pass_right(k - 1).wait_recv()
            pass_left(k - 1).wait_recv()
            legendre_sum(k - 1)

        @pl.when(k == 2)
        def _():
            exchange(0, 2, sent, arrived, a_send, a_recv)

        @pl.when(k >= 3)
        def _():
            exchange(k - 1, 1, sent, arrived, a_send, a_recv)

        @pl.when(k == 3)
        def _():
            exchange_all(0, 2, sent, arrived, a_send, a_recv).wait_recv()

        @pl.when(k == 4)
        def _():
            grid_sum(0, False)

        return carry

    lax.fori_loop(0, CHUNKS + 1, gather_step, 0)

    def late_sum(k, carry):
        @pl.when(k >= 2)
        def _():
            exchange_all(k, 1, sent, arrived, a_send, a_recv).wait_recv()

        grid_sum(k, False)
        return carry

    lax.fori_loop(1, CHUNKS - 1, late_sum, 0)
    exchange_all(CHUNKS - 1, 1, sent, arrived, a_send, a_recv).wait_recv()
    grid_sum(CHUNKS - 1, True)

    def grid_back(k):
        t = tr[k], ti[k]
        d = jnp.zeros((width, LANES), F32), jnp.zeros((width, LANES), F32)
        sign = 1.0 - 2.0 * (column_orders[k] & 1).astype(F32)
        for s in range(XMAX // 2):
            even = jnp.dot(table[k, :width], update[s, :HALF], preferred_element_type=F32)
            odd = jnp.dot(table[k, width:], update[s, HALF:], preferred_element_type=F32)
            for side in range(2):
                span = slice(LANES * side, LANES * (side + 1))
                if s + side > 0:
                    d = back(d, t)
                d = d[0] + (even[:, span] + sign * edge[s, 0:1, span]), d[1] + odd[:, span]
        keep = column_orders[k] < half_length
        d0 = jnp.where(keep, d[0] * scale, 0.0).reshape(WAVE, 8, LANES)
        d1 = jnp.where(keep, d[1] * scale, 0.0).reshape(WAVE, 8, LANES)
        sent_back[k] = jnp.concatenate([d0, d1], axis=1).astype(BF16)

    def legendre_back(k):
        turn[...] = arrived_back[k].reshape(WAVE * 16, LANES).astype(F32)
        for c in range(2):
            for ab in range(2):
                for i in range(PAIRS):
                    at = 2 * c + ab
                    wide[WAVE * i : WAVE * (i + 1), LANES * at : LANES * (at + 1)] = turn[
                        pl.ds(c * 8 + 2 * i + ab, WAVE, stride=16), :
                    ].astype(BF16)
        spread = jnp.dot(wide[...], pick_ref[...], preferred_element_type=F32)
        for i in range(PAIRS):
            q = orders[k, i : i + 1, :] >> 7
            values = jnp.concatenate(
                [
                    spread[WAVE * i : WAVE * (i + 1), LANES * lat : LANES * (lat + 1)]
                    for lat in range(LATS)
                ],
                axis=0,
            )
            values = values.T.astype(BF16)
            result = jnp.dot(values[: 2 * ROWS], packed[i], preferred_element_type=F32)
            for t in range(PB):
                span = slice(LANES * t, LANES * (t + 1))
                if t < NB:
                    block = jnp.where(q <= t, result[:ROWS, span], result[ROWS:, span])
                else:
                    block = result[ROWS:, span]
                coeff[t, pl.ds(i, ROWS, stride=PAIRS), :] = block
        m = orders[k]
        q, s = m >> 7, m & (LANES - 1)
        flipped[...] = reverse(coeff[NB].astype(BF16))
        own_rows = lambda d: pl.ds(pl.multiple_of(d * ROWS, 16), ROWS)
        places = (
            (opposite, across, BF16), (part_right, right, F32), (part_left, left, F32), (part_own, g, F32)
        )
        for place, d, kind in places:
            for t in range(NB):
                shared = (q == t) & (lane < s)
                block = jnp.where(shared, flipped[own_rows(d), :], coeff[t, own_rows(d), :])
                place[k, ROWS * t : ROWS * (t + 1), :] = block.astype(kind)
            place[k, NB * ROWS :, :] = fold(coeff[NB, own_rows(d), :], s).astype(kind)
            if place is opposite:
                sum_first_right(k).start()
                sum_first_left(k).start()

    def sum_second(k):
        cut = LEFT_PART
        to_right[k, :cut] = (part_right[k, :cut] + first_left[k].astype(F32)).astype(BF16)
        to_right[k, cut:] = part_right[k, cut:].astype(BF16)
        sum_second_right(k).start()
        sum_first_left(k).wait_recv()
        to_left[k, :cut] = part_left[k, :cut].astype(BF16)
        to_left[k, cut:] = (part_left[k, cut:] + first_right[k].astype(F32)).astype(BF16)
        sum_second_left(k).start()

    def unpack(k):
        m = orders[k]
        q = m >> 7
        whole = lambda at: (
            part_own[k, at, :] + second_left[k, at, :].astype(F32) + second_right[k, at, :].astype(F32)
        )
        total = [whole(slice(ROWS * t, ROWS * (t + 1))) for t in range(NB)]
        total.append(recover(total, whole(slice(NB * ROWS, SENT)), m, F32))
        for t in range(NB):
            n = lane + LANES * t
            other = jnp.where(NB - 1 - t == q, total[NB], total[NB - 1 - t])
            both = jnp.where(n >= m, total[t], 0.0), jnp.where(n >= M - 1 - m, other, 0.0)
            count = FD * PAIRS
            for ab in range(2):
                for c in range(2):
                    rows[t, pl.ds(2 * ab + c, count, stride=4), :] = both[ab][count * c : count * (c + 1)]
        for f in range(FD):
            for r in range(GROUP):
                at = 2 * (f * GROUP + r)
                results[k, f, r] = jnp.concatenate(
                    [rows[t, at : at + 2, :] for t in range(NB)], axis=1
                )

    def back_step(k):
        grid_back(k)
        exchange(k, 1, sent_back, arrived_back, b_send, b_recv)

    def ahead(k, carry):
        back_step(k)
        return carry

    lax.fori_loop(0, 3, ahead, 0)

    def scatter_step(k, carry):
        @pl.when(k < CHUNKS)
        def _():
            pack_legendre(k)
            exchange_all(k, 1, sent_back, arrived_back, b_send, b_recv).wait_recv()
            legendre_back(k)

        @pl.when((k >= 1) & (k <= CHUNKS))
        def _():
            sum_first_right(k - 1).wait_recv()
            sum_second(k - 1)

        @pl.when((k >= 1) & (k + 2 < CHUNKS))
        def _():
            back_step(k + 2)

        @pl.when(k >= 4)
        def _():
            sum_second_right(k - 4).wait_recv()
            sum_second_left(k - 4).wait_recv()
            unpack(k - 4)
            out_copy(k - 4).start()

        return carry

    lax.fori_loop(0, CHUNKS + 4, scatter_step, 0)

    def finish(k, carry):
        for copy in (own_right, own_left, pass_right, pass_left):
            copy(k).wait_send()
        for copy in (sum_first_right, sum_first_left, sum_second_right, sum_second_left):
            copy(k).wait_send()
        exchange_all(k, 1, sent_back, arrived_back, b_send, b_recv).wait_send()
        out_copy(k).wait()
        return carry

    lax.fori_loop(0, CHUNKS, finish, 0)
    for k, count in ((0, 2), (2, 1), (3, 1), (4, 1)):
        exchange_all(k, count, sent, arrived, a_send, a_recv).wait_send()


PIECES = 5


def hand_over(src_ref, dst_ref, held, sem_in, sem_out):
    count = src_ref.shape[1] // PIECES
    spans = [pl.ds(n * count, count) for n in range(PIECES)]
    reads = [
        pltpu.make_async_copy(src_ref.at[:, at], held.at[:, at], sem_in.at[n])
        for n, at in enumerate(spans)
    ]
    writes = [
        pltpu.make_async_copy(held.at[:, at], dst_ref.at[:, at], sem_out.at[n])
        for n, at in enumerate(spans)
    ]
    for read in reads:
        read.start()
    for read, write in zip(reads, writes):
        read.wait()
        write.start()
    for write in writes:
        write.wait()


VMEM = pl.BlockSpec(memory_space=pltpu.VMEM)
SMEM = pl.BlockSpec(memory_space=pltpu.SMEM)
ANY = pl.BlockSpec(memory_space=pl.ANY)


def local(spec_in, legendre, wave_order, row_length, quad_weight, mixing, square_gain):
    fixed = np.concatenate([wave_tables(), lane_maps()], axis=1)
    fixed = fixed.reshape(BLOCK, XMAX // 2, 2 * LANES).transpose(1, 0, 2)
    width = WAVE * GROUP
    message = pltpu.VMEM((CHUNKS, WAVE, 16, LANES), BF16)
    full = pltpu.VMEM((CHUNKS, SENT, LANES), F32)
    short = pltpu.VMEM((CHUNKS, SENT, LANES), BF16)
    turns = pltpu.VMEM((CHUNKS, width, LANES), F32)
    places = pltpu.VMEM((LATS * LANES, LATS * LANES), BF16)
    copies = pltpu.SemaphoreType.DMA((4, CHUNKS))
    each = pltpu.SemaphoreType.DMA((CHUNKS,))
    result = pl.pallas_call(
        kernel,
        out_shape=jax.ShapeDtypeStruct((FD, GROUP * CHUNKS, 2, M), F32),
        in_specs=[ANY] * 3 + [SMEM] * 4 + [VMEM] * 2,
        out_specs=ANY,
        scratch_shapes=[
            pltpu.VMEM((GROUP * CHUNKS, FLD * WAVE, M), BF16),
            pltpu.VMEM((BLOCK, 2 * BLOCK), BF16),
            places,
            places,
            pltpu.VMEM((CHUNKS, FD, GROUP, 2, M), BF16),
            pltpu.VMEM((NB, 2 * ROWS, LANES), F32),
            pltpu.VMEM((CHUNKS, ROWS, LANES), I32),
            pltpu.VMEM((2 * LANES, LANES), BF16),
            pltpu.VMEM((CHUNKS, width, LANES), I32),
            pltpu.VMEM((CHUNKS, FLD, SENT, LANES), BF16),
            pltpu.VMEM((PB, FLD * ROWS, LANES), F32),
            pltpu.VMEM((FLD * ROWS, LANES), F32),
            pltpu.VMEM((PAIRS, LANES, PACKED), BF16),
            pltpu.VMEM((PAIRS * WAVE, LATS * LANES), BF16),
            pltpu.VMEM((WAVE * 16, LANES), F32),
            message,
            message,
            pltpu.VMEM((CHUNKS, 2 * width, HALF), BF16),
            pltpu.VMEM((CHUNKS, EVEN + HALF, width), BF16),
            pltpu.VMEM((XMAX // 2, 2 * width, 2 * LANES), BF16),
            pltpu.VMEM((XMAX // 2, EVEN + HALF, 2 * LANES), F32),
            pltpu.VMEM((XMAX // 2, BLOCK, 2 * LANES), BF16),
            pltpu.VMEM((XMAX // 2, 8, 2 * LANES), F32),
            turns,
            turns,
            message,
            message,
            short,
            full,
            full,
            full,
            short,
            short,
            pltpu.VMEM((CHUNKS, LEFT_PART, LANES), BF16),
            pltpu.VMEM((CHUNKS, SENT - LEFT_PART, LANES), BF16),
            short,
            short,
            pltpu.VMEM((CHUNKS, FD, GROUP, 2, M), F32),
            each,
            each,
            pltpu.SemaphoreType.DMA,
            each,
            copies,
            copies,
            each,
            each,
            each,
            each,
            copies,
            copies,
        ],
        compiler_params=pltpu.CompilerParams(
            collective_id=0, has_side_effects=True, vmem_limit_bytes=60 << 20
        ),
    )(
        spec_in, legendre, jnp.asarray(fixed),
        wave_order, row_length, quad_weight, square_gain,
        wave_order.reshape(NB, LANES), mixing,
    )
    return pl.pallas_call(
        hand_over,
        out_shape=jax.ShapeDtypeStruct(result.shape, F32),
        in_specs=[ANY],
        out_specs=ANY,
        scratch_shapes=[
            pltpu.VMEM(result.shape, F32),
            pltpu.SemaphoreType.DMA((PIECES,)),
            pltpu.SemaphoreType.DMA((PIECES,)),
        ],
        compiler_params=pltpu.CompilerParams(vmem_limit_bytes=60 << 20),
    )(result)

def solution(mesh):
    in_specs = (P("fld", "wave", None, None), P("wave", "fld", None), P(), P(), P(), P(), P())
    out_specs = P("fld", "wave", None, None)
    return jax.shard_map(local, mesh=mesh, in_specs=in_specs, out_specs=out_specs, check_vma=False)
```

```python
import functools
import math

import jax
import jax.numpy as jnp
import numpy as np
from jax import lax
from jax.experimental import pallas as pl
from jax.experimental.pallas import tpu as pltpu
from jax.sharding import PartitionSpec as P

M = 1280
FL = 24
BLOCK = 512
LANES = 128
NB = M // LANES
PB = NB + 1
PACKED = PB * LANES
CHUNKS = 5
PAIRS = 4
WAVE = 32
FLD = 4
LATS = 4
FD = FL // FLD
ROWS = 2 * FD * PAIRS
HALF = BLOCK // 2
EVEN = HALF + 16
XMAX = 12
F32, BF16, I32 = jnp.float32, jnp.bfloat16, jnp.int32


def wave_tables():
    v = np.arange(BLOCK)
    angle = (v[:, None] * v[None, :] % BLOCK) * (2.0 * math.pi / BLOCK)
    return np.concatenate([np.cos(angle), -np.sin(angle)], axis=1).astype(np.float32)


def lane_maps():
    width = LATS * LANES
    lat_a, ab_a, level_a, half_a = (np.full(width, -1) for _ in range(4))
    for lat in range(LATS):
        for ab in range(2):
            for g in range(FLD):
                for c in range(2):
                    for f in range(FD):
                        at = LANES * lat + ((ab * FLD + g) * 2 + c) * FD + f
                        lat_a[at], ab_a[at], half_a[at], level_a[at] = lat, ab, c, FD * g + f
    lat_b, ab_b, level_b, half_b = (np.full(width, -2) for _ in range(4))
    for c in range(2):
        for ab in range(2):
            for lat in range(LATS):
                for f in range(FL):
                    at = LANES * (2 * c + ab) + FL * lat + f
                    lat_b[at], ab_b[at], half_b[at], level_b[at] = lat, ab, c, f
    same = (
        (lat_a[:, None] == lat_b[None, :])
        & (ab_a[:, None] == ab_b[None, :])
        & (half_a[:, None] == half_b[None, :])
    )
    pick = same & (level_a[:, None] == level_b[None, :])
    return pick.T.astype(np.float32)


def turn_pair(t):
    a = (t - 0.25) * (2.0 * math.pi)
    s = a * a
    sine = a * (
        1.0
        + s
        * (
            -1.0 / 6
            + s * (1.0 / 120 + s * (-1.0 / 5040 + s * (1.0 / 362880 - s * (1.0 / 39916800))))
        )
    )
    cosine = 1.0 + s * (
        -0.5
        + s
        * (
            1.0 / 24
            + s * (-1.0 / 720 + s * (1.0 / 40320 + s * (-1.0 / 3628800 + s * (1.0 / 479001600))))
        )
    )
    return -sine, cosine


def times(a, b):
    return a[0] * b[0] - a[1] * b[1], a[0] * b[1] + a[1] * b[0]


def back(a, b):
    return a[0] * b[0] + a[1] * b[1], a[1] * b[0] - a[0] * b[1]


SENT = NB * ROWS + 16
LEFT_PART = SENT // 32 * 16
GROUP = 8
MESH = pl.DeviceIdType.MESH
OTHERS = sorted(
    ((dz, dx, dc) for dz in range(4) for dx in range(4) for dc in range(2) if dz + dx + dc > 0),
    key=lambda d: -(min(d[0], 4 - d[0]) + min(d[1], 4 - d[1])),
)


def load_packed(leg_ref, packed_ref, first, q):
    q = jnp.broadcast_to(q.astype(F32), (LANES, LANES)).astype(BF16)
    spare = None
    for t in range(NB):
        one = leg_ref[first, :, LANES * t : LANES * (t + 1)]
        at = NB - 1 - t
        two = leg_ref[first + 1, :, LANES * at : LANES * (at + 1)]
        packed_ref[:, LANES * t : LANES * (t + 1)] = jnp.where(q <= t, one, two)
        spare = two if t == 0 else jnp.where(q == t, two, spare)
    packed_ref[:, LANES * NB :] = spare


def kernel(
    spec_ref, leg_ref, fixed_ref, own_ref, lengths_ref, weights_ref, gains_ref,
    order_ref, mixing_ref, out_ref,
    legs, base_ref, pick_ref, turn_ref, spec, rows, orders, mix_ref, column_orders,
    gathered, coeff, flipped, packed, wide, turn, sent, arrived, table, turned, waves, grid, update, edge,
    tr, ti, sent_back, arrived_back, opposite, part_right, part_left, part_own, to_right, to_left,
    first_left, first_right, second_left, second_right, results,
    leg_sem, spec_sem, const_sem, out_sem, ag_send, ag_recv, a_send, a_recv, b_send, b_recv,
    rs_send, rs_recv,
):
    w = lax.axis_index("wave")
    g = lax.axis_index("fld")
    right, left, across = lax.rem(g + 1, FLD), lax.rem(g + 3, FLD), lax.rem(g + 2, FLD)

    def spec_copy(k):
        return pltpu.make_async_copy(
            spec_ref.at[:, pl.ds(k * GROUP, GROUP)], spec.at[k], spec_sem.at[k]
        )

    def out_copy(k):
        return pltpu.make_async_copy(
            results.at[k], out_ref.at[:, pl.ds(k * GROUP, GROUP)], out_sem.at[k]
        )

    fixed_copy = pltpu.make_async_copy(fixed_ref, grid.at[:, pl.ds(0, BLOCK)], const_sem)

    def leg_copy(k):
        rows = pl.ds(k * GROUP, GROUP)
        return pltpu.make_async_copy(leg_ref.at[rows], legs.at[rows], leg_sem.at[k])

    def remote(src, dst, send, recv, to):
        return pltpu.make_async_remote_copy(
            src_ref=src, dst_ref=dst, send_sem=send, recv_sem=recv, device_id=to, device_id_type=MESH
        )

    to_r, to_l = (w, right), (w, left)
    head, rest = pl.ds(0, LEFT_PART), pl.ds(LEFT_PART, SENT - LEFT_PART)

    def own_right(k):
        block = gathered.at[k, g]
        return remote(block, block, ag_send.at[0, k], ag_recv.at[0, k], to_r)

    def own_left(k):
        block = gathered.at[k, g]
        return remote(block, block, ag_send.at[1, k], ag_recv.at[1, k], to_l)

    def pass_right(k):
        block = gathered.at[k, left, head]
        return remote(block, block, ag_send.at[2, k], ag_recv.at[2, k], to_r)

    def pass_left(k):
        block = gathered.at[k, right, rest]
        return remote(block, block, ag_send.at[3, k], ag_recv.at[3, k], to_l)

    def sum_first_right(k):
        return remote(
            opposite.at[k, head], first_left.at[k], rs_send.at[0, k], rs_recv.at[0, k], to_r
        )

    def sum_first_left(k):
        return remote(
            opposite.at[k, rest], first_right.at[k], rs_send.at[1, k], rs_recv.at[1, k], to_l
        )

    def sum_second_right(k):
        return remote(to_right.at[k], second_left.at[k], rs_send.at[2, k], rs_recv.at[2, k], to_r)

    def sum_second_left(k):
        return remote(to_left.at[k], second_right.at[k], rs_send.at[3, k], rs_recv.at[3, k], to_l)

    def exchange_all(k, count, src, dst, send, recv):
        some, others = pl.ds(k, count), pl.ds(0, WAVE - 1)
        return remote(src.at[some, others], dst.at[some, others], send.at[k], recv.at[k], (w, g))

    z, x, core = w // 8, lax.rem(w // 2, 4), lax.rem(w, 2)

    def exchange(k, count, src, dst, send, recv):
        some = pl.ds(k, count)
        for dz, dx, dc in OTHERS:
            to = lax.rem(z + dz, 4) * 8 + lax.rem(x + dx, 4) * 2 + lax.rem(core + dc, 2)
            remote(src.at[some, to], dst.at[some, w], send.at[k], recv.at[k], (to, g)).start()
        for n in range(count):
            dst[k + n, w] = src[k + n, w]

    for k in range(CHUNKS):
        spec_copy(k).start()
    fixed_copy.start()
    for k in range(CHUNKS):
        leg_copy(k).start()
    barrier = pltpu.get_barrier_semaphore()

    def greet(d, carry):
        pl.semaphore_signal(
            barrier, inc=1, device_id=(lax.rem(w + d, WAVE), g), device_id_type=MESH
        )
        return carry

    for to in (to_r, to_l):
        pl.semaphore_signal(barrier, inc=1, device_id=to, device_id_type=MESH)
    lax.fori_loop(1, WAVE, greet, 0)

    lane = lax.broadcasted_iota(I32, (ROWS, LANES), 1)
    pair_of_row = lax.broadcasted_iota(I32, (ROWS, LANES), 0) & (PAIRS - 1)

    def reverse(values):
        places = [lax.broadcasted_iota(I32, (LANES, LANES), dim) for dim in range(2)]
        flip = (places[0] + places[1] == LANES - 1).astype(F32)
        if values.dtype == BF16:
            return jnp.dot(values, flip.astype(BF16), preferred_element_type=F32)
        return jnp.dot(
            values, flip, precision=lax.Precision.HIGHEST, preferred_element_type=F32
        )

    def fold(spare, s):
        value = jnp.sum(jnp.where(lane == LANES - 1 - s, spare, 0.0), axis=1, keepdims=True)
        value = jnp.broadcast_to(value, (ROWS, LANES))
        spot = lane[:16]
        out = jnp.zeros((16, LANES), F32)
        for n in range(ROWS // 16):
            out = jnp.where(spot == n, value[16 * n : 16 * (n + 1)], out)
        return out

    def unfold(extras):
        spot = lane[:16]
        return jnp.concatenate(
            [
                jnp.broadcast_to(
                    jnp.sum(jnp.where(spot == n, extras, 0.0), axis=1, keepdims=True), (16, LANES)
                )
                for n in range(ROWS // 16)
            ],
            axis=0,
        )

    def recover(blocks, extras, m, kind):
        q, s = m >> 7, m & (LANES - 1)
        shared = blocks[0]
        for t in range(1, NB):
            shared = jnp.where(q == t, blocks[t], shared)
        back_again = reverse(shared.astype(kind))
        spot = LANES - 1 - s
        return jnp.where(lane > spot, back_again, jnp.where(lane == spot, unfold(extras), 0.0))

    def pack(k):
        first_row = (w * CHUNKS + k) * GROUP
        m = jnp.full((ROWS, LANES), own_ref[first_row], I32)
        for i in range(1, PAIRS):
            m = jnp.where(pair_of_row == i, own_ref[first_row + 2 * i], m)
        orders[k] = m
        q = m >> 7
        spec_copy(k).wait()
        for f in range(FD):
            for r in range(GROUP):
                values = spec[k, f, r].astype(F32)
                at = 2 * (f * GROUP + r)
                for t in range(NB):
                    rows[t, at : at + 2, :] = values[:, LANES * t : LANES * (t + 1)]
        first, second = [], []
        for t in range(NB):
            n = lane + LANES * t
            half = [
                jnp.concatenate(
                    [rows[t, pl.ds(2 * ab + c, FD * PAIRS, stride=4), :] for c in range(2)], axis=0
                )
                for ab in range(2)
            ]
            first.append(jnp.where(n >= m, half[0], 0.0))
            second.append(jnp.where(n >= M - 1 - m, half[1], 0.0))
        s = m & (LANES - 1)
        spare = second[NB - 1]
        for t in range(1, NB):
            spare = jnp.where(q == t, second[NB - 1 - t], spare)
        turned_round = reverse(spare.astype(BF16))
        for t in range(NB):
            shared = jnp.where(lane >= s, first[t], turned_round)
            block = jnp.where(q < t, first[t], jnp.where(q == t, shared, second[NB - 1 - t]))
            gathered[k, g, ROWS * t : ROWS * (t + 1), :] = block.astype(BF16)
        gathered[k, g, NB * ROWS :, :] = fold(spare, s).astype(BF16)

    def first_pack(k, carry):
        pack(k)

        @pl.when(k == 0)
        def _():
            pl.semaphore_wait(barrier, WAVE + 1)
            own_right(0).start()
            own_left(0).start()

        return carry

    lax.fori_loop(0, 2, first_pack, 0)

    spot = lax.broadcasted_iota(I32, (1, LANES), 1)
    lat_of = lambda x: sum((x >= FL * n).astype(I32) for n in range(1, LATS))
    level_of = lambda x: x - FL * lat_of(x)
    length, weight = jnp.zeros((1, LANES), I32), jnp.zeros((1, LANES), F32)
    for lat in range(LATS):
        at = (g * LATS + lat) * WAVE + w
        length = jnp.where(spot >= FL * lat, lengths_ref[at], length)
        weight = jnp.where(spot >= FL * lat, weights_ref[at], weight)
    gain = jnp.zeros((1, LANES), F32)
    for f in range(FL):
        gain = jnp.where(level_of(spot) == f, gains_ref[f], gain)
    gain = jnp.concatenate([gain, gain], axis=1)
    real_length = length.astype(F32)
    root = lax.rsqrt(real_length)
    scale = weight * (root * (1.5 - 0.5 * real_length * root * root))
    half_length = length >> 1
    inverse_length = 1.0 / real_length
    count = length >> 9

    spot = lax.broadcasted_iota(I32, (FL, LANES), 1)
    level = lax.broadcasted_iota(I32, (FL, LANES), 0)
    hot = ((level_of(spot) == level) & (spot < LATS * FL)).astype(F32)
    across_levels = (((0,), (0,)), ((), ()))
    spread = lax.dot_general(
        mixing_ref[...], hot, across_levels, precision=lax.Precision.HIGHEST,
        preferred_element_type=F32,
    )
    spread = lax.dot_general(
        hot, spread, across_levels, precision=lax.Precision.HIGHEST, preferred_element_type=F32
    )
    lats = [lat_of(lax.broadcasted_iota(I32, (LANES, LANES), dim)) for dim in range(2)]
    spread = jnp.where(lats[0] == lats[1], spread, 0.0)
    high_part = spread.astype(BF16)
    mix_ref[:LANES] = high_part
    mix_ref[LANES:] = (spread - high_part.astype(F32)).astype(BF16)

    width = WAVE * GROUP

    def tables(k):
        spot = lax.broadcasted_iota(I32, (width, LANES), 1)
        row = lax.broadcasted_iota(I32, (width, LANES), 0)
        row = (row >> 3) * (CHUNKS * GROUP) + k * GROUP + (row & 7)
        m = jnp.broadcast_to(order_ref[0:1, :], (width, LANES))
        for n in range(1, NB):
            m = jnp.where((row >> 7) == n, order_ref[n : n + 1, :], m)
        m = jnp.where(spot == (row & 127), m, 0).astype(F32)
        m = jnp.broadcast_to(jnp.sum(m, axis=1, keepdims=True), (width, LANES))
        across_lanes = m.T[0:1, :].astype(I32)
        m = m.astype(I32)
        column_orders[k] = m
        t = jnp.where(m < half_length, m.astype(F32) * inverse_length, 0.0)
        tr[k], ti[k] = turn_pair(t)

        spot = lax.broadcasted_iota(I32, (width, BLOCK), 1)
        m = jnp.concatenate([m & (BLOCK - 1)] * (BLOCK // LANES), axis=1)
        hot = (spot == m).astype(F32).astype(BF16)
        for half in range(2):
            table[k, half * width : (half + 1) * width] = jnp.dot(
                hot, base_ref[:, half * BLOCK : half * BLOCK + HALF], preferred_element_type=F32
            ).astype(BF16)
        spot = lax.broadcasted_iota(I32, (BLOCK, width), 0)
        hot = (spot == (across_lanes & (BLOCK - 1))).astype(F32).astype(BF16)
        turned[k, :EVEN] = jnp.dot(
            base_ref[:EVEN, :BLOCK], hot, preferred_element_type=F32
        ).astype(BF16)
        turned[k, EVEN:] = jnp.dot(
            base_ref[:HALF, BLOCK:], hot, preferred_element_type=F32
        ).astype(BF16)

    waves[0, :, :LANES] = jnp.zeros((2 * width, LANES), BF16)
    fixed_copy.wait()
    side = 2 * LANES
    for n in range(4):
        base_ref[:, side * n : side * (n + 1)] = grid[n, :BLOCK].astype(BF16)
    for n in range(2):
        pick_ref[:, side * n : side * (n + 1)] = grid[4 + n, :BLOCK].astype(BF16)
        turn_ref[side * n : side * (n + 1), :] = grid[4 + n, :BLOCK].T.astype(BF16)
    for s in range(XMAX // 2):
        grid[s] = jnp.zeros((EVEN + HALF, side), F32)

    def pack_legendre(k):
        for i in range(PAIRS):
            load_packed(legs, packed.at[i], GROUP * k + 2 * i, orders[k, i : i + 1, :] >> 7)

    def spread_group(k, d):
        group = pl.ds(pl.multiple_of(d * ROWS, 16), ROWS)
        blocks = []
        for t in range(NB):
            blocks.append(gathered[k, d, ROWS * t : ROWS * (t + 1), :].astype(F32))
            coeff[t, group, :] = blocks[t]
        extras = gathered[k, d, NB * ROWS :, :].astype(F32)
        coeff[NB, group, :] = recover(blocks, extras, orders[k], BF16)

    def legendre_sum(k):
        spread_group(k, across)
        for i in range(PAIRS):
            m = orders[k, i : i + 1, :]
            q = m >> 7
            spot = lax.broadcasted_iota(I32, (1, LANES), 1)
            weights = []
            for t in range(PB):
                block = coeff[t, pl.ds(i, ROWS, stride=PAIRS), :]
                if t < NB:
                    lead = jnp.where(spot + LANES * t >= m, block, 0.0)
                    other = jnp.where(q > t, block, 0.0)
                else:
                    lead, other = jnp.zeros_like(block), block
                weights.append(
                    jnp.concatenate([lead, other, jnp.zeros((32, LANES), F32)], axis=0).astype(BF16)
                )
            fourier = lax.dot_general(
                packed[i],
                jnp.concatenate(weights, axis=1),
                (((1,), (1,)), ((), ())),
                preferred_element_type=F32,
            ).astype(BF16)
            for lat in range(LATS):
                wide[WAVE * i : WAVE * (i + 1), LANES * lat : LANES * (lat + 1)] = fourier[
                    WAVE * lat : WAVE * (lat + 1)
                ]
        placed = jnp.dot(wide[...], turn_ref[...], preferred_element_type=F32)
        for c in range(2):
            for ab in range(2):
                for i in range(PAIRS):
                    at = 2 * c + ab
                    turn[pl.ds(c * 8 + 2 * i + ab, WAVE, stride=16), :] = placed[
                        WAVE * i : WAVE * (i + 1), LANES * at : LANES * (at + 1)
                    ]
        sent[k] = turn[...].reshape(WAVE, 16, LANES).astype(BF16)

    def grid_sum(k, last):
        keep = column_orders[k] < half_length
        one = tr[k], ti[k]
        two = times(one, one)
        four = times(two, two)
        eight = times(four, four)
        ten = times(eight, two)
        x = arrived[k].astype(F32)
        x = jnp.concatenate(
            [x[:, :8].reshape(width, LANES), x[:, 8:].reshape(width, LANES)], axis=0
        ).astype(BF16)
        x = jnp.dot(
            jnp.concatenate([x, x], axis=1), mix_ref[...], preferred_element_type=F32
        )
        x0 = jnp.where(keep, x[:width], 0.0)
        x1 = jnp.where(keep, x[width:], 0.0)
        h = times((x0, x1), ten)
        for s in range(XMAX // 2):
            for side in range(0 if s else 1, 2):
                span = slice(LANES * side, LANES * (side + 1))
                waves[s, :width, span] = h[0].astype(BF16)
                waves[s, width:, span] = h[1].astype(BF16)
                h = back(h, one)
        for s in range(XMAX // 2):
            even = grid[s, :EVEN] + jnp.dot(
                turned[k, :EVEN], waves[s, :width], preferred_element_type=F32
            )
            odd = grid[s, EVEN:] + jnp.dot(
                turned[k, EVEN:], waves[s, width:], preferred_element_type=F32
            )
            if not last:
                grid[s, :EVEN] = even
                grid[s, EVEN:] = odd
                continue
            high = XMAX - 1 - 2 * s
            live = jnp.concatenate(
                [(high < count).astype(F32), (high - 1 < count).astype(F32)], axis=1
            )

            def column(values):
                mixed = values * float(M) ** (-0.5)
                return (mixed + gain * mixed * mixed) * live

            one = column(even[:HALF] + odd)
            two = column(even[:HALF] - odd)
            two = jnp.where(lax.broadcasted_iota(I32, two.shape, 0) == 0, 0.0, two)
            update[s, :HALF] = (one + two).astype(BF16)
            update[s, HALF:] = (one - two).astype(BF16)
            edge[s] = column(even[HALF : HALF + 8])

    own_right(1).start()
    own_left(1).start()
    pack(2)
    tables(0)

    def some_tables(k, carry):
        tables(k)
        return carry

    def gather_step(k, carry):
        @pl.when(k < CHUNKS)
        def _():
            own_right(k).wait_recv()
            pass_right(k).start()
            own_left(k).wait_recv()
            pass_left(k).start()

        @pl.when(k + 3 < CHUNKS)
        def _():
            pack(k + 3)
            lax.fori_loop(2 * k + 1, 2 * k + 3, some_tables, 0)

        @pl.when(k + 2 < CHUNKS)
        def _():
            own_right(k + 2).start()
            own_left(k + 2).start()

        @pl.when((k >= 1) & (k <= CHUNKS))
        def _():
            leg_copy(k - 1).wait()
            pack_legendre(k - 1)
            for d in (g, left, right):
                spread_group(k - 1, d)
            pass_right(k - 1).wait_recv()
            pass_left(k - 1).wait_recv()
            legendre_sum(k - 1)

        @pl.when(k == 2)
        def _():
            exchange(0, 2, sent, arrived, a_send, a_recv)

        @pl.when(k >= 3)
        def _():
            exchange(k - 1, 1, sent, arrived, a_send, a_recv)

        @pl.when(k == 3)
        def _():
            exchange_all(0, 2, sent, arrived, a_send, a_recv).wait_recv()

        @pl.when(k == 4)
        def _():
            grid_sum(0, False)

        return carry

    lax.fori_loop(0, CHUNKS + 1, gather_step, 0)

    def late_sum(k, carry):
        @pl.when(k >= 2)
        def _():
            exchange_all(k, 1, sent, arrived, a_send, a_recv).wait_recv()

        grid_sum(k, False)
        return carry

    lax.fori_loop(1, CHUNKS - 1, late_sum, 0)
    exchange_all(CHUNKS - 1, 1, sent, arrived, a_send, a_recv).wait_recv()
    grid_sum(CHUNKS - 1, True)

    def grid_back(k):
        t = tr[k], ti[k]
        d = jnp.zeros((width, LANES), F32), jnp.zeros((width, LANES), F32)
        sign = 1.0 - 2.0 * (column_orders[k] & 1).astype(F32)
        for s in range(XMAX // 2):
            even = jnp.dot(table[k, :width], update[s, :HALF], preferred_element_type=F32)
            odd = jnp.dot(table[k, width:], update[s, HALF:], preferred_element_type=F32)
            for side in range(0 if s else 1, 2):
                span = slice(LANES * side, LANES * (side + 1))
                if s > 0:
                    d = back(d, t)
                d = d[0] + (even[:, span] + sign * edge[s, 0:1, span]), d[1] + odd[:, span]
        keep = column_orders[k] < half_length
        d0 = jnp.where(keep, d[0] * scale, 0.0).reshape(WAVE, 8, LANES)
        d1 = jnp.where(keep, d[1] * scale, 0.0).reshape(WAVE, 8, LANES)
        sent_back[k] = jnp.concatenate([d0, d1], axis=1).astype(BF16)

    def legendre_back(k):
        turn[...] = arrived_back[k].reshape(WAVE * 16, LANES).astype(F32)
        for c in range(2):
            for ab in range(2):
                for i in range(PAIRS):
                    at = 2 * c + ab
                    wide[WAVE * i : WAVE * (i + 1), LANES * at : LANES * (at + 1)] = turn[
                        pl.ds(c * 8 + 2 * i + ab, WAVE, stride=16), :
                    ].astype(BF16)
        spread = jnp.dot(wide[...], pick_ref[...], preferred_element_type=F32)
        for i in range(PAIRS):
            q = orders[k, i : i + 1, :] >> 7
            values = jnp.concatenate(
                [
                    spread[WAVE * i : WAVE * (i + 1), LANES * lat : LANES * (lat + 1)]
                    for lat in range(LATS)
                ],
                axis=0,
            )
            values = values.T.astype(BF16)
            result = jnp.dot(values[: 2 * ROWS], packed[i], preferred_element_type=F32)
            for t in range(PB):
                span = slice(LANES * t, LANES * (t + 1))
                if t < NB:
                    block = jnp.where(q <= t, result[:ROWS, span], result[ROWS:, span])
                else:
                    block = result[ROWS:, span]
                coeff[t, pl.ds(i, ROWS, stride=PAIRS), :] = block
        m = orders[k]
        q, s = m >> 7, m & (LANES - 1)
        flipped[...] = reverse(coeff[NB].astype(BF16))
        own_rows = lambda d: pl.ds(pl.multiple_of(d * ROWS, 16), ROWS)
        places = (
            (opposite, across, BF16), (part_right, right, F32), (part_left, left, F32), (part_own, g, F32)
        )
        for place, d, kind in places:
            for t in range(NB):
                shared = (q == t) & (lane < s)
                block = jnp.where(shared, flipped[own_rows(d), :], coeff[t, own_rows(d), :])
                place[k, ROWS * t : ROWS * (t + 1), :] = block.astype(kind)
            place[k, NB * ROWS :, :] = fold(coeff[NB, own_rows(d), :], s).astype(kind)
            if place is opposite:
                sum_first_right(k).start()
                sum_first_left(k).start()

    def sum_second(k):
        cut = LEFT_PART
        to_right[k, :cut] = (part_right[k, :cut] + first_left[k].astype(F32)).astype(BF16)
        to_right[k, cut:] = part_right[k, cut:].astype(BF16)
        sum_second_right(k).start()
        sum_first_left(k).wait_recv()
        to_left[k, :cut] = part_left[k, :cut].astype(BF16)
        to_left[k, cut:] = (part_left[k, cut:] + first_right[k].astype(F32)).astype(BF16)
        sum_second_left(k).start()

    def unpack(k):
        m = orders[k]
        q = m >> 7
        whole = lambda at: (
            part_own[k, at, :] + second_left[k, at, :].astype(F32) + second_right[k, at, :].astype(F32)
        )
        total = [whole(slice(ROWS * t, ROWS * (t + 1))) for t in range(NB)]
        total.append(recover(total, whole(slice(NB * ROWS, SENT)), m, F32))
        for t in range(NB):
            n = lane + LANES * t
            other = jnp.where(NB - 1 - t == q, total[NB], total[NB - 1 - t])
            both = jnp.where(n >= m, total[t], 0.0), jnp.where(n >= M - 1 - m, other, 0.0)
            count = FD * PAIRS
            for ab in range(2):
                for c in range(2):
                    rows[t, pl.ds(2 * ab + c, count, stride=4), :] = both[ab][count * c : count * (c + 1)]
        for f in range(FD):
            for r in range(GROUP):
                at = 2 * (f * GROUP + r)
                results[k, f, r] = jnp.concatenate(
                    [rows[t, at : at + 2, :] for t in range(NB)], axis=1
                )

    def back_step(k):
        grid_back(k)
        exchange(k, 1, sent_back, arrived_back, b_send, b_recv)

    def ahead(k, carry):
        back_step(k)
        return carry

    lax.fori_loop(0, 3, ahead, 0)

    def scatter_step(k, carry):
        @pl.when(k < CHUNKS)
        def _():
            pack_legendre(k)
            exchange_all(k, 1, sent_back, arrived_back, b_send, b_recv).wait_recv()
            legendre_back(k)

        @pl.when((k >= 1) & (k <= CHUNKS))
        def _():
            sum_first_right(k - 1).wait_recv()
            sum_second(k - 1)

        @pl.when((k >= 1) & (k + 2 < CHUNKS))
        def _():
            back_step(k + 2)

        @pl.when(k >= 4)
        def _():
            sum_second_right(k - 4).wait_recv()
            sum_second_left(k - 4).wait_recv()
            unpack(k - 4)
            out_copy(k - 4).start()

        return carry

    lax.fori_loop(0, CHUNKS + 4, scatter_step, 0)

    def finish(k, carry):
        for copy in (own_right, own_left, pass_right, pass_left):
            copy(k).wait_send()
        for copy in (sum_first_right, sum_first_left, sum_second_right, sum_second_left):
            copy(k).wait_send()
        exchange_all(k, 1, sent_back, arrived_back, b_send, b_recv).wait_send()
        out_copy(k).wait()
        return carry

    lax.fori_loop(0, CHUNKS, finish, 0)
    for k, count in ((0, 2), (2, 1), (3, 1), (4, 1)):
        exchange_all(k, count, sent, arrived, a_send, a_recv).wait_send()


PIECES = 5


def hand_over(src_ref, dst_ref, held, sem_in, sem_out):
    count = src_ref.shape[1] // PIECES
    spans = [pl.ds(n * count, count) for n in range(PIECES)]
    reads = [
        pltpu.make_async_copy(src_ref.at[:, at], held.at[:, at], sem_in.at[n])
        for n, at in enumerate(spans)
    ]
    writes = [
        pltpu.make_async_copy(held.at[:, at], dst_ref.at[:, at], sem_out.at[n])
        for n, at in enumerate(spans)
    ]
    for read in reads:
        read.start()
    for read, write in zip(reads, writes):
        read.wait()
        write.start()
    for write in writes:
        write.wait()


VMEM = pl.BlockSpec(memory_space=pltpu.VMEM)
SMEM = pl.BlockSpec(memory_space=pltpu.SMEM)
ANY = pl.BlockSpec(memory_space=pl.ANY)


def local(spec_in, legendre, wave_order, row_length, quad_weight, mixing, square_gain):
    fixed = np.concatenate([wave_tables(), lane_maps()], axis=1)
    fixed = fixed.reshape(BLOCK, XMAX // 2, 2 * LANES).transpose(1, 0, 2)
    width = WAVE * GROUP
    message = pltpu.VMEM((CHUNKS, WAVE, 16, LANES), BF16)
    full = pltpu.VMEM((CHUNKS, SENT, LANES), F32)
    short = pltpu.VMEM((CHUNKS, SENT, LANES), BF16)
    turns = pltpu.VMEM((CHUNKS, width, LANES), F32)
    places = pltpu.VMEM((LATS * LANES, LATS * LANES), BF16)
    copies = pltpu.SemaphoreType.DMA((4, CHUNKS))
    each = pltpu.SemaphoreType.DMA((CHUNKS,))
    result = pl.pallas_call(
        kernel,
        out_shape=jax.ShapeDtypeStruct((FD, GROUP * CHUNKS, 2, M), F32),
        in_specs=[ANY] * 3 + [SMEM] * 4 + [VMEM] * 2,
        out_specs=ANY,
        scratch_shapes=[
            pltpu.VMEM((GROUP * CHUNKS, FLD * WAVE, M), BF16),
            pltpu.VMEM((BLOCK, 2 * BLOCK), BF16),
            places,
            places,
            pltpu.VMEM((CHUNKS, FD, GROUP, 2, M), BF16),
            pltpu.VMEM((NB, 2 * ROWS, LANES), F32),
            pltpu.VMEM((CHUNKS, ROWS, LANES), I32),
            pltpu.VMEM((2 * LANES, LANES), BF16),
            pltpu.VMEM((CHUNKS, width, LANES), I32),
            pltpu.VMEM((CHUNKS, FLD, SENT, LANES), BF16),
            pltpu.VMEM((PB, FLD * ROWS, LANES), F32),
            pltpu.VMEM((FLD * ROWS, LANES), F32),
            pltpu.VMEM((PAIRS, LANES, PACKED), BF16),
            pltpu.VMEM((PAIRS * WAVE, LATS * LANES), BF16),
            pltpu.VMEM((WAVE * 16, LANES), F32),
            message,
            message,
            pltpu.VMEM((CHUNKS, 2 * width, HALF), BF16),
            pltpu.VMEM((CHUNKS, EVEN + HALF, width), BF16),
            pltpu.VMEM((XMAX // 2, 2 * width, 2 * LANES), BF16),
            pltpu.VMEM((XMAX // 2, EVEN + HALF, 2 * LANES), F32),
            pltpu.VMEM((XMAX // 2, BLOCK, 2 * LANES), BF16),
            pltpu.VMEM((XMAX // 2, 8, 2 * LANES), F32),
            turns,
            turns,
            message,
            message,
            short,
            full,
            full,
            full,
            short,
            short,
            pltpu.VMEM((CHUNKS, LEFT_PART, LANES), BF16),
            pltpu.VMEM((CHUNKS, SENT - LEFT_PART, LANES), BF16),
            short,
            short,
            pltpu.VMEM((CHUNKS, FD, GROUP, 2, M), F32),
            each,
            each,
            pltpu.SemaphoreType.DMA,
            each,
            copies,
            copies,
            each,
            each,
            each,
            each,
            copies,
            copies,
        ],
        compiler_params=pltpu.CompilerParams(
            collective_id=0, has_side_effects=True, vmem_limit_bytes=60 << 20
        ),
    )(
        spec_in, legendre, jnp.asarray(fixed),
        wave_order, row_length, quad_weight, square_gain,
        wave_order.reshape(NB, LANES), mixing,
    )
    return pl.pallas_call(
        hand_over,
        out_shape=jax.ShapeDtypeStruct(result.shape, F32),
        in_specs=[ANY],
        out_specs=ANY,
        scratch_shapes=[
            pltpu.VMEM(result.shape, F32),
            pltpu.SemaphoreType.DMA((PIECES,)),
            pltpu.SemaphoreType.DMA((PIECES,)),
        ],
        compiler_params=pltpu.CompilerParams(vmem_limit_bytes=60 << 20),
    )(result)

def solution(mesh):
    in_specs = (P("fld", "wave", None, None), P("wave", "fld", None), P(), P(), P(), P(), P())
    out_specs = P("fld", "wave", None, None)
    return jax.shard_map(local, mesh=mesh, in_specs=in_specs, out_specs=out_specs, check_vma=False)
```
